32 devices in a mesh: grp: 2 (over y), row: 4 (over z), col: 2 (over x), pair: 2 (over core).
Axes of the slice: x: 2, y: 2, z: 4, core: 2. Of those that a mesh axis runs over, the one named last changes fastest.
Arguments:
- features_in: bfloat16 [128, 32, 512], P('grp', 'row', ('col', 'pair')), parts along dimension 0, may hold values from -8 to 8
- filters_one: bfloat16 [64, 3, 3, 64], replicated, may hold values from -0.25 to 0.25
- filters_two: bfloat16 [512, 3, 3, 256], P('row'), may hold values from -0.125 to 0.125
- out_grad: bfloat16 [1024, 128, 8], P(('grp', 'row'), ('col', 'pair')), parts along dimension 0, may hold values from -24 to 24
Outputs:
- input_grad: bfloat16 [128, 32, 512], P('grp', 'row', ('col', 'pair')), parts along dimension 0
- grad_one: float32 [128, 3, 3, 64], P('grp'), parts along dimension 0
- grad_two: float32 [1024, 3, 3, 256], P(('grp', 'row')), parts along dimension 0
The draws below stay inside these ranges and needn't reach their ends.
There are 2 independent parts, one for each index of `grp`. The reference program is written for one: setup_inputs(seed, part) draws one part's arguments, and reference() takes and returns one part's arrays. A program takes and returns all parts, laid end to end along the dimension named above; an argument that names none is the same for every part. Nothing has to cross between parts.
All inputs are finite; a program needn't handle non-finite values.
Results may differ from the reference program's by a relative error of at most 0.015.
Values may be sent and summed in bfloat16 or wider, within the bound.
A program may use at most 64 MiB of HBM per device.

```python
import math
import jax
import jax.numpy as jnp
from jax import lax

C1 = 64
F2 = 512
C2 = 256
H = 32
W = 512
H2 = 8
W2 = 128


def mixed_field(key, shape, base_scale):
    values = jax.random.normal(jax.random.fold_in(key, 13), shape, jnp.float32)
    return (jnp.clip(values, -6.0, 6.0) * base_scale).astype(jnp.bfloat16)


def draw_features_in(key, part):
    return mixed_field(key, (C1, H, W), 1.0)


def draw_out_grad(key, part):
    return mixed_field(key, (F2, W2, H2), 3.0)


def level_of(stream_key, extent, split, low, top_value):
    level, own = 1.0, jax.random.fold_in(stream_key, 6)
    for position, shards_of in split:
        heights = jnp.exp(jax.random.uniform(jax.random.fold_in(own, position), (shards_of,), jnp.float32, low / len(split), top_value / len(split)))
        level = level * jnp.repeat(heights, extent[position] // shards_of).reshape([-1 if axis == position else 1 for axis in range(len(extent))])
    return level


def noise(stream_key, shape, width, most, pieces=(), held_as=jnp.bfloat16):
    entries = jax.random.normal(stream_key, shape, jnp.float32) * width
    if len(pieces) > 0:
        entries = level_of(stream_key, shape, pieces, -0.22, 0.18) * entries
    return jnp.clip(entries, min=-most, max=most).astype(held_as)


def setup_inputs(seed: int = 0, part: int = 0) -> dict:
    splits = jax.random.split(jax.random.key(seed), 5)
    own_keys = jax.random.split(jax.random.fold_in(splits[4], part), 5)
    features_in = draw_features_in(jax.random.fold_in(jax.random.fold_in(splits[4], part), 71), part)
    filters_one = noise(splits[1], (C1, 3, 3, C1), (9 * C1) ** -0.5, 0.25)
    filters_two = noise(splits[2], (F2, 3, 3, C2), (9 * C2) ** -0.5, 0.125, ((0, 4),))
    out_grad = draw_out_grad(jax.random.fold_in(jax.random.fold_in(splits[4], part), 71), part)
    return dict(features_in=features_in, filters_one=filters_one, filters_two=filters_two, out_grad=out_grad)


def conv_same(values, kernel):
    return lax.conv_general_dilated(values.astype(jnp.float32)[None], kernel.astype(jnp.float32), (1, 1), ((1, 1), (1, 1)), dimension_numbers=('NCHW', 'OHWI', 'NCHW'), precision=lax.Precision.HIGHEST)[0]

def conv_back(gradient, kernel):
    flipped = jnp.transpose(kernel[:, ::-1, ::-1, :], (3, 1, 2, 0))
    return conv_same(gradient, flipped)

def filter_grad(gradient, values):
    padded = jnp.pad(values.astype(jnp.float32), ((0, 0), (1, 1), (1, 1)))
    row_count, col_count = (gradient.shape[1], gradient.shape[2])
    wide_grad = gradient.astype(jnp.float32)
    tap_list = []
    for row_tap in range(3):
        tap_row = []
        for col_tap in range(3):
            window = padded[:, row_tap:row_tap + row_count, col_tap:col_tap + col_count]
            tap_row.append(jnp.einsum('ohw,chw->oc', wide_grad, window, precision=lax.Precision.HIGHEST))
        tap_list.append(jnp.stack(tap_row, 1))
    return jnp.stack(tap_list, 1)

def silu_slope(values):
    sigmoid_value = jax.nn.sigmoid(values)
    return sigmoid_value * (1.0 + values * (1.0 - sigmoid_value))

def pool_map(active):
    channels, row_count, col_count = active.shape
    folded = active.reshape(channels, row_count // 4, 2, 2, col_count // 4, 2, 2).mean(axis=(3, 6))
    return jnp.transpose(folded, (0, 2, 4, 1, 3)).reshape(channels * 4, row_count // 4, col_count // 4)

def unpool_map(gradient):
    quad_count, row_count, col_count = gradient.shape
    ordered = jnp.transpose(gradient.reshape(quad_count // 4, 2, 2, row_count, col_count), (0, 3, 1, 4, 2))
    spread = jnp.broadcast_to(ordered[:, :, :, None, :, :, None], (quad_count // 4, row_count, 2, 2, col_count, 2, 2)) * 0.25
    return spread.reshape(quad_count // 4, row_count * 4, col_count * 4)

def reference(features_in, filters_one, filters_two, out_grad):
    pre_one = conv_same(features_in, filters_one)
    pooled = pool_map(jax.nn.silu(pre_one)).astype(jnp.bfloat16)
    pre_two = conv_same(pooled, filters_two)
    grad_pre_two = (jnp.transpose(out_grad, (0, 2, 1)).astype(jnp.float32) * silu_slope(pre_two)).astype(jnp.bfloat16)
    grad_two = filter_grad(grad_pre_two, pooled) / math.sqrt(H2 * W2)
    grad_pooled = conv_back(grad_pre_two, filters_two)
    grad_pre_one = (unpool_map(grad_pooled) * silu_slope(pre_one)).astype(jnp.bfloat16)
    grad_one = filter_grad(grad_pre_one, features_in) / math.sqrt(H * W)
    input_grad = conv_back(grad_pre_one, filters_one).astype(jnp.bfloat16)
    return (input_grad, grad_one, grad_two)
```

```python
import functools
import math

import jax
import jax.numpy as jnp
from jax import lax
from jax.experimental import pallas as pl
from jax.experimental.pallas import tpu as pltpu
from jax.sharding import PartitionSpec as P

MESH = pl.DeviceIdType.MESH
VMEM = pl.BlockSpec(memory_space=pltpu.VMEM)
ANY = pl.BlockSpec(memory_space=pl.ANY)
STRIP = ("col", "pair")
BF = jnp.bfloat16
F32 = jnp.float32

EDGE = 4

DIAGONALS = [(a, b) for a in (-1, 1) for b in (-1, 1)]
WAYS = [(0, -1), (0, 1), (-1, 0), (1, 0)] + DIAGONALS

BY_LANES = (((1,), (1,)), ((), ()))
BY_ROWS = (((0,), (0,)), ((), ()))


def place():
    return lax.axis_index("row"), lax.axis_index(STRIP)


def device_at(row, strip):
    pairs = lax.axis_size("pair")
    return (lax.axis_index("grp"), row, lax.div(strip, pairs), lax.rem(strip, pairs))


def sems(count):
    return [pltpu.SemaphoreType.DMA((count,)), pltpu.SemaphoreType.DMA((count,))]


def post(count, me, device_of, source, landing, send_sem, recv_sem):
    def copy_of(step, slot):
        peer = lax.rem(me + step, count)
        return pltpu.make_async_remote_copy(
            src_ref=source(peer),
            dst_ref=landing.at[me if slot is None else slot],
            send_sem=send_sem.at[step],
            recv_sem=recv_sem.at[me if slot is None else slot],
            device_id=device_of(peer),
            device_id_type=MESH,
        )

    @pl.loop(1, count)
    def _(step):
        copy_of(step, None).start()

    def finish():
        @pl.loop(1, count)
        def _(step):
            copy_of(step, None).wait_send()
            copy_of(step, lax.rem(me + step, count)).wait_recv()

    return finish


def iota(shape, dim):
    return lax.broadcasted_iota(jnp.int32, shape, dim)


def dot(a, b, numbers=(((1,), (0,)), ((), ()))):
    return lax.dot_general(a, b, numbers, preferred_element_type=F32)


def slope(values):
    s = 1.0 / (1.0 + jnp.exp(-values))
    return s * (1.0 + values * (1.0 - s))


def total_of(count, landing):
    value = landing[0].astype(F32)
    for i in range(1, count):
        value += landing[i].astype(F32)
    return value


def whole_kernel(
    rows, strips, band, height2,
    x_any, f1_any, f2_any, up_any,
    ig_out, g1_out, g2_out,
    x_in, f1, f2, up_in, x_wide, x_turned, own, edges_f, edges, from_side, from_row, from_corner, from_up,
    tile, patches, w1, spread_one, pre, block, gathered, up_wide, up, pool3, near3, spread,
    blocks, landed, grad_f, grad, grad_own, pool_all, near_all, pool_map, near_map,
    mine_blocks, one_landed, one_part, one_parts, one_mine, one_all, g1_wide,
    load_sem, a_send, a_recv, b_send, b_recv, c_send, c_recv,
    d1_send, d1_recv, d2_send, d2_recv, d3_send, d3_recv,
    p_send, p_on, p_recv, n_send, n_on, n_recv,
):
    row, strip = place()
    cols, pairs = lax.axis_size("col"), lax.axis_size("pair")
    col, pair = lax.axis_index("col"), lax.axis_index("pair")
    channels = f1.shape[1]
    filters = f2.shape[1]
    quads = 4 * channels
    width = x_in.shape[1]
    width2 = width // 4
    band2 = band // 4
    span = width2 + 2 * EDGE
    full2 = width2 * strips
    mid = pl.ds(EDGE, width2)

    def row_device(i):
        return device_at(i, strip)

    def strip_device(i):
        return device_at(row, i)

    def there(way):
        a, b = row + way[0], strip + way[1]
        return (a >= 0) & (a < rows) & (b >= 0) & (b < strips)

    barrier = pltpu.get_barrier_semaphore()
    for step in range(1, rows):
        pl.semaphore_signal(barrier, inc=1, device_id=row_device(lax.rem(row + step, rows)), device_id_type=MESH)
    for step in range(1, strips):
        pl.semaphore_signal(
            barrier, inc=1, device_id=strip_device(lax.rem(strip + step, strips)), device_id_type=MESH
        )
    for way in DIAGONALS:
        @pl.when(there(way))
        def _(way=way):
            pl.semaphore_signal(
                barrier, inc=1, device_id=device_at(row + way[0], strip + way[1]), device_id_type=MESH
            )
    loads = [
        pltpu.make_async_copy(source, target, load_sem.at[n])
        for n, (source, target) in enumerate([(x_any, x_in), (up_any, up_in), (f1_any, f1), (f2_any, f2)])
    ]
    for load in loads:
        load.start()

    shape = (width, width)
    pick = (iota(shape, 1) == 4 * (iota(shape, 0) % width2) + iota(shape, 0) // width2).astype(BF)
    low_half = iota((width2, 128), 1) < channels
    loads[0].wait()
    x_wide[...] = x_in[...].astype(F32)
    for h in range(band):
        line = x_wide[pl.ds(h, channels, stride=band), :].astype(BF)
        x_turned[pl.ds(2 * h * channels, channels), :] = line
        x_turned[pl.ds((2 * h + 1) * channels, channels), :] = line
    turned = dot(pick, x_turned[...], BY_LANES)
    for h in range(band):
        lanes = slice(h * 128, (h + 1) * 128)
        for half in range(2):
            even = turned[2 * half * width2 : (2 * half + 1) * width2, lanes]
            odd = turned[(2 * half + 1) * width2 : (2 * half + 2) * width2, lanes]
            value = jnp.where(low_half, even, odd)
            tile[h + 2, mid, pl.ds(half * 128, 128)] = value
            own[pl.ds(h * width2, width2), pl.ds(half * 128, 128)] = value.astype(BF)
    for h in range(band):
        edges_f[0, pl.ds(h * EDGE, EDGE)] = tile[h + 2, pl.ds(EDGE, EDGE)]
        edges_f[1, pl.ds(h * EDGE, EDGE)] = tile[h + 2, pl.ds(width2, EDGE)]
    edges[...] = edges_f[:, : band * EDGE].astype(BF)
    loads[1].wait()

    diagonals = (jnp.where(row > 0, 1, 0) + jnp.where(row < rows - 1, 1, 0)) * (
        jnp.where(strip > 0, 1, 0) + jnp.where(strip < strips - 1, 1, 0)
    )
    pl.semaphore_wait(barrier, rows - 1 + strips - 1 + diagonals)
    edge_rows = band * EDGE
    up_edge = 2 * height2

    def slot_of(way):
        side, top = (way[1] + 1) // 2, (way[0] + 1) // 2
        if way[0] == 0:
            return from_side.at[side]
        if way[1] == 0:
            return from_row.at[top]
        return from_corner.at[2 * top + side]

    def source_of(way):
        side = (way[1] + 1) // 2
        if way[0] == 0:
            return edges.at[side]
        if way[1] == 0:
            return own.at[pl.ds(0 if way[0] < 0 else (band - 2) * width2, 2 * width2)]
        return edges.at[side, pl.ds(0 if way[0] < 0 else edge_rows - 16, 16)]

    def border(way, arriving=False):
        back = (-way[0], -way[1])
        land = way if arriving else back
        return pltpu.make_async_remote_copy(
            src_ref=source_of(way),
            dst_ref=slot_of(land),
            send_sem=a_send.at[WAYS.index(way)],
            recv_sem=a_recv.at[WAYS.index(land)],
            device_id=device_at(row + way[0], strip + way[1]),
            device_id_type=MESH,
        )

    def up_border(side, arriving=False):
        land = side if arriving else 1 - side
        return pltpu.make_async_remote_copy(
            src_ref=up_in.at[pl.ds(0 if side == 0 else up_in.shape[0] - up_edge, up_edge)],
            dst_ref=from_up.at[land],
            send_sem=a_send.at[len(WAYS) + side],
            recv_sem=a_recv.at[len(WAYS) + land],
            device_id=device_at(row, strip + (-1, 1)[side]),
            device_id_type=MESH,
        )

    for way in WAYS:
        @pl.when(there(way))
        def _(way=way):
            border(way).start()

        @pl.when(jnp.logical_not(there(way)))
        def _(way=way):
            slot = slot_of(way)
            slot[...] = jnp.zeros(slot.shape, slot.dtype)

    for side in range(2):
        @pl.when(there((0, (-1, 1)[side])))
        def _(side=side):
            up_border(side).start()

        @pl.when(jnp.logical_not(there((0, (-1, 1)[side]))))
        def _(side=side):
            from_up[side] = jnp.zeros(from_up.shape[1:], BF)

    loads[2].wait()
    zero = jnp.zeros((channels, channels), F32)
    nothing = jnp.zeros((channels, 128), BF)
    for i in range(3):
        a, b, c = [f1[3 * i + j].astype(F32) for j in range(3)]
        bc, ab, za, cz = [
            jnp.concatenate(two, 1).astype(BF) for two in ((b, c), (a, b), (zero, a), (c, zero))
        ]
        table = (
            (bc, nothing, za, nothing),
            (ab, cz, nothing, nothing),
            (za, bc, nothing, nothing),
            (nothing, ab, nothing, cz),
        )
        for p in range(4):
            for k in range(4):
                w1[pl.ds(p * channels, channels), pl.ds(i * 512 + k * 128, 128)] = table[p][k]
    shape = (quads, quads)
    for i in range(2):
        target = 4 * (iota(shape, 0) % channels) + 2 * i + iota(shape, 0) // (2 * channels)
        spread_one[pl.ds(i * quads, quads)] = (iota(shape, 1) == target).astype(BF)

    for way in WAYS:
        @pl.when(there(way))
        def _(way=way):
            border(way, True).wait_recv()
    for side in range(2):
        edge = from_side[side].astype(F32)
        at = pl.ds(0 if side == 0 else EDGE + width2, EDGE)
        for h in range(band):
            tile[h + 2, at] = edge[h * EDGE : (h + 1) * EDGE]
        beyond = from_row[side].astype(F32)
        for h in range(2):
            tile[h if side == 0 else band + 2 + h, mid] = beyond[h * width2 : (h + 1) * width2]
        for top in range(2):
            corner = from_corner[2 * top + side].astype(F32)
            for h in range(2):
                start = 16 - 2 * EDGE + h * EDGE if top == 0 else h * EDGE
                tile[h if top == 0 else band + 2 + h, at] = corner[start : start + EDGE]
    for h in range(band + 4):
        here = tile[h]
        patches[h, :, pl.ds(0, quads)] = here.astype(BF)
        patches[h, :, pl.ds(quads, 128)] = pltpu.roll(here[:, quads - 128 :], 1, 0).astype(BF)
        patches[h, :, pl.ds(quads + 128, 128)] = pltpu.roll(here[:, :128], span - 1, 0).astype(BF)

    lines = band + 2
    windows = jnp.concatenate([patches[i : i + lines].reshape(lines * span, 512) for i in range(3)], 1)
    pre[0:lines] = dot(windows, w1[...], BY_LANES).reshape(lines, span, quads)

    def silu(values):
        return values / (1.0 + jnp.exp(-values))

    terms = []
    for i in range(2):
        total = []
        for u in range(band2):
            at = 1 + 4 * u + 2 * i
            total.append((silu(pre[at]) + silu(pre[at + 1])) * 0.25)
        total = jnp.concatenate(total, 0)
        upper = total.astype(BF)
        terms.append((upper, (total - upper.astype(F32)).astype(BF)))
    pooled = jnp.zeros((band2 * span, quads), F32)
    for i in range(2):
        for term in terms[i]:
            pooled += dot(term, spread_one[pl.ds(i * quads, quads)])
    at_col = strip * width2 - EDGE + iota((band2 * span, quads), 0) % span
    pooled = jnp.where((at_col >= 0) & (at_col < full2), pooled, 0.0).astype(BF)
    block[...] = pooled
    finish = post(rows, row, row_device, lambda peer: block, gathered, b_send, b_recv)
    gathered[row] = pooled

    for h in range(lines):
        pre[h] = slope(pre[h]) * 0.25
    for side in range(2):
        @pl.when(there((0, (-1, 1)[side])))
        def _(side=side):
            up_border(side, True).wait_recv()
    up_wide[pl.ds(0, up_edge)] = from_up[0].astype(F32)
    up_wide[pl.ds(up_edge, width2 * height2)] = up_in[...].astype(F32)
    up_wide[pl.ds(up_edge + width2 * height2, up_edge)] = from_up[1].astype(F32)
    for u in range(height2):
        up[u, pl.ds(0, 2)] = jnp.zeros((2, filters), F32)
        up[u, pl.ds(2, width2 + 4)] = up_wide[pl.ds(u, width2 + 4, stride=height2), :]
        up[u, pl.ds(width2 + 6, 2)] = jnp.zeros((2, filters), F32)
    pool3[0] = jnp.zeros(pool3.shape[1:], BF)
    pool3[height2 + 1] = jnp.zeros(pool3.shape[1:], BF)
    for j in range(3):
        near3[j, 0] = jnp.zeros(near3.shape[2:], BF)
        near3[j, height2 + 1] = jnp.zeros(near3.shape[2:], BF)
    spread[0] = jnp.zeros(spread.shape[1:], F32)
    spread[height2 + 1] = jnp.zeros(spread.shape[1:], F32)
    loads[3].wait()
    finish()

    def across(source, table, send_sem, recv_sem, step):
        return pltpu.make_async_remote_copy(
            src_ref=source,
            dst_ref=table.at[strip],
            send_sem=send_sem.at[step],
            recv_sem=recv_sem.at[strip],
            device_id=device_at(row, lax.rem(col + step, cols) * pairs + pair),
            device_id_type=MESH,
        )

    def onward(table, send_sem, recv_sem, column, step):
        slot = column * pairs + pair
        return pltpu.make_async_remote_copy(
            src_ref=table.at[slot],
            dst_ref=table.at[slot],
            send_sem=send_sem.at[column * pairs + step],
            recv_sem=recv_sem.at[slot],
            device_id=device_at(row, col * pairs + lax.rem(pair + step, pairs)),
            device_id_type=MESH,
        )

    def arrival(table, send_sem, recv_sem, slot):
        return pltpu.make_async_remote_copy(
            src_ref=table.at[slot],
            dst_ref=table.at[slot],
            send_sem=send_sem.at[0],
            recv_sem=recv_sem.at[slot],
            device_id=device_at(row, lax.rem(col + 1, cols) * pairs + pair),
            device_id_type=MESH,
        )

    def share(table, send_sem, on_sem, recv_sem):
        for step in range(1, cols):
            across(table.at[strip], table, send_sem, recv_sem, step).start()
        for step in range(1, pairs):
            onward(table, on_sem, recv_sem, col, step).start()

    def pass_on(table, send_sem, on_sem, recv_sem):
        for step in range(1, cols):
            column = lax.rem(col + step, cols)
            arrival(table, send_sem, recv_sem, column * pairs + pair).wait_recv()
            for other in range(1, pairs):
                onward(table, on_sem, recv_sem, column, other).start()

    def settle(table, send_sem, on_sem, recv_sem):
        for step in range(1, cols):
            across(table.at[strip], table, send_sem, recv_sem, step).wait_send()
        for step in range(cols):
            column = lax.rem(col + step, cols)
            for other in range(1, pairs):
                onward(table, on_sem, recv_sem, column, other).wait_send()
                slot = column * pairs + lax.rem(pair + other, pairs)
                arrival(table, send_sem, recv_sem, slot).wait_recv()

    for u in range(height2):
        r, k = divmod(u, band2)
        here = gathered[r, pl.ds(k * span, span)]
        wide = here.astype(F32)
        pool3[u + 1, :, pl.ds(0, quads)] = pltpu.roll(wide, 1, 0).astype(BF)
        pool3[u + 1, :, pl.ds(quads, quads)] = here
        pool3[u + 1, :, pl.ds(2 * quads, quads)] = pltpu.roll(wide, span - 1, 0).astype(BF)
        pool_all[strip, pl.ds(u * width2, width2)] = wide[EDGE : EDGE + width2].astype(BF)
    pool_sems = (p_send, p_on, p_recv)
    share(pool_all, *pool_sems)
    spots = height2 * span
    windows = jnp.concatenate([pool3[i : i + height2].reshape(spots, 3 * quads) for i in range(3)], 1)
    kernel = jnp.concatenate([f2[t] for t in range(9)], 1)
    pre_two = dot(windows, kernel, BY_LANES)
    near = up[0:height2].reshape(spots, filters) * slope(pre_two)
    near3[0, 1 : height2 + 1] = pltpu.roll(near, spots - 1, 0).astype(BF).reshape(height2, span, filters)
    near3[1, 1 : height2 + 1] = near.astype(BF).reshape(height2, span, filters)
    near3[2, 1 : height2 + 1] = pltpu.roll(near, 1, 0).astype(BF).reshape(height2, span, filters)
    total = jnp.zeros((spots, quads), F32)
    if filters % 128 == 0:
        windows = [near3[j, 2 - i : 2 - i + height2].reshape(spots, filters) for i in range(3) for j in range(3)]
        total = dot(jnp.concatenate(windows, 1), f2[...].reshape(9 * filters, quads))
    else:
        for t in range(9):
            i, j = divmod(t, 3)
            total += dot(near3[j, 2 - i : 2 - i + height2].reshape(spots, filters), f2[t])
    spread[1 : height2 + 1] = total.reshape(height2, span, quads)

    lane = iota((1, quads), 1)
    low_row = (lane // 2) % 2 == 1
    low_col = lane % 2 == 1
    at_row = iota((16, quads), 0)

    def fill(peer):
        top = peer * band2
        cells = [spread[top + 1 + k] for k in range(band2)]
        cells.append(jnp.where(low_row, spread[top], spread[top + band2 + 1]))
        tail = jnp.zeros((16, quads), F32)
        for k, cell in enumerate(cells):
            blocks[peer, pl.ds(k * width2, width2)] = cell[EDGE : EDGE + width2].astype(BF)
            rim = jnp.where(low_col, cell[EDGE - 1 : EDGE], cell[EDGE + width2 : EDGE + width2 + 1])
            tail = jnp.where(at_row == k, rim, tail)
        blocks[peer, pl.ds((band2 + 1) * width2, 16)] = tail.astype(BF)

    for peer in range(rows):
        fill(peer)
    finish = post(rows, row, row_device, lambda peer: blocks.at[peer], landed, c_send, c_recv)
    landed[row] = blocks[row]
    for u in range(height2):
        near_all[strip, pl.ds(u * width2, width2)] = near[
            u * span + EDGE : u * span + EDGE + width2
        ].astype(BF)
    near_sems = (n_send, n_on, n_recv)
    share(near_all, *near_sems)
    pass_on(pool_all, *pool_sems)
    finish()
    parts = total_of(rows, landed).astype(BF)
    parts = dot(parts, spread_one[...], BY_LANES)

    for line in range(lines):
        h = line - 1
        if h < 0:
            k, i, inside = band2, 1, row > 0
        elif h >= band:
            k, i, inside = band2, 0, row < rows - 1
        else:
            k, i, inside = h // 4, (h // 2) % 2, None
        some = parts[:, i * quads : (i + 1) * quads]
        body = some[k * width2 : (k + 1) * width2] * pre[line, mid]
        rim = some[(band2 + 1) * width2 + k : (band2 + 1) * width2 + k + 1]
        left = jnp.where(strip > 0, rim * pre[line, pl.ds(EDGE - 1, 1)], 0.0)
        right = jnp.where(strip < strips - 1, rim * pre[line, pl.ds(EDGE + width2, 1)], 0.0)
        if inside is not None:
            body, left, right = [jnp.where(inside, value, 0.0) for value in (body, left, right)]
        else:
            grad_f[h, pl.ds(0, EDGE)] = jnp.zeros((EDGE, quads), F32)
            grad_f[h, mid] = body
            grad_f[h, pl.ds(EDGE + width2, EDGE)] = jnp.zeros((EDGE, quads), F32)
            grad_own[h] = grad_f[h].astype(BF)
        at = min(max(h, 0), band - 1)
        if inside is not None:
            at = band
            grad_f[at, pl.ds(0, EDGE)] = jnp.zeros((EDGE, quads), F32)
            grad_f[at, mid] = body
            grad_f[at, pl.ds(EDGE + width2, EDGE)] = jnp.zeros((EDGE, quads), F32)
        grad_f[at, pl.ds(EDGE - 1, 1)] = left
        grad_f[at, pl.ds(EDGE + width2, 1)] = right
        grad[line] = grad_f[at].astype(BF)

    low = iota((channels, 128), 1) < channels
    halves, ends = [], []
    own_spots = band * span
    windows = jnp.concatenate([patches[1 + i : 1 + i + band].reshape(own_spots, 512) for i in range(3)], 1)
    taps = dot(grad_own[...].reshape(own_spots, quads), windows, BY_ROWS)

    def cut(i, p, k):
        return taps[p * channels : (p + 1) * channels, i * 512 + k * 128 : i * 512 + (k + 1) * 128]

    for i in range(3):
        bc = pltpu.roll(cut(i, 0, 0) + cut(i, 2, 1), 64, 1)
        ab = cut(i, 1, 0) + cut(i, 3, 1)
        za = pltpu.roll(cut(i, 0, 2) + cut(i, 2, 0), 64, 1)
        cz = cut(i, 1, 1) + cut(i, 3, 3)
        halves.append(ab + jnp.where(low, za, bc))
        ends.append(cz + bc)
    packed = halves + [jnp.where(low, ends[0], pltpu.roll(ends[1], 64, 1)), jnp.where(low, ends[2], 0.0)]
    packed = jnp.concatenate(packed, 0).astype(BF)
    piece = mine_blocks.shape[1]
    for s in range(strips):
        start, stop = s * piece, min((s + 1) * piece, packed.shape[0])
        if stop > start:
            mine_blocks[s, pl.ds(0, stop - start)] = packed[start:stop]
        if stop - start < piece:
            begin = max(stop - start, 0)
            mine_blocks[s, pl.ds(begin, piece - begin)] = jnp.zeros((piece - begin, 128), BF)
    finish = post(strips, strip, strip_device, lambda peer: mine_blocks.at[peer], one_landed, d1_send, d1_recv)
    one_landed[strip] = mine_blocks[strip]

    pass_on(near_all, *near_sems)
    cells = jnp.concatenate([grad[2 - i : 2 - i + band].reshape(own_spots, quads) for i in range(3)], 1)
    kernel = jnp.concatenate([w1[:, i * 512 : (i + 1) * 512] for i in range(3)], 0)
    total = dot(cells, kernel)
    before = pltpu.roll(total[:, quads : quads + 128], own_spots - 1, 0)
    after = pltpu.roll(total[:, quads + 128 :], 1, 0)
    sides = (total[:, :128] + after, total[:, 128:quads] + before)
    turned = []
    for h in range(band):
        lines_of = []
        for b in range(4):
            value = sides[b // 2][h * span + EDGE : h * span + EDGE + width2]
            lines_of.append(jnp.where(low_half == (b % 2 == 0), value, 0.0).astype(BF))
        turned.append(jnp.concatenate(lines_of, 0))
    turned = dot(jnp.concatenate(turned, 1), pick, BY_ROWS)
    for h in range(band):
        at = 2 * h * channels
        x_wide[pl.ds(h, channels, stride=band), :] = (
            turned[at : at + channels] + turned[at + channels : at + 2 * channels]
        )
    ig_out[...] = x_wide[...].astype(BF)

    finish()
    part = total_of(strips, one_landed).astype(BF)
    one_part[...] = part
    finish = post(rows, row, row_device, lambda peer: one_part, one_parts, d2_send, d2_recv)
    one_parts[row] = part

    settle(pool_all, *pool_sems)
    settle(near_all, *near_sems)
    near_map[0] = jnp.zeros(near_map.shape[1:], BF)
    near_map[height2 + 1] = jnp.zeros(near_map.shape[1:], BF)
    at_lane = iota((filters, full2), 1)

    def assemble(u):
        at = u * width2
        if not isinstance(u, int):
            at = pl.multiple_of(at, width2)
        line = [near_all[s, pl.ds(at, width2)].astype(F32) for s in range(strips)]
        line = jnp.concatenate(line, 0).T
        after = jnp.where(at_lane < full2 - 1, pltpu.roll(line, full2 - 1, 1), 0.0)
        before = jnp.where(at_lane > 0, pltpu.roll(line, 1, 1), 0.0)
        for j, value in enumerate((after, line, before)):
            near_map[u + 1, pl.ds(j * filters, filters)] = value.astype(BF)
        for s in range(strips):
            pool_map[u, pl.ds(s * width2, width2)] = pool_all[s, pl.ds(at, width2)]

    chunk = max(1, 1024 // full2)
    steps = height2 // chunk
    if steps == 1:
        for u in range(height2):
            assemble(u)
    else:
        pl.loop(0, height2)(assemble)

    def filter_taps(i, step):
        at = step * chunk
        left = jnp.concatenate([near_map[at + k + 2 - i] for k in range(chunk)], 1)
        right = pool_map[pl.ds(at, chunk)].reshape(chunk * full2, quads)
        return dot(left, right).reshape(3, filters, quads)

    def filter_gradient(i):
        g2_out[3 * i : 3 * i + 3] = filter_taps(i, 0)
        if steps > 1:
            @pl.loop(1, steps)
            def _(step):
                g2_out[3 * i : 3 * i + 3] += filter_taps(i, step)

    filter_gradient(0)
    finish()
    part = total_of(rows, one_parts).astype(BF)
    one_mine[...] = part
    finish = post(strips, strip, strip_device, lambda peer: one_mine, one_all, d3_send, d3_recv)
    one_all[strip] = part
    filter_gradient(1)
    filter_gradient(2)
    for way in WAYS:
        @pl.when(there(way))
        def _(way=way):
            border(way).wait_send()
    for side in range(2):
        @pl.when(there((0, (-1, 1)[side])))
        def _(side=side):
            up_border(side).wait_send()
    finish()
    done = one_all[...].astype(F32).reshape(strips * piece, 128)
    rolled = pltpu.roll(done, 64, 1)
    for i in range(3):
        for j in range(3):
            k = i if j < 2 else 3 + i // 2
            value = done if (j if j < 2 else i % 2) == 0 else rolled
            g1_out[3 * i + j] = value[k * channels : (k + 1) * channels, :channels]


def local(features_in, filters_one, filters_two, out_grad):
    channels, band, width = features_in.shape
    rows, strips = lax.axis_size("row"), lax.axis_size(STRIP)
    cols, pairs = lax.axis_size("col"), lax.axis_size("pair")
    filters = filters_two.shape[0]
    quads = 4 * channels
    height2 = out_grad.shape[2]
    width2, band2 = width // 4, band // 4
    span = width2 + 2 * EDGE
    full2 = width2 * strips
    spots = (band2 + 1) * width2 + 16
    piece = -(-5 * channels // strips // 16) * 16

    def v(shape, kind=BF):
        return pltpu.VMEM(shape, kind)

    scratch = [
        v((channels * band, width)),
        v((9, channels, channels)),
        v((9, filters, quads)),
        v((width2 * height2, filters)),
        v((channels * band, width), F32),
        v((2 * channels * band, width)),
        v((band * width2, quads)),
        v((2, band * EDGE + 8, quads), F32),
        v((2, band * EDGE, quads)),
        v((2, band * EDGE, quads)),
        v((2, 2 * width2, quads)),
        v((4, 16, quads)),
        v((2, 2 * height2, filters)),
        v((band + 5, span, quads), F32),
        v((band + 4, span, 512)),
        v((quads, 3 * 512)),
        v((2 * quads, quads)),
        v((band + 3, span, quads), F32),
        v((band2 * span, quads)),
        v((rows, band2 * span, quads)),
        v((span * height2, filters), F32),
        v((height2 + 1, span, filters), F32),
        v((height2 + 2, span, 3 * quads)),
        v((3, height2 + 2, span, filters)),
        v((height2 + 2, span, quads), F32),
        v((rows, spots, quads)),
        v((rows, spots, quads)),
        v((band + 2, span, quads), F32),
        v((band + 2, span, quads)),
        v((band, span, quads)),
        v((strips, height2 * width2, quads)),
        v((strips, height2 * width2, filters)),
        v((height2, full2, quads)),
        v((height2 + 2, 3 * filters, full2)),
        v((strips, piece, 128)),
        v((strips, piece, 128)),
        v((piece, 128)),
        v((rows, piece, 128)),
        v((piece, 128)),
        v((strips, piece, 128)),
        v((8, 128)),
        pltpu.SemaphoreType.DMA((4,)),
    ]
    scratch += sems(len(WAYS) + 2) + sems(rows) + sems(rows) + sems(strips) + sems(rows) + sems(strips)
    for _ in range(2):
        scratch += [
            pltpu.SemaphoreType.DMA((cols,)),
            pltpu.SemaphoreType.DMA((cols * pairs,)),
            pltpu.SemaphoreType.DMA((strips,)),
        ]
    share = 1 if rows * strips <= 64 else 2
    ig, g1, g2 = pl.pallas_call(
        functools.partial(whole_kernel, rows, strips, band, height2),
        out_shape=(
            jax.ShapeDtypeStruct((channels * band, width), BF),
            jax.ShapeDtypeStruct((9, channels, channels), F32),
            jax.ShapeDtypeStruct((9, filters, quads), F32),
        ),
        in_specs=[ANY] * 4,
        out_specs=(VMEM,) * 3,
        scratch_shapes=scratch,
        compiler_params=pltpu.CompilerParams(
            collective_id=0, has_side_effects=True, vmem_limit_bytes=share * 28 * 1024 * 1024
        ),
    )(
        features_in.reshape(channels * band, width),
        jnp.transpose(filters_one, (1, 2, 0, 3)).reshape(9, channels, channels),
        jnp.transpose(filters_two, (1, 2, 0, 3)).reshape(9, filters, quads),
        jnp.transpose(out_grad, (1, 2, 0)).reshape(width2 * height2, filters),
    )
    scale_one = 1.0 / math.sqrt(band * rows * width * strips)
    scale_two = 1.0 / math.sqrt(height2 * full2)
    grad_one = jnp.transpose((g1 * scale_one).reshape(3, 3, channels, channels), (2, 0, 1, 3))
    grad_two = jnp.transpose((g2 * scale_two).reshape(3, 3, filters, quads), (2, 0, 1, 3))
    return (ig.reshape(channels, band, width), grad_one, grad_two)


def solution(mesh):
    in_specs = (
        P("grp", "row", ("col", "pair")),
        P(),
        P("row", None, None, None),
        P(("grp", "row"), ("col", "pair"), None),
    )
    out_specs = (
        P("grp", "row", ("col", "pair")),
        P("grp", None, None, None),
        P(("grp", "row"), None, None, None),
    )
    return jax.shard_map(local, mesh=mesh, in_specs=in_specs, out_specs=out_specs, check_vma=False)
```

```python
import functools
import math

import jax
import jax.numpy as jnp
from jax import lax
from jax.experimental import pallas as pl
from jax.experimental.pallas import tpu as pltpu
from jax.sharding import PartitionSpec as P

MESH = pl.DeviceIdType.MESH
VMEM = pl.BlockSpec(memory_space=pltpu.VMEM)
HBM = pl.BlockSpec(memory_space=pltpu.HBM)
STRIP = ("col", "pair")
BF = jnp.bfloat16
F32 = jnp.float32

EDGE = 4

DIAGONALS = [(a, b) for a in (-1, 1) for b in (-1, 1)]
WAYS = [(0, -1), (0, 1), (-1, 0), (1, 0)] + DIAGONALS

BY_LANES = (((1,), (1,)), ((), ()))
BY_ROWS = (((0,), (0,)), ((), ()))


def place():
    return lax.axis_index("row"), lax.axis_index(STRIP)


def device_at(row, strip):
    pairs = lax.axis_size("pair")
    return (lax.axis_index("grp"), row, lax.div(strip, pairs), lax.rem(strip, pairs))


def sems(count):
    return [pltpu.SemaphoreType.DMA((count,)), pltpu.SemaphoreType.DMA((count,))]


def post(count, me, device_of, source, landing, send_sem, recv_sem):
    def copy_of(step, slot):
        peer = lax.rem(me + step, count)
        return pltpu.make_async_remote_copy(
            src_ref=source(peer),
            dst_ref=landing.at[me if slot is None else slot],
            send_sem=send_sem.at[step],
            recv_sem=recv_sem.at[me if slot is None else slot],
            device_id=device_of(peer),
            device_id_type=MESH,
        )

    @pl.loop(1, count)
    def _(step):
        copy_of(step, None).start()

    def finish():
        @pl.loop(1, count)
        def _(step):
            copy_of(step, None).wait_send()
            copy_of(step, lax.rem(me + step, count)).wait_recv()

    return finish


def iota(shape, dim):
    return lax.broadcasted_iota(jnp.int32, shape, dim)


def dot(a, b, numbers=(((1,), (0,)), ((), ()))):
    return lax.dot_general(a, b, numbers, preferred_element_type=F32)


def slope(values):
    s = 1.0 / (1.0 + jnp.exp(-values))
    return s * (1.0 + values * (1.0 - s))


def total_of(count, landing):
    value = landing[0].astype(F32)
    for i in range(1, count):
        value += landing[i].astype(F32)
    return value


def whole_kernel(
    rows, strips, band, height2, scale_one, scale_two,
    x_any, f1_any, f2_any, up_any,
    ig_out, g1_out, g2_out,
    x_in, f1, f2, up_in, x_wide, x_turned, own, edges_f, edges, from_side, from_row, from_corner, from_up,
    tile, patches, w1, spread_one, pre, block, gathered, up_wide, up, pool3, near3, spread,
    blocks, landed, grad_f, grad, grad_own, pool_all, near_all, pool_map, near_map,
    mine_blocks, one_landed, one_part, one_parts, one_mine, one_all, g1_wide,
    load_sem, a_send, a_recv, b_send, b_recv, c_send, c_recv,
    d1_send, d1_recv, d2_send, d2_recv, d3_send, d3_recv,
    p_send, p_on, p_recv, n_send, n_on, n_recv,
):
    row, strip = place()
    cols, pairs = lax.axis_size("col"), lax.axis_size("pair")
    col, pair = lax.axis_index("col"), lax.axis_index("pair")
    channels = f1.shape[1]
    filters = f2.shape[1]
    quads = 4 * channels
    width = x_in.shape[1]
    width2 = width // 4
    band2 = band // 4
    span = width2 + 2 * EDGE
    full2 = width2 * strips
    mid = pl.ds(EDGE, width2)

    def row_device(i):
        return device_at(i, strip)

    def strip_device(i):
        return device_at(row, i)

    def there(way):
        a, b = row + way[0], strip + way[1]
        return (a >= 0) & (a < rows) & (b >= 0) & (b < strips)

    barrier = pltpu.get_barrier_semaphore()
    for step in range(1, rows):
        pl.semaphore_signal(barrier, inc=1, device_id=row_device(lax.rem(row + step, rows)), device_id_type=MESH)
    for step in range(1, strips):
        pl.semaphore_signal(
            barrier, inc=1, device_id=strip_device(lax.rem(strip + step, strips)), device_id_type=MESH
        )
    for way in DIAGONALS:
        @pl.when(there(way))
        def _(way=way):
            pl.semaphore_signal(
                barrier, inc=1, device_id=device_at(row + way[0], strip + way[1]), device_id_type=MESH
            )
    loads = [
        pltpu.make_async_copy(source, target, load_sem.at[n])
        for n, (source, target) in enumerate([(x_any, x_in), (up_any, up_in), (f1_any, f1), (f2_any, f2)])
    ]
    for load in loads:
        load.start()

    shape = (width, width)
    pick = (iota(shape, 1) == 4 * (iota(shape, 0) % width2) + iota(shape, 0) // width2).astype(BF)
    low_half = iota((width2, 128), 1) < channels
    loads[0].wait()
    x_wide[...] = x_in[...].astype(F32)
    for h in range(band):
        line = x_wide[pl.ds(h, channels, stride=band), :].astype(BF)
        x_turned[pl.ds(2 * h * channels, channels), :] = line
        x_turned[pl.ds((2 * h + 1) * channels, channels), :] = line
    turned = dot(pick, x_turned[...], BY_LANES)
    for h in range(band):
        lanes = slice(h * 128, (h + 1) * 128)
        for half in range(2):
            even = turned[2 * half * width2 : (2 * half + 1) * width2, lanes]
            odd = turned[(2 * half + 1) * width2 : (2 * half + 2) * width2, lanes]
            value = jnp.where(low_half, even, odd)
            tile[h + 2, mid, pl.ds(half * 128, 128)] = value
            own[pl.ds(h * width2, width2), pl.ds(half * 128, 128)] = value.astype(BF)
    for h in range(band):
        edges_f[0, pl.ds(h * EDGE, EDGE)] = tile[h + 2, pl.ds(EDGE, EDGE)]
        edges_f[1, pl.ds(h * EDGE, EDGE)] = tile[h + 2, pl.ds(width2, EDGE)]
    edges[...] = edges_f[:, : band * EDGE].astype(BF)
    loads[1].wait()

    diagonals = (jnp.where(row > 0, 1, 0) + jnp.where(row < rows - 1, 1, 0)) * (
        jnp.where(strip > 0, 1, 0) + jnp.where(strip < strips - 1, 1, 0)
    )
    pl.semaphore_wait(barrier, rows - 1 + strips - 1 + diagonals)
    edge_rows = band * EDGE
    up_edge = 2 * height2

    def slot_of(way):
        side, top = (way[1] + 1) // 2, (way[0] + 1) // 2
        if way[0] == 0:
            return from_side.at[side]
        if way[1] == 0:
            return from_row.at[top]
        return from_corner.at[2 * top + side]

    def source_of(way):
        side = (way[1] + 1) // 2
        if way[0] == 0:
            return edges.at[side]
        if way[1] == 0:
            return own.at[pl.ds(0 if way[0] < 0 else (band - 2) * width2, 2 * width2)]
        return edges.at[side, pl.ds(0 if way[0] < 0 else edge_rows - 16, 16)]

    def border(way, arriving=False):
        back = (-way[0], -way[1])
        land = way if arriving else back
        return pltpu.make_async_remote_copy(
            src_ref=source_of(way),
            dst_ref=slot_of(land),
            send_sem=a_send.at[WAYS.index(way)],
            recv_sem=a_recv.at[WAYS.index(land)],
            device_id=device_at(row + way[0], strip + way[1]),
            device_id_type=MESH,
        )

    def up_border(side, arriving=False):
        land = side if arriving else 1 - side
        return pltpu.make_async_remote_copy(
            src_ref=up_in.at[pl.ds(0 if side == 0 else up_in.shape[0] - up_edge, up_edge)],
            dst_ref=from_up.at[land],
            send_sem=a_send.at[len(WAYS) + side],
            recv_sem=a_recv.at[len(WAYS) + land],
            device_id=device_at(row, strip + (-1, 1)[side]),
            device_id_type=MESH,
        )

    for way in WAYS:
        @pl.when(there(way))
        def _(way=way):
            border(way).start()

        @pl.when(jnp.logical_not(there(way)))
        def _(way=way):
            slot = slot_of(way)
            slot[...] = jnp.zeros(slot.shape, slot.dtype)

    for side in range(2):
        @pl.when(there((0, (-1, 1)[side])))
        def _(side=side):
            up_border(side).start()

        @pl.when(jnp.logical_not(there((0, (-1, 1)[side]))))
        def _(side=side):
            from_up[side] = jnp.zeros(from_up.shape[1:], BF)

    loads[2].wait()
    zero = jnp.zeros((channels, channels), F32)
    nothing = jnp.zeros((channels, 128), BF)
    for i in range(3):
        a, b, c = [f1[3 * i + j].astype(F32) for j in range(3)]
        bc, ab, za, cz = [
            jnp.concatenate(two, 1).astype(BF) for two in ((b, c), (a, b), (zero, a), (c, zero))
        ]
        table = (
            (bc, nothing, za, nothing),
            (ab, cz, nothing, nothing),
            (za, bc, nothing, nothing),
            (nothing, ab, nothing, cz),
        )
        for p in range(4):
            for k in range(4):
                w1[pl.ds(p * channels, channels), pl.ds(i * 512 + k * 128, 128)] = table[p][k]
    shape = (quads, quads)
    for i in range(2):
        target = 4 * (iota(shape, 0) % channels) + 2 * i + iota(shape, 0) // (2 * channels)
        spread_one[pl.ds(i * quads, quads)] = (iota(shape, 1) == target).astype(BF)

    for way in WAYS:
        @pl.when(there(way))
        def _(way=way):
            border(way, True).wait_recv()
    for side in range(2):
        edge = from_side[side].astype(F32)
        at = pl.ds(0 if side == 0 else EDGE + width2, EDGE)
        for h in range(band):
            tile[h + 2, at] = edge[h * EDGE : (h + 1) * EDGE]
        beyond = from_row[side].astype(F32)
        for h in range(2):
            tile[h if side == 0 else band + 2 + h, mid] = beyond[h * width2 : (h + 1) * width2]
        for top in range(2):
            corner = from_corner[2 * top + side].astype(F32)
            for h in range(2):
                start = 16 - 2 * EDGE + h * EDGE if top == 0 else h * EDGE
                tile[h if top == 0 else band + 2 + h, at] = corner[start : start + EDGE]
    for h in range(band + 4):
        here = tile[h]
        patches[h, :, pl.ds(0, quads)] = here.astype(BF)
        patches[h, :, pl.ds(quads, 128)] = pltpu.roll(here[:, quads - 128 :], 1, 0).astype(BF)
        patches[h, :, pl.ds(quads + 128, 128)] = pltpu.roll(here[:, :128], span - 1, 0).astype(BF)

    lines = band + 2
    windows = jnp.concatenate([patches[i : i + lines].reshape(lines * span, 512) for i in range(3)], 1)
    pre[0:lines] = dot(windows, w1[...], BY_LANES).reshape(lines, span, quads)

    def silu(values):
        return values / (1.0 + jnp.exp(-values))

    terms = []
    for i in range(2):
        total = []
        for u in range(band2):
            at = 1 + 4 * u + 2 * i
            total.append((silu(pre[at]) + silu(pre[at + 1])) * 0.25)
        total = jnp.concatenate(total, 0)
        upper = total.astype(BF)
        terms.append((upper, (total - upper.astype(F32)).astype(BF)))
    pooled = jnp.zeros((band2 * span, quads), F32)
    for i in range(2):
        for term in terms[i]:
            pooled += dot(term, spread_one[pl.ds(i * quads, quads)])
    at_col = strip * width2 - EDGE + iota((band2 * span, quads), 0) % span
    pooled = jnp.where((at_col >= 0) & (at_col < full2), pooled, 0.0).astype(BF)
    block[...] = pooled
    finish = post(rows, row, row_device, lambda peer: block, gathered, b_send, b_recv)
    gathered[row] = pooled

    for h in range(lines):
        pre[h] = slope(pre[h]) * 0.25
    for side in range(2):
        @pl.when(there((0, (-1, 1)[side])))
        def _(side=side):
            up_border(side, True).wait_recv()
    up_wide[pl.ds(0, up_edge)] = from_up[0].astype(F32)
    up_wide[pl.ds(up_edge, width2 * height2)] = up_in[...].astype(F32)
    up_wide[pl.ds(up_edge + width2 * height2, up_edge)] = from_up[1].astype(F32)
    for u in range(height2):
        up[u, pl.ds(0, 2)] = jnp.zeros((2, filters), F32)
        up[u, pl.ds(2, width2 + 4)] = up_wide[pl.ds(u, width2 + 4, stride=height2), :]
        up[u, pl.ds(width2 + 6, 2)] = jnp.zeros((2, filters), F32)
    pool3[0] = jnp.zeros(pool3.shape[1:], BF)
    pool3[height2 + 1] = jnp.zeros(pool3.shape[1:], BF)
    for j in range(3):
        near3[j, 0] = jnp.zeros(near3.shape[2:], BF)
        near3[j, height2 + 1] = jnp.zeros(near3.shape[2:], BF)
    spread[0] = jnp.zeros(spread.shape[1:], F32)
    spread[height2 + 1] = jnp.zeros(spread.shape[1:], F32)
    loads[3].wait()
    finish()

    def across(source, table, send_sem, recv_sem, step):
        return pltpu.make_async_remote_copy(
            src_ref=source,
            dst_ref=table.at[strip],
            send_sem=send_sem.at[step],
            recv_sem=recv_sem.at[strip],
            device_id=device_at(row, lax.rem(col + step, cols) * pairs + pair),
            device_id_type=MESH,
        )

    def onward(table, send_sem, recv_sem, column, step):
        slot = column * pairs + pair
        return pltpu.make_async_remote_copy(
            src_ref=table.at[slot],
            dst_ref=table.at[slot],
            send_sem=send_sem.at[column * pairs + step],
            recv_sem=recv_sem.at[slot],
            device_id=device_at(row, col * pairs + lax.rem(pair + step, pairs)),
            device_id_type=MESH,
        )

    def arrival(table, send_sem, recv_sem, slot):
        return pltpu.make_async_remote_copy(
            src_ref=table.at[slot],
            dst_ref=table.at[slot],
            send_sem=send_sem.at[0],
            recv_sem=recv_sem.at[slot],
            device_id=device_at(row, lax.rem(col + 1, cols) * pairs + pair),
            device_id_type=MESH,
        )

    def share(table, send_sem, on_sem, recv_sem):
        for step in range(1, cols):
            across(table.at[strip], table, send_sem, recv_sem, step).start()
        for step in range(1, pairs):
            onward(table, on_sem, recv_sem, col, step).start()

    def pass_on(table, send_sem, on_sem, recv_sem):
        for step in range(1, cols):
            column = lax.rem(col + step, cols)
            arrival(table, send_sem, recv_sem, column * pairs + pair).wait_recv()
            for other in range(1, pairs):
                onward(table, on_sem, recv_sem, column, other).start()

    def settle(table, send_sem, on_sem, recv_sem):
        for step in range(1, cols):
            across(table.at[strip], table, send_sem, recv_sem, step).wait_send()
        for step in range(cols):
            column = lax.rem(col + step, cols)
            for other in range(1, pairs):
                onward(table, on_sem, recv_sem, column, other).wait_send()
                slot = column * pairs + lax.rem(pair + other, pairs)
                arrival(table, send_sem, recv_sem, slot).wait_recv()

    for u in range(height2):
        r, k = divmod(u, band2)
        here = gathered[r, pl.ds(k * span, span)]
        wide = here.astype(F32)
        pool3[u + 1, :, pl.ds(0, quads)] = pltpu.roll(wide, 1, 0).astype(BF)
        pool3[u + 1, :, pl.ds(quads, quads)] = here
        pool3[u + 1, :, pl.ds(2 * quads, quads)] = pltpu.roll(wide, span - 1, 0).astype(BF)
        pool_all[strip, pl.ds(u * width2, width2)] = wide[EDGE : EDGE + width2].astype(BF)
    pool_sems = (p_send, p_on, p_recv)
    share(pool_all, *pool_sems)
    spots = height2 * span
    windows = jnp.concatenate([pool3[i : i + height2].reshape(spots, 3 * quads) for i in range(3)], 1)
    kernel = jnp.concatenate([f2[t] for t in range(9)], 1)
    pre_two = dot(windows, kernel, BY_LANES)
    near = up[0:height2].reshape(spots, filters) * slope(pre_two)
    near3[0, 1 : height2 + 1] = pltpu.roll(near, spots - 1, 0).astype(BF).reshape(height2, span, filters)
    near3[1, 1 : height2 + 1] = near.astype(BF).reshape(height2, span, filters)
    near3[2, 1 : height2 + 1] = pltpu.roll(near, 1, 0).astype(BF).reshape(height2, span, filters)
    total = jnp.zeros((spots, quads), F32)
    if filters % 128 == 0:
        windows = [near3[j, 2 - i : 2 - i + height2].reshape(spots, filters) for i in range(3) for j in range(3)]
        total = dot(jnp.concatenate(windows, 1), f2[...].reshape(9 * filters, quads))
    else:
        for t in range(9):
            i, j = divmod(t, 3)
            total += dot(near3[j, 2 - i : 2 - i + height2].reshape(spots, filters), f2[t])
    spread[1 : height2 + 1] = total.reshape(height2, span, quads)

    lane = iota((1, quads), 1)
    low_row = (lane // 2) % 2 == 1
    low_col = lane % 2 == 1
    at_row = iota((16, quads), 0)

    def fill(peer):
        top = peer * band2
        cells = [spread[top + 1 + k] for k in range(band2)]
        cells.append(jnp.where(low_row, spread[top], spread[top + band2 + 1]))
        tail = jnp.zeros((16, quads), F32)
        for k, cell in enumerate(cells):
            blocks[peer, pl.ds(k * width2, width2)] = cell[EDGE : EDGE + width2].astype(BF)
            rim = jnp.where(low_col, cell[EDGE - 1 : EDGE], cell[EDGE + width2 : EDGE + width2 + 1])
            tail = jnp.where(at_row == k, rim, tail)
        blocks[peer, pl.ds((band2 + 1) * width2, 16)] = tail.astype(BF)

    for peer in range(rows):
        fill(peer)
    finish = post(rows, row, row_device, lambda peer: blocks.at[peer], landed, c_send, c_recv)
    landed[row] = blocks[row]
    for u in range(height2):
        near_all[strip, pl.ds(u * width2, width2)] = near[
            u * span + EDGE : u * span + EDGE + width2
        ].astype(BF)
    near_sems = (n_send, n_on, n_recv)
    share(near_all, *near_sems)
    pass_on(pool_all, *pool_sems)
    finish()
    parts = total_of(rows, landed).astype(BF)
    parts = dot(parts, spread_one[...], BY_LANES)

    for line in range(lines):
        h = line - 1
        if h < 0:
            k, i, inside = band2, 1, row > 0
        elif h >= band:
            k, i, inside = band2, 0, row < rows - 1
        else:
            k, i, inside = h // 4, (h // 2) % 2, None
        some = parts[:, i * quads : (i + 1) * quads]
        body = some[k * width2 : (k + 1) * width2] * pre[line, mid]
        rim = some[(band2 + 1) * width2 + k : (band2 + 1) * width2 + k + 1]
        left = jnp.where(strip > 0, rim * pre[line, pl.ds(EDGE - 1, 1)], 0.0)
        right = jnp.where(strip < strips - 1, rim * pre[line, pl.ds(EDGE + width2, 1)], 0.0)
        if inside is not None:
            body, left, right = [jnp.where(inside, value, 0.0) for value in (body, left, right)]
        else:
            grad_f[h, pl.ds(0, EDGE)] = jnp.zeros((EDGE, quads), F32)
            grad_f[h, mid] = body
            grad_f[h, pl.ds(EDGE + width2, EDGE)] = jnp.zeros((EDGE, quads), F32)
            grad_own[h] = grad_f[h].astype(BF)
        at = min(max(h, 0), band - 1)
        if inside is not None:
            at = band
            grad_f[at, pl.ds(0, EDGE)] = jnp.zeros((EDGE, quads), F32)
            grad_f[at, mid] = body
            grad_f[at, pl.ds(EDGE + width2, EDGE)] = jnp.zeros((EDGE, quads), F32)
        grad_f[at, pl.ds(EDGE - 1, 1)] = left
        grad_f[at, pl.ds(EDGE + width2, 1)] = right
        grad[line] = grad_f[at].astype(BF)

    low = iota((channels, 128), 1) < channels
    halves, ends = [], []
    own_spots = band * span
    windows = jnp.concatenate([patches[1 + i : 1 + i + band].reshape(own_spots, 512) for i in range(3)], 1)
    taps = dot(grad_own[...].reshape(own_spots, quads), windows, BY_ROWS)

    def cut(i, p, k):
        return taps[p * channels : (p + 1) * channels, i * 512 + k * 128 : i * 512 + (k + 1) * 128]

    for i in range(3):
        bc = pltpu.roll(cut(i, 0, 0) + cut(i, 2, 1), 64, 1)
        ab = cut(i, 1, 0) + cut(i, 3, 1)
        za = pltpu.roll(cut(i, 0, 2) + cut(i, 2, 0), 64, 1)
        cz = cut(i, 1, 1) + cut(i, 3, 3)
        halves.append(ab + jnp.where(low, za, bc))
        ends.append(cz + bc)
    packed = halves + [jnp.where(low, ends[0], pltpu.roll(ends[1], 64, 1)), jnp.where(low, ends[2], 0.0)]
    packed = jnp.concatenate(packed, 0).astype(BF)
    piece = mine_blocks.shape[1]
    for s in range(strips):
        start, stop = s * piece, min((s + 1) * piece, packed.shape[0])
        if stop > start:
            mine_blocks[s, pl.ds(0, stop - start)] = packed[start:stop]
        if stop - start < piece:
            begin = max(stop - start, 0)
            mine_blocks[s, pl.ds(begin, piece - begin)] = jnp.zeros((piece - begin, 128), BF)
    finish = post(strips, strip, strip_device, lambda peer: mine_blocks.at[peer], one_landed, d1_send, d1_recv)
    one_landed[strip] = mine_blocks[strip]

    pass_on(near_all, *near_sems)
    cells = jnp.concatenate([grad[2 - i : 2 - i + band].reshape(own_spots, quads) for i in range(3)], 1)
    kernel = jnp.concatenate([w1[:, i * 512 : (i + 1) * 512] for i in range(3)], 0)
    total = dot(cells, kernel)
    before = pltpu.roll(total[:, quads : quads + 128], own_spots - 1, 0)
    after = pltpu.roll(total[:, quads + 128 :], 1, 0)
    sides = (total[:, :128] + after, total[:, 128:quads] + before)
    turned = []
    for h in range(band):
        lines_of = []
        for b in range(4):
            value = sides[b // 2][h * span + EDGE : h * span + EDGE + width2]
            lines_of.append(jnp.where(low_half == (b % 2 == 0), value, 0.0).astype(BF))
        turned.append(jnp.concatenate(lines_of, 0))
    turned = dot(jnp.concatenate(turned, 1), pick, BY_ROWS)
    for h in range(band):
        at = 2 * h * channels
        x_wide[pl.ds(h, channels, stride=band), :] = (
            turned[at : at + channels] + turned[at + channels : at + 2 * channels]
        )
    ig_out[...] = x_wide[...].astype(BF)

    finish()
    part = total_of(strips, one_landed).astype(BF)
    one_part[...] = part
    finish = post(rows, row, row_device, lambda peer: one_part, one_parts, d2_send, d2_recv)
    one_parts[row] = part

    settle(pool_all, *pool_sems)
    settle(near_all, *near_sems)
    near_map[0] = jnp.zeros(near_map.shape[1:], BF)
    near_map[height2 + 1] = jnp.zeros(near_map.shape[1:], BF)
    at_lane = iota((filters, full2), 1)

    def assemble(u):
        at = u * width2
        if not isinstance(u, int):
            at = pl.multiple_of(at, width2)
        line = [near_all[s, pl.ds(at, width2)].astype(F32) for s in range(strips)]
        line = jnp.concatenate(line, 0).T
        after = jnp.where(at_lane < full2 - 1, pltpu.roll(line, full2 - 1, 1), 0.0)
        before = jnp.where(at_lane > 0, pltpu.roll(line, 1, 1), 0.0)
        for j, value in enumerate((after, line, before)):
            near_map[u + 1, pl.ds(j * filters, filters)] = value.astype(BF)
        for s in range(strips):
            pool_map[u, pl.ds(s * width2, width2)] = pool_all[s, pl.ds(at, width2)]

    chunk = max(1, 1024 // full2)
    steps = height2 // chunk
    if steps == 1:
        for u in range(height2):
            assemble(u)
    else:
        pl.loop(0, height2)(assemble)

    def filter_taps(i, step):
        at = step * chunk
        left = jnp.concatenate([near_map[at + k + 2 - i] for k in range(chunk)], 1)
        right = pool_map[pl.ds(at, chunk)].reshape(chunk * full2, quads)
        return scale_two * dot(left, right).reshape(3, filters, quads)

    def filter_gradient(i):
        g2_out[3 * i : 3 * i + 3] = filter_taps(i, 0)
        if steps > 1:
            @pl.loop(1, steps)
            def _(step):
                g2_out[3 * i : 3 * i + 3] += filter_taps(i, step)

    filter_gradient(0)
    finish()
    part = total_of(rows, one_parts).astype(BF)
    one_mine[...] = part
    finish = post(strips, strip, strip_device, lambda peer: one_mine, one_all, d3_send, d3_recv)
    one_all[strip] = part
    filter_gradient(1)
    filter_gradient(2)
    for way in WAYS:
        @pl.when(there(way))
        def _(way=way):
            border(way).wait_send()
    for side in range(2):
        @pl.when(there((0, (-1, 1)[side])))
        def _(side=side):
            up_border(side).wait_send()
    finish()
    done = scale_one * one_all[...].astype(F32).reshape(strips * piece, 128)
    rolled = pltpu.roll(done, 64, 1)
    for i in range(3):
        for j in range(3):
            k = i if j < 2 else 3 + i // 2
            value = done if (j if j < 2 else i % 2) == 0 else rolled
            g1_out[3 * i + j] = value[k * channels : (k + 1) * channels, :channels]


def write_kernel(*refs):
    count = len(refs) // 2
    sources, targets, sem = refs[:count], refs[count:-1], refs[-1]
    copies = [pltpu.make_async_copy(sources[n], targets[n], sem.at[n]) for n in range(count)]
    for copy in copies:
        copy.start()
    for copy in copies:
        copy.wait()


def write_out(*arrays):
    arrays = [pltpu.with_memory_space_constraint(a, pltpu.VMEM) for a in arrays]
    return pl.pallas_call(
        write_kernel,
        out_shape=tuple(jax.ShapeDtypeStruct(a.shape, a.dtype) for a in arrays),
        in_specs=[VMEM] * len(arrays),
        out_specs=(HBM,) * len(arrays),
        scratch_shapes=[pltpu.SemaphoreType.DMA((len(arrays),))],
    )(*arrays)


def local(features_in, filters_one, filters_two, out_grad):
    channels, band, width = features_in.shape
    rows, strips = lax.axis_size("row"), lax.axis_size(STRIP)
    cols, pairs = lax.axis_size("col"), lax.axis_size("pair")
    filters = filters_two.shape[0]
    quads = 4 * channels
    height2 = out_grad.shape[2]
    width2, band2 = width // 4, band // 4
    span = width2 + 2 * EDGE
    full2 = width2 * strips
    spots = (band2 + 1) * width2 + 16
    piece = -(-5 * channels // strips // 16) * 16

    def v(shape, kind=BF):
        return pltpu.VMEM(shape, kind)

    scratch = [
        v((channels * band, width)),
        v((9, channels, channels)),
        v((9, filters, quads)),
        v((width2 * height2, filters)),
        v((channels * band, width), F32),
        v((2 * channels * band, width)),
        v((band * width2, quads)),
        v((2, band * EDGE + 8, quads), F32),
        v((2, band * EDGE, quads)),
        v((2, band * EDGE, quads)),
        v((2, 2 * width2, quads)),
        v((4, 16, quads)),
        v((2, 2 * height2, filters)),
        v((band + 5, span, quads), F32),
        v((band + 4, span, 512)),
        v((quads, 3 * 512)),
        v((2 * quads, quads)),
        v((band + 3, span, quads), F32),
        v((band2 * span, quads)),
        v((rows, band2 * span, quads)),
        v((span * height2, filters), F32),
        v((height2 + 1, span, filters), F32),
        v((height2 + 2, span, 3 * quads)),
        v((3, height2 + 2, span, filters)),
        v((height2 + 2, span, quads), F32),
        v((rows, spots, quads)),
        v((rows, spots, quads)),
        v((band + 2, span, quads), F32),
        v((band + 2, span, quads)),
        v((band, span, quads)),
        v((strips, height2 * width2, quads)),
        v((strips, height2 * width2, filters)),
        v((height2, full2, quads)),
        v((height2 + 2, 3 * filters, full2)),
        v((strips, piece, 128)),
        v((strips, piece, 128)),
        v((piece, 128)),
        v((rows, piece, 128)),
        v((piece, 128)),
        v((strips, piece, 128)),
        v((8, 128)),
        pltpu.SemaphoreType.DMA((4,)),
    ]
    scratch += sems(len(WAYS) + 2) + sems(rows) + sems(rows) + sems(strips) + sems(rows) + sems(strips)
    for _ in range(2):
        scratch += [
            pltpu.SemaphoreType.DMA((cols,)),
            pltpu.SemaphoreType.DMA((cols * pairs,)),
            pltpu.SemaphoreType.DMA((strips,)),
        ]
    arguments = (
        features_in.reshape(channels * band, width),
        jnp.transpose(filters_one, (1, 2, 0, 3)).reshape(9, channels, channels),
        jnp.transpose(filters_two, (1, 2, 0, 3)).reshape(9, filters, quads),
        jnp.transpose(out_grad, (1, 2, 0)).reshape(width2 * height2, filters),
    )
    arguments = [pltpu.with_memory_space_constraint(a, pltpu.HBM) for a in arguments]
    share = 1 if rows * strips <= 64 else 2
    scale_one = 1.0 / math.sqrt(band * rows * width * strips)
    scale_two = 1.0 / math.sqrt(height2 * full2)
    ig, g1, g2 = pl.pallas_call(
        functools.partial(whole_kernel, rows, strips, band, height2, scale_one, scale_two),
        out_shape=(
            jax.ShapeDtypeStruct((channels * band, width), BF),
            jax.ShapeDtypeStruct((9, channels, channels), F32),
            jax.ShapeDtypeStruct((9, filters, quads), F32),
        ),
        in_specs=[HBM] * 4,
        out_specs=(VMEM,) * 3,
        scratch_shapes=scratch,
        compiler_params=pltpu.CompilerParams(
            collective_id=0, has_side_effects=True, vmem_limit_bytes=share * 28 * 1024 * 1024
        ),
    )(*arguments)
    ig, g1, g2 = write_out(ig, g1, g2)
    grad_one = jnp.transpose(g1.reshape(3, 3, channels, channels), (2, 0, 1, 3))
    grad_two = jnp.transpose(g2.reshape(3, 3, filters, quads), (2, 0, 1, 3))
    return (ig.reshape(channels, band, width), grad_one, grad_two)


def solution(mesh):
    in_specs = (
        P("grp", "row", ("col", "pair")),
        P(),
        P("row", None, None, None),
        P(("grp", "row"), ("col", "pair"), None),
    )
    out_specs = (
        P("grp", "row", ("col", "pair")),
        P("grp", None, None, None),
        P(("grp", "row"), None, None, None),
    )
    return jax.shard_map(local, mesh=mesh, in_specs=in_specs, out_specs=out_specs, check_vma=False)
```

```python
import functools
import math

import jax
import jax.numpy as jnp
from jax import lax
from jax.experimental import pallas as pl
from jax.experimental.pallas import tpu as pltpu
from jax.sharding import PartitionSpec as P

MESH = pl.DeviceIdType.MESH
VMEM = pl.BlockSpec(memory_space=pltpu.VMEM)
HBM = pl.BlockSpec(memory_space=pltpu.HBM)
STRIP = ("col", "pair")
BF = jnp.bfloat16
F32 = jnp.float32

EDGE = 4

DIAGONALS = [(a, b) for a in (-1, 1) for b in (-1, 1)]
WAYS = [(0, -1), (0, 1), (-1, 0), (1, 0)] + DIAGONALS

BY_LANES = (((1,), (1,)), ((), ()))
BY_ROWS = (((0,), (0,)), ((), ()))


def place():
    return lax.axis_index("row"), lax.axis_index(STRIP)


def device_at(row, strip):
    pairs = lax.axis_size("pair")
    return (lax.axis_index("grp"), row, lax.div(strip, pairs), lax.rem(strip, pairs))


def sems(count):
    return [pltpu.SemaphoreType.DMA((count,)), pltpu.SemaphoreType.DMA((count,))]


def around(count, me):
    return lambda step: lax.rem(me + step, count)


def far_first(count, me):
    def peer(step):
        up = step - 1
        up += jnp.where(up >= me, 1, 0)
        down = count - step
        down -= jnp.where(down <= me, 1, 0)
        return jnp.where(me < count // 2, down, up)

    return peer


def post(count, me, order, device_of, source, landing, send_sem, recv_sem):
    def copy_of(step, slot):
        peer = order(step)
        return pltpu.make_async_remote_copy(
            src_ref=source(peer),
            dst_ref=landing.at[slot(peer)],
            send_sem=send_sem.at[step],
            recv_sem=recv_sem.at[slot(peer)],
            device_id=device_of(peer),
            device_id_type=MESH,
        )

    @pl.loop(1, count)
    def _(step):
        copy_of(step, lambda peer: me).start()

    def finish():
        @pl.loop(1, count)
        def _(step):
            copy_of(step, lambda peer: me).wait_send()
            copy_of(step, lambda peer: peer).wait_recv()

    return finish


def iota(shape, dim):
    return lax.broadcasted_iota(jnp.int32, shape, dim)


def dot(a, b, numbers=(((1,), (0,)), ((), ()))):
    return lax.dot_general(a, b, numbers, preferred_element_type=F32)


def slope(values):
    s = 1.0 / (1.0 + jnp.exp(-values))
    return s * (1.0 + values * (1.0 - s))


def total_of(count, landing):
    value = landing[0].astype(F32)
    for i in range(1, count):
        value += landing[i].astype(F32)
    return value


def whole_kernel(
    rows, strips, band, height2, scale_one, scale_two,
    x_any, f1_any, f2_any, up_any,
    ig_out, g1_out, g2_out,
    x_in, f1, f2, up_in, x_wide, x_turned, own, edges_f, edges, from_side, from_row, from_corner, from_up,
    tile, patches, w1, spread_one, pre, block_f, block, gathered, up_wide, up, pool_f, pool3, near3, spread,
    blocks, landed, grad_f, grad, grad_own, rims_f, rims, rim_rows, rim_side, rim_row, rim_corner, pool_all, near_all, pool_map, near_map,
    mine_blocks, one_landed, one_part, one_parts, one_mine, one_all, g1_wide,
    load_sem, a_send, a_recv, e_send, e_recv, b_send, b_recv, c_send, c_recv,
    d1_send, d1_recv, d2_send, d2_recv, d3_send, d3_recv,
    p_send, p_on, p_recv, n_send, n_on, n_recv,
):
    row, strip = place()
    cols, pairs = lax.axis_size("col"), lax.axis_size("pair")
    col, pair = lax.axis_index("col"), lax.axis_index("pair")
    channels = f1.shape[1]
    filters = f2.shape[1]
    quads = 4 * channels
    width = x_in.shape[1]
    width2 = width // 4
    band2 = band // 4
    span = width2 + 2 * EDGE
    full2 = width2 * strips
    mid = pl.ds(EDGE, width2)
    reach = width2 + 4

    def row_device(i):
        return device_at(i, strip)

    def strip_device(i):
        return device_at(row, i)

    def there(way):
        a, b = row + way[0], strip + way[1]
        return (a >= 0) & (a < rows) & (b >= 0) & (b < strips)

    barrier = pltpu.get_barrier_semaphore()
    for step in range(1, rows):
        pl.semaphore_signal(barrier, inc=1, device_id=row_device(lax.rem(row + step, rows)), device_id_type=MESH)
    for step in range(1, strips):
        pl.semaphore_signal(
            barrier, inc=1, device_id=strip_device(lax.rem(strip + step, strips)), device_id_type=MESH
        )
    for way in DIAGONALS:
        @pl.when(there(way))
        def _(way=way):
            pl.semaphore_signal(
                barrier, inc=1, device_id=device_at(row + way[0], strip + way[1]), device_id_type=MESH
            )
    loads = [
        pltpu.make_async_copy(source, target, load_sem.at[n])
        for n, (source, target) in enumerate([(x_any, x_in), (up_any, up_in), (f1_any, f1), (f2_any, f2)])
    ]
    for load in loads:
        load.start()

    shape = (width, width)
    pick = (iota(shape, 1) == 4 * (iota(shape, 0) % width2) + iota(shape, 0) // width2).astype(BF)
    low_half = iota((width2, 128), 1) < channels
    loads[0].wait()
    x_wide[...] = x_in[...].astype(F32)
    for h in range(band):
        line = x_wide[pl.ds(h, channels, stride=band), :].astype(BF)
        x_turned[pl.ds(2 * h * channels, channels), :] = line
        x_turned[pl.ds((2 * h + 1) * channels, channels), :] = line
    turned = dot(pick, x_turned[...], BY_LANES)
    for h in range(band):
        lanes = slice(h * 128, (h + 1) * 128)
        for half in range(2):
            even = turned[2 * half * width2 : (2 * half + 1) * width2, lanes]
            odd = turned[(2 * half + 1) * width2 : (2 * half + 2) * width2, lanes]
            value = jnp.where(low_half, even, odd)
            tile[h + 1, mid, pl.ds(half * 128, 128)] = value
            own[pl.ds(h * width2, width2), pl.ds(half * 128, 128)] = value.astype(BF)
    for h in range(band):
        edges_f[0, pl.ds(h * EDGE, EDGE)] = tile[h + 1, pl.ds(EDGE, EDGE)]
        edges_f[1, pl.ds(h * EDGE, EDGE)] = tile[h + 1, pl.ds(width2, EDGE)]
    edges[...] = edges_f[:, : band * EDGE].astype(BF)
    loads[1].wait()

    diagonals = (jnp.where(row > 0, 1, 0) + jnp.where(row < rows - 1, 1, 0)) * (
        jnp.where(strip > 0, 1, 0) + jnp.where(strip < strips - 1, 1, 0)
    )
    pl.semaphore_wait(barrier, rows - 1 + strips - 1 + diagonals)
    edge_rows = band * EDGE
    up_edge = 2 * height2

    def corner_of(way):
        return (way[1] + 1) // 2, (way[0] + 1) // 2

    def border(kind, way, arriving=False):
        (source_of, slot_of, send_sem, recv_sem), back = kind, (-way[0], -way[1])
        land = way if arriving else back
        return pltpu.make_async_remote_copy(
            src_ref=source_of(way),
            dst_ref=slot_of(land),
            send_sem=send_sem.at[WAYS.index(way)],
            recv_sem=recv_sem.at[WAYS.index(land)],
            device_id=device_at(row + way[0], strip + way[1]),
            device_id_type=MESH,
        )

    def start_border(kind, way):
        @pl.when(there(way))
        def _():
            border(kind, way).start()

    def clear_border(kind, way):
        @pl.when(jnp.logical_not(there(way)))
        def _():
            slot = kind[1](way)
            slot[...] = jnp.zeros(slot.shape, slot.dtype)

    def end_border(kind, way):
        @pl.when(there(way))
        def _():
            border(kind, way, True).wait_recv()

    def sent_border(kind, way):
        @pl.when(there(way))
        def _():
            border(kind, way).wait_send()

    def slots(side_slots, row_slots, corner_slots):
        def slot_of(way):
            side, top = corner_of(way)
            if way[0] == 0:
                return side_slots.at[side]
            if way[1] == 0:
                return row_slots.at[top]
            return corner_slots.at[2 * top + side]

        return slot_of

    def cell_source(way):
        side = corner_of(way)[0]
        if way[0] == 0:
            return edges.at[side]
        if way[1] == 0:
            return own.at[pl.ds(0 if way[0] < 0 else (band - 1) * width2, width2)]
        return edges.at[side, pl.ds(0 if way[0] < 0 else edge_rows - 16, 16)]

    def rim_source(way):
        side, top = corner_of(way)
        return rim_rows.at[top] if way[1] == 0 else rims.at[side]

    cell_kind = (cell_source, slots(from_side, from_row, from_corner), a_send, a_recv)
    rim_kind = (rim_source, slots(rim_side, rim_row, rim_corner), e_send, e_recv)

    def up_border(side, arriving=False):
        land = side if arriving else 1 - side
        return pltpu.make_async_remote_copy(
            src_ref=up_in.at[pl.ds(0 if side == 0 else up_in.shape[0] - up_edge, up_edge)],
            dst_ref=from_up.at[land],
            send_sem=a_send.at[len(WAYS) + side],
            recv_sem=a_recv.at[len(WAYS) + land],
            device_id=device_at(row, strip + (-1, 1)[side]),
            device_id_type=MESH,
        )

    for way in WAYS:
        start_border(cell_kind, way)
    for way in WAYS:
        clear_border(cell_kind, way)
        clear_border(rim_kind, way)
    for side in range(2):
        @pl.when(there((0, (-1, 1)[side])))
        def _(side=side):
            up_border(side).start()

        @pl.when(jnp.logical_not(there((0, (-1, 1)[side]))))
        def _(side=side):
            from_up[side] = jnp.zeros(from_up.shape[1:], BF)

    loads[2].wait()
    zero = jnp.zeros((channels, channels), F32)
    nothing = jnp.zeros((channels, 128), BF)
    for i in range(3):
        a, b, c = [f1[3 * i + j].astype(F32) for j in range(3)]
        bc, ab, za, cz = [
            jnp.concatenate(two, 1).astype(BF) for two in ((b, c), (a, b), (zero, a), (c, zero))
        ]
        table = (
            (bc, nothing, za, nothing),
            (ab, cz, nothing, nothing),
            (za, bc, nothing, nothing),
            (nothing, ab, nothing, cz),
        )
        for p in range(4):
            for k in range(4):
                w1[pl.ds(p * channels, channels), pl.ds(i * 512 + k * 128, 128)] = table[p][k]
    shape = (quads, quads)
    for i in range(2):
        target = 4 * (iota(shape, 0) % channels) + 2 * i + iota(shape, 0) // (2 * channels)
        spread_one[pl.ds(i * quads, quads)] = (iota(shape, 1) == target).astype(BF)

    def widen(line):
        here = tile[line]
        patches[line, :, pl.ds(0, quads)] = here.astype(BF)
        patches[line, :, pl.ds(quads, 128)] = pltpu.roll(here[:, quads - 128 :], 1, 0).astype(BF)
        patches[line, :, pl.ds(quads + 128, 128)] = pltpu.roll(here[:, :128], span - 1, 0).astype(BF)

    def silu(values):
        return values / (1.0 + jnp.exp(-values))

    def pool(h):
        total = (silu(pre[h]) + silu(pre[h + 1])) * 0.25
        upper = total.astype(BF)
        both = jnp.concatenate([upper, (total - upper.astype(F32)).astype(BF)], 0)
        both = dot(both, spread_one[pl.ds((h // 2) % 2 * quads, quads)])
        return both[:span] + both[span:]

    side_at = [pl.ds(0, EDGE), pl.ds(EDGE + width2, EDGE)]
    for way in WAYS[:2]:
        end_border(cell_kind, way)
    for side in range(2):
        edge = from_side[side].astype(F32)
        for h in range(band):
            tile[h + 1, side_at[side]] = edge[h * EDGE : (h + 1) * EDGE]
    for line in range(1, band + 1):
        widen(line)
    windows = jnp.concatenate(
        [patches[1 + i : band - 1 + i].reshape((band - 2) * span, 512) for i in range(3)], 1
    )
    pre[1 : band - 1] = dot(windows, w1[...], BY_LANES).reshape(band - 2, span, quads)
    halves = {h: pool(h) for h in range(2, band - 2, 2)}

    for way in WAYS[2:]:
        end_border(cell_kind, way)
    for top in range(2):
        line = 0 if top == 0 else band + 1
        tile[line, mid] = from_row[top].astype(F32)
        for side in range(2):
            corner = from_corner[2 * top + side].astype(F32)
            tile[line, side_at[side]] = corner[16 - EDGE :] if top == 0 else corner[:EDGE]
        widen(line)
    windows = jnp.concatenate(
        [jnp.concatenate([patches[i], patches[band - 1 + i]], 0) for i in range(3)], 1
    )
    ends = dot(windows, w1[...], BY_LANES)
    pre[0] = ends[:span]
    pre[band - 1] = ends[span:]
    for h in (0, band - 2):
        halves[h] = pool(h)
    pooled = jnp.concatenate([halves[4 * u] + halves[4 * u + 2] for u in range(band2)], 0)
    at_col = strip * width2 - EDGE + iota((band2 * span, quads), 0) % span
    pooled = jnp.where((at_col >= 0) & (at_col < full2), pooled, 0.0)
    for u in range(band2):
        block_f[pl.ds(u * reach, reach)] = pooled[u * span + 2 : u * span + 2 + reach]
    pooled = block_f[: band2 * reach].astype(BF)
    block[...] = pooled
    finish = post(rows, row, far_first(rows, row), row_device, lambda peer: block, gathered, b_send, b_recv)
    gathered[row] = pooled

    for h in range(band):
        pre[h] = slope(pre[h]) * 0.25
    grad_f[...] = jnp.zeros(grad_f.shape, F32)
    rims_f[...] = jnp.zeros(rims_f.shape, F32)
    for u in range(height2):
        pool_f[u, pl.ds(0, 2)] = jnp.zeros((2, quads), F32)
        pool_f[u, pl.ds(2 + reach, 2)] = jnp.zeros((2, quads), F32)
    for side in range(2):
        @pl.when(there((0, (-1, 1)[side])))
        def _(side=side):
            up_border(side, True).wait_recv()
    up_wide[pl.ds(0, up_edge)] = from_up[0].astype(F32)
    up_wide[pl.ds(up_edge, width2 * height2)] = up_in[...].astype(F32)
    up_wide[pl.ds(up_edge + width2 * height2, up_edge)] = from_up[1].astype(F32)
    for u in range(height2):
        up[u, pl.ds(0, 2)] = jnp.zeros((2, filters), F32)
        up[u, pl.ds(2, width2 + 4)] = up_wide[pl.ds(u, width2 + 4, stride=height2), :]
        up[u, pl.ds(width2 + 6, 2)] = jnp.zeros((2, filters), F32)
    pool3[0] = jnp.zeros(pool3.shape[1:], BF)
    pool3[height2 + 1] = jnp.zeros(pool3.shape[1:], BF)
    for j in range(3):
        near3[j, 0] = jnp.zeros(near3.shape[2:], BF)
        near3[j, height2 + 1] = jnp.zeros(near3.shape[2:], BF)
    loads[3].wait()
    finish()

    def across(source, table, send_sem, recv_sem, step):
        return pltpu.make_async_remote_copy(
            src_ref=source,
            dst_ref=table.at[strip],
            send_sem=send_sem.at[step],
            recv_sem=recv_sem.at[strip],
            device_id=device_at(row, lax.rem(col + step, cols) * pairs + pair),
            device_id_type=MESH,
        )

    def onward(table, send_sem, recv_sem, column, step):
        slot = column * pairs + pair
        return pltpu.make_async_remote_copy(
            src_ref=table.at[slot],
            dst_ref=table.at[slot],
            send_sem=send_sem.at[column * pairs + step],
            recv_sem=recv_sem.at[slot],
            device_id=device_at(row, col * pairs + lax.rem(pair + step, pairs)),
            device_id_type=MESH,
        )

    def arrival(table, send_sem, recv_sem, slot):
        return pltpu.make_async_remote_copy(
            src_ref=table.at[slot],
            dst_ref=table.at[slot],
            send_sem=send_sem.at[0],
            recv_sem=recv_sem.at[slot],
            device_id=device_at(row, lax.rem(col + 1, cols) * pairs + pair),
            device_id_type=MESH,
        )

    def share(table, send_sem, on_sem, recv_sem):
        for step in range(1, cols):
            across(table.at[strip], table, send_sem, recv_sem, step).start()
        for step in range(1, pairs):
            onward(table, on_sem, recv_sem, col, step).start()

    def pass_on(table, send_sem, on_sem, recv_sem):
        for step in range(1, cols):
            column = lax.rem(col + step, cols)
            arrival(table, send_sem, recv_sem, column * pairs + pair).wait_recv()
            for other in range(1, pairs):
                onward(table, on_sem, recv_sem, column, other).start()

    def settle(table, send_sem, on_sem, recv_sem):
        for step in range(1, cols):
            across(table.at[strip], table, send_sem, recv_sem, step).wait_send()
        for step in range(cols):
            column = lax.rem(col + step, cols)
            for other in range(1, pairs):
                onward(table, on_sem, recv_sem, column, other).wait_send()
                slot = column * pairs + lax.rem(pair + other, pairs)
                arrival(table, send_sem, recv_sem, slot).wait_recv()

    for u in range(height2):
        r, k = divmod(u, band2)
        pool_f[u, pl.ds(2, reach)] = gathered[r].astype(F32)[k * reach : (k + 1) * reach]
        wide = pool_f[u]
        pool3[u + 1, :, pl.ds(0, quads)] = pltpu.roll(wide, 1, 0).astype(BF)
        pool3[u + 1, :, pl.ds(quads, quads)] = wide.astype(BF)
        pool3[u + 1, :, pl.ds(2 * quads, quads)] = pltpu.roll(wide, span - 1, 0).astype(BF)
        pool_all[strip, pl.ds(u * width2, width2)] = wide[EDGE : EDGE + width2].astype(BF)
    pool_sems = (p_send, p_on, p_recv)
    share(pool_all, *pool_sems)
    spots = height2 * span
    windows = jnp.concatenate([pool3[i : i + height2].reshape(spots, 3 * quads) for i in range(3)], 1)
    kernel = jnp.concatenate([f2[t] for t in range(9)], 1)
    pre_two = dot(windows, kernel, BY_LANES)
    near = up[0:height2].reshape(spots, filters) * slope(pre_two)
    near3[0, 1 : height2 + 1] = pltpu.roll(near, spots - 1, 0).astype(BF).reshape(height2, span, filters)
    near3[1, 1 : height2 + 1] = near.astype(BF).reshape(height2, span, filters)
    near3[2, 1 : height2 + 1] = pltpu.roll(near, 1, 0).astype(BF).reshape(height2, span, filters)
    total = jnp.zeros((spots, quads), F32)
    if filters % 128 == 0:
        windows = [near3[j, 2 - i : 2 - i + height2].reshape(spots, filters) for i in range(3) for j in range(3)]
        total = dot(jnp.concatenate(windows, 1), f2[...].reshape(9 * filters, quads))
    else:
        for t in range(9):
            i, j = divmod(t, 3)
            total += dot(near3[j, 2 - i : 2 - i + height2].reshape(spots, filters), f2[t])
    spread[...] = total.reshape(height2, span, quads)

    def fill(peer):
        for k in range(band2):
            cell = spread[peer * band2 + k]
            blocks[peer, pl.ds(k * width2, width2)] = cell[EDGE : EDGE + width2].astype(BF)

    for peer in range(rows):
        fill(peer)
    finish = post(rows, row, far_first(rows, row), row_device, lambda peer: blocks.at[peer], landed, c_send, c_recv)
    landed[row] = blocks[row]
    for u in range(height2):
        near_all[strip, pl.ds(u * width2, width2)] = near[
            u * span + EDGE : u * span + EDGE + width2
        ].astype(BF)
    near_sems = (n_send, n_on, n_recv)
    share(near_all, *near_sems)
    pass_on(pool_all, *pool_sems)
    finish()
    parts = total_of(rows, landed).astype(BF)
    parts = dot(parts, spread_one[...], BY_LANES)

    pass_on(near_all, *near_sems)
    for h in range(band):
        k, i = h // 4, (h // 2) % 2
        body = parts[k * width2 : (k + 1) * width2, i * quads : (i + 1) * quads] * pre[h, mid]
        grad_f[h + 1, mid] = body
        grad_own[h] = grad_f[h + 1].astype(BF)
        rims_f[0, pl.ds(h, 1)] = body[:1]
        rims_f[1, pl.ds(h, 1)] = body[width2 - 1 :]
        if h in (0, band - 1):
            rim_rows[h // (band - 1)] = body.astype(BF)
    rims[...] = rims_f[...].astype(BF)
    for way in WAYS:
        start_border(rim_kind, way)

    low = iota((channels, 128), 1) < channels
    halves, ends = [], []
    own_spots = band * span
    windows = jnp.concatenate([patches[i : i + band].reshape(own_spots, 512) for i in range(3)], 1)
    taps = dot(grad_own[...].reshape(own_spots, quads), windows, BY_ROWS)

    def cut(i, p, k):
        return taps[p * channels : (p + 1) * channels, i * 512 + k * 128 : i * 512 + (k + 1) * 128]

    for i in range(3):
        bc = pltpu.roll(cut(i, 0, 0) + cut(i, 2, 1), 64, 1)
        ab = cut(i, 1, 0) + cut(i, 3, 1)
        za = pltpu.roll(cut(i, 0, 2) + cut(i, 2, 0), 64, 1)
        cz = cut(i, 1, 1) + cut(i, 3, 3)
        halves.append(ab + jnp.where(low, za, bc))
        ends.append(cz + bc)
    packed = halves + [jnp.where(low, ends[0], pltpu.roll(ends[1], 64, 1)), jnp.where(low, ends[2], 0.0)]
    packed = jnp.concatenate(packed, 0).astype(BF)
    piece = mine_blocks.shape[1]
    for s in range(strips):
        start, stop = s * piece, min((s + 1) * piece, packed.shape[0])
        if stop > start:
            mine_blocks[s, pl.ds(0, stop - start)] = packed[start:stop]
        if stop - start < piece:
            begin = max(stop - start, 0)
            mine_blocks[s, pl.ds(begin, piece - begin)] = jnp.zeros((piece - begin, 128), BF)
    finish = post(strips, strip, around(strips, strip), strip_device, lambda peer: mine_blocks.at[peer], one_landed, d1_send, d1_recv)
    one_landed[strip] = mine_blocks[strip]

    settle(pool_all, *pool_sems)
    settle(near_all, *near_sems)
    near_map[0] = jnp.zeros(near_map.shape[1:], BF)
    near_map[height2 + 1] = jnp.zeros(near_map.shape[1:], BF)
    at_lane = iota((filters, full2), 1)

    def assemble(u):
        at = u * width2
        if not isinstance(u, int):
            at = pl.multiple_of(at, width2)
        line = [near_all[s, pl.ds(at, width2)].astype(F32) for s in range(strips)]
        line = jnp.concatenate(line, 0).T
        after = jnp.where(at_lane < full2 - 1, pltpu.roll(line, full2 - 1, 1), 0.0)
        before = jnp.where(at_lane > 0, pltpu.roll(line, 1, 1), 0.0)
        for j, value in enumerate((after, line, before)):
            near_map[u + 1, pl.ds(j * filters, filters)] = value.astype(BF)
        for s in range(strips):
            pool_map[u, pl.ds(s * width2, width2)] = pool_all[s, pl.ds(at, width2)]

    chunk = max(1, 1024 // full2)
    steps = height2 // chunk
    if steps == 1:
        for u in range(height2):
            assemble(u)
    else:
        pl.loop(0, height2)(assemble)

    def filter_taps(i, step):
        at = step * chunk
        left = jnp.concatenate([near_map[at + k + 2 - i] for k in range(chunk)], 1)
        right = pool_map[pl.ds(at, chunk)].reshape(chunk * full2, quads)
        return scale_two * dot(left, right).reshape(3, filters, quads)

    def filter_gradient(i):
        g2_out[3 * i : 3 * i + 3] = filter_taps(i, 0)
        if steps > 1:
            @pl.loop(1, steps)
            def _(step):
                g2_out[3 * i : 3 * i + 3] += filter_taps(i, step)

    filter_gradient(0)

    finish()
    part = total_of(strips, one_landed).astype(BF)
    one_part[...] = part
    finish = post(rows, row, far_first(rows, row), row_device, lambda peer: one_part, one_parts, d2_send, d2_recv)
    one_parts[row] = part

    for way in WAYS:
        end_border(rim_kind, way)
    for h in range(band):
        for side, at in ((0, EDGE - 1), (1, EDGE + width2)):
            grad_f[h + 1, pl.ds(at, 1)] = rim_side[side].astype(F32)[h : h + 1]
    for top, line, h in ((0, 0, band - 1), (1, band + 1, 0)):
        grad_f[line, mid] = rim_row[top].astype(F32)
        for side, at in ((0, EDGE - 1), (1, EDGE + width2)):
            grad_f[line, pl.ds(at, 1)] = rim_corner[2 * top + side].astype(F32)[h : h + 1]
    for line in range(band + 2):
        grad[line] = grad_f[line].astype(BF)
    cells = jnp.concatenate([grad[2 - i : 2 - i + band].reshape(own_spots, quads) for i in range(3)], 1)
    kernel = jnp.concatenate([w1[:, i * 512 : (i + 1) * 512] for i in range(3)], 0)
    total = dot(cells, kernel)
    before = pltpu.roll(total[:, quads : quads + 128], own_spots - 1, 0)
    after = pltpu.roll(total[:, quads + 128 :], 1, 0)
    sides = (total[:, :128] + after, total[:, 128:quads] + before)
    turned = []
    for h in range(band):
        lines_of = []
        for b in range(4):
            value = sides[b // 2][h * span + EDGE : h * span + EDGE + width2]
            lines_of.append(jnp.where(low_half == (b % 2 == 0), value, 0.0).astype(BF))
        turned.append(jnp.concatenate(lines_of, 0))
    turned = dot(jnp.concatenate(turned, 1), pick, BY_ROWS)
    for h in range(band):
        at = 2 * h * channels
        x_wide[pl.ds(h, channels, stride=band), :] = (
            turned[at : at + channels] + turned[at + channels : at + 2 * channels]
        )
    ig_out[...] = x_wide[...].astype(BF)

    filter_gradient(1)
    finish()
    part = total_of(rows, one_parts).astype(BF)
    one_mine[...] = part
    finish = post(strips, strip, around(strips, strip), strip_device, lambda peer: one_mine, one_all, d3_send, d3_recv)
    one_all[strip] = part
    filter_gradient(2)
    for way in WAYS:
        sent_border(cell_kind, way)
        sent_border(rim_kind, way)
    for side in range(2):
        @pl.when(there((0, (-1, 1)[side])))
        def _(side=side):
            up_border(side).wait_send()
    finish()
    done = scale_one * one_all[...].astype(F32).reshape(strips * piece, 128)
    rolled = pltpu.roll(done, 64, 1)
    for i in range(3):
        for j in range(3):
            k = i if j < 2 else 3 + i // 2
            value = done if (j if j < 2 else i % 2) == 0 else rolled
            g1_out[3 * i + j] = value[k * channels : (k + 1) * channels, :channels]


def write_kernel(*refs):
    count = len(refs) // 2
    sources, targets, sem = refs[:count], refs[count:-1], refs[-1]
    copies = [pltpu.make_async_copy(sources[n], targets[n], sem.at[n]) for n in range(count)]
    for copy in copies:
        copy.start()
    for copy in copies:
        copy.wait()


def write_out(*arrays):
    arrays = [pltpu.with_memory_space_constraint(a, pltpu.VMEM) for a in arrays]
    return pl.pallas_call(
        write_kernel,
        out_shape=tuple(jax.ShapeDtypeStruct(a.shape, a.dtype) for a in arrays),
        in_specs=[VMEM] * len(arrays),
        out_specs=(HBM,) * len(arrays),
        scratch_shapes=[pltpu.SemaphoreType.DMA((len(arrays),))],
    )(*arrays)


def local(features_in, filters_one, filters_two, out_grad):
    channels, band, width = features_in.shape
    rows, strips = lax.axis_size("row"), lax.axis_size(STRIP)
    cols, pairs = lax.axis_size("col"), lax.axis_size("pair")
    filters = filters_two.shape[0]
    quads = 4 * channels
    height2 = out_grad.shape[2]
    width2, band2 = width // 4, band // 4
    span = width2 + 2 * EDGE
    full2 = width2 * strips
    spots = band2 * width2
    piece = -(-5 * channels // strips // 16) * 16

    def v(shape, kind=BF):
        return pltpu.VMEM(shape, kind)

    scratch = [
        v((channels * band, width)),
        v((9, channels, channels)),
        v((9, filters, quads)),
        v((width2 * height2, filters)),
        v((channels * band, width), F32),
        v((2 * channels * band, width)),
        v((band * width2, quads)),
        v((2, band * EDGE + 8, quads), F32),
        v((2, band * EDGE, quads)),
        v((2, band * EDGE, quads)),
        v((2, width2, quads)),
        v((4, 16, quads)),
        v((2, 2 * height2, filters)),
        v((band + 3, span, quads), F32),
        v((band + 2, span, 512)),
        v((quads, 3 * 512)),
        v((2 * quads, quads)),
        v((band + 1, span, quads), F32),
        v((band2 * (width2 + 4) + 8, quads), F32),
        v((band2 * (width2 + 4), quads)),
        v((rows, band2 * (width2 + 4), quads)),
        v((span * height2, filters), F32),
        v((height2 + 1, span, filters), F32),
        v((height2 + 1, span, quads), F32),
        v((height2 + 2, span, 3 * quads)),
        v((3, height2 + 2, span, filters)),
        v((height2, span, quads), F32),
        v((rows, spots, quads)),
        v((rows, spots, quads)),
        v((band + 3, span, quads), F32),
        v((band + 2, span, quads)),
        v((band, span, quads)),
        v((2, 16, quads), F32),
        v((2, 16, quads)),
        v((2, width2, quads)),
        v((2, 16, quads)),
        v((2, width2, quads)),
        v((4, 16, quads)),
        v((strips, height2 * width2, quads)),
        v((strips, height2 * width2, filters)),
        v((height2, full2, quads)),
        v((height2 + 2, 3 * filters, full2)),
        v((strips, piece, 128)),
        v((strips, piece, 128)),
        v((piece, 128)),
        v((rows, piece, 128)),
        v((piece, 128)),
        v((strips, piece, 128)),
        v((8, 128)),
        pltpu.SemaphoreType.DMA((4,)),
    ]
    scratch += sems(len(WAYS) + 2) + sems(len(WAYS)) + sems(rows) + sems(rows) + sems(strips) + sems(rows) + sems(strips)
    for _ in range(2):
        scratch += [
            pltpu.SemaphoreType.DMA((cols,)),
            pltpu.SemaphoreType.DMA((cols * pairs,)),
            pltpu.SemaphoreType.DMA((strips,)),
        ]
    arguments = (
        features_in.reshape(channels * band, width),
        jnp.transpose(filters_one, (1, 2, 0, 3)).reshape(9, channels, channels),
        jnp.transpose(filters_two, (1, 2, 0, 3)).reshape(9, filters, quads),
        jnp.transpose(out_grad, (1, 2, 0)).reshape(width2 * height2, filters),
    )
    arguments = [pltpu.with_memory_space_constraint(a, pltpu.HBM) for a in arguments]
    share = 1 if rows * strips <= 64 else 2
    scale_one = 1.0 / math.sqrt(band * rows * width * strips)
    scale_two = 1.0 / math.sqrt(height2 * full2)
    ig, g1, g2 = pl.pallas_call(
        functools.partial(whole_kernel, rows, strips, band, height2, scale_one, scale_two),
        out_shape=(
            jax.ShapeDtypeStruct((channels * band, width), BF),
            jax.ShapeDtypeStruct((9, channels, channels), F32),
            jax.ShapeDtypeStruct((9, filters, quads), F32),
        ),
        in_specs=[HBM] * 4,
        out_specs=(VMEM,) * 3,
        scratch_shapes=scratch,
        compiler_params=pltpu.CompilerParams(
            collective_id=0, has_side_effects=True, vmem_limit_bytes=share * 28 * 1024 * 1024
        ),
    )(*arguments)
    ig, g1, g2 = write_out(ig, g1, g2)
    grad_one = jnp.transpose(g1.reshape(3, 3, channels, channels), (2, 0, 1, 3))
    grad_two = jnp.transpose(g2.reshape(3, 3, filters, quads), (2, 0, 1, 3))
    return (ig.reshape(channels, band, width), grad_one, grad_two)


def solution(mesh):
    in_specs = (
        P("grp", "row", ("col", "pair")),
        P(),
        P("row", None, None, None),
        P(("grp", "row"), ("col", "pair"), None),
    )
    out_specs = (
        P("grp", "row", ("col", "pair")),
        P("grp", None, None, None),
        P(("grp", "row"), None, None, None),
    )
    return jax.shard_map(local, mesh=mesh, in_specs=in_specs, out_specs=out_specs, check_vma=False)
```

```python
import functools
import math

import jax
import jax.numpy as jnp
from jax import lax
from jax.experimental import pallas as pl
from jax.experimental.pallas import tpu as pltpu
from jax.sharding import PartitionSpec as P

MESH = pl.DeviceIdType.MESH
VMEM = pl.BlockSpec(memory_space=pltpu.VMEM)
HBM = pl.BlockSpec(memory_space=pltpu.HBM)
STRIP = ("col", "pair")
BF = jnp.bfloat16
F32 = jnp.float32

EDGE = 4

DIAGONALS = [(a, b) for a in (-1, 1) for b in (-1, 1)]
WAYS = [(0, -1), (0, 1), (-1, 0), (1, 0)] + DIAGONALS

BY_LANES = (((1,), (1,)), ((), ()))
BY_ROWS = (((0,), (0,)), ((), ()))


def place():
    return lax.axis_index("row"), lax.axis_index(STRIP)


def device_at(row, strip):
    pairs = lax.axis_size("pair")
    return (lax.axis_index("grp"), row, lax.div(strip, pairs), lax.rem(strip, pairs))


def sems(count):
    return [pltpu.SemaphoreType.DMA((count,)), pltpu.SemaphoreType.DMA((count,))]


def around(count, me):
    return lambda step: lax.rem(me + step, count)


def far_first(count, me):
    def peer(step):
        up = step - 1
        up += jnp.where(up >= me, 1, 0)
        down = count - step
        down -= jnp.where(down <= me, 1, 0)
        return jnp.where(me < count // 2, down, up)

    return peer


def post(count, me, order, device_of, source, landing, send_sem, recv_sem):
    def copy_of(step, slot):
        peer = order(step)
        return pltpu.make_async_remote_copy(
            src_ref=source(peer),
            dst_ref=landing.at[slot(peer)],
            send_sem=send_sem.at[step],
            recv_sem=recv_sem.at[slot(peer)],
            device_id=device_of(peer),
            device_id_type=MESH,
        )

    def start(low=1, high=count):
        @pl.loop(low, high)
        def _(step):
            copy_of(step, lambda peer: me).start()

    def finish(low=1, high=count):
        @pl.loop(low, high)
        def _(step):
            copy_of(step, lambda peer: me).wait_send()
            copy_of(step, lambda peer: peer).wait_recv()

    return start, finish


def iota(shape, dim):
    return lax.broadcasted_iota(jnp.int32, shape, dim)


def dot(a, b, numbers=(((1,), (0,)), ((), ()))):
    return lax.dot_general(a, b, numbers, preferred_element_type=F32)


def slope(values):
    s = 1.0 / (1.0 + jnp.exp(-values))
    return s * (1.0 + values * (1.0 - s))


def total_of(count, landing):
    value = landing[0].astype(F32)
    for i in range(1, count):
        value += landing[i].astype(F32)
    return value


def whole_kernel(
    rows, strips, band, height2, scale_one, scale_two,
    x_any, f1_any, f2_any, up_any,
    ig_out, g1_out, g2_out,
    x_in, f1, f2, up_in, x_wide, x_turned, own, edges_f, edges, from_side, from_row, from_corner, from_up,
    tile, patches, w1, w1_down, spread_one, spread_back, f2_down, pre, block_f, block, gathered, up_wide, up, pool_f, pool3, near3, sum_two,
    blocks, landed, grad_f, grad, grad_own, rims_f, rims, rim_rows, rim_side, rim_row, rim_corner, pool_all, near_all, pool_map, near_map,
    mine_blocks, one_landed, one_part, one_parts, one_mine, one_all, g1_wide,
    load_sem, a_send, a_recv, e_send, e_recv, b_send, b_recv, c_send, c_recv,
    d1_send, d1_recv, d2_send, d2_recv, d3_send, d3_recv,
    p_send, p_on, p_recv, n_send, n_on, n_recv,
):
    row, strip = place()
    cols, pairs = lax.axis_size("col"), lax.axis_size("pair")
    col, pair = lax.axis_index("col"), lax.axis_index("pair")
    channels = f1.shape[1]
    filters = f2.shape[1]
    quads = 4 * channels
    width = x_in.shape[1]
    width2 = width // 4
    band2 = band // 4
    span = width2 + 2 * EDGE
    full2 = width2 * strips
    mid = pl.ds(EDGE, width2)
    reach = width2 + 4

    def row_device(i):
        return device_at(i, strip)

    def strip_device(i):
        return device_at(row, i)

    def there(way):
        a, b = row + way[0], strip + way[1]
        return (a >= 0) & (a < rows) & (b >= 0) & (b < strips)

    barrier = pltpu.get_barrier_semaphore()
    for step in range(1, rows):
        pl.semaphore_signal(barrier, inc=1, device_id=row_device(lax.rem(row + step, rows)), device_id_type=MESH)
    for step in range(1, strips):
        pl.semaphore_signal(
            barrier, inc=1, device_id=strip_device(lax.rem(strip + step, strips)), device_id_type=MESH
        )
    for way in DIAGONALS:
        @pl.when(there(way))
        def _(way=way):
            pl.semaphore_signal(
                barrier, inc=1, device_id=device_at(row + way[0], strip + way[1]), device_id_type=MESH
            )
    loads = [
        pltpu.make_async_copy(source, target, load_sem.at[n])
        for n, (source, target) in enumerate([(x_any, x_in), (up_any, up_in), (f1_any, f1), (f2_any, f2)])
    ]
    for load in loads:
        load.start()

    shape = (width, width)
    pick = (iota(shape, 1) == 4 * (iota(shape, 0) % width2) + iota(shape, 0) // width2).astype(BF)
    low_half = iota((width2, 128), 1) < channels
    shape = (quads, quads)
    for i in range(2):
        target = 4 * (iota(shape, 0) % channels) + 2 * i + iota(shape, 0) // (2 * channels)
        spread_one[pl.ds(i * quads, quads)] = (iota(shape, 1) == target).astype(BF)
        target = 4 * (iota(shape, 1) % channels) + 2 * i + iota(shape, 1) // (2 * channels)
        spread_back[:, pl.ds(i * quads, quads)] = (iota(shape, 0) == target).astype(BF)
    grad_f[...] = jnp.zeros(grad_f.shape, F32)
    rims_f[...] = jnp.zeros(rims_f.shape, F32)
    sum_two[...] = jnp.zeros(sum_two.shape, F32)
    for u in range(height2):
        pool_f[u, pl.ds(0, 2)] = jnp.zeros((2, quads), F32)
        pool_f[u, pl.ds(2 + reach, 2)] = jnp.zeros((2, quads), F32)
    for j in range(3):
        near3[j, 0] = jnp.zeros(near3.shape[2:], BF)
        near3[j, height2 + 1] = jnp.zeros(near3.shape[2:], BF)
    loads[0].wait()
    x_wide[...] = x_in[...].astype(F32)
    for h in range(band):
        line = x_wide[pl.ds(h, channels, stride=band), :].astype(BF)
        x_turned[pl.ds(2 * h * channels, channels), :] = line
        x_turned[pl.ds((2 * h + 1) * channels, channels), :] = line
    turned = dot(pick, x_turned[...], BY_LANES)
    for h in range(band):
        lanes = slice(h * 128, (h + 1) * 128)
        for half in range(2):
            even = turned[2 * half * width2 : (2 * half + 1) * width2, lanes]
            odd = turned[(2 * half + 1) * width2 : (2 * half + 2) * width2, lanes]
            value = jnp.where(low_half, even, odd)
            tile[h + 1, mid, pl.ds(half * 128, 128)] = value
            own[pl.ds(h * width2, width2), pl.ds(half * 128, 128)] = value.astype(BF)
    for h in range(band):
        edges_f[0, pl.ds(h * EDGE, EDGE)] = tile[h + 1, pl.ds(EDGE, EDGE)]
        edges_f[1, pl.ds(h * EDGE, EDGE)] = tile[h + 1, pl.ds(width2, EDGE)]
    edges[...] = edges_f[:, : band * EDGE].astype(BF)

    diagonals = (jnp.where(row > 0, 1, 0) + jnp.where(row < rows - 1, 1, 0)) * (
        jnp.where(strip > 0, 1, 0) + jnp.where(strip < strips - 1, 1, 0)
    )
    pl.semaphore_wait(barrier, rows - 1 + strips - 1 + diagonals)
    edge_rows = band * EDGE
    up_edge = 2 * height2

    def corner_of(way):
        return (way[1] + 1) // 2, (way[0] + 1) // 2

    def border(kind, way, arriving=False):
        (source_of, slot_of, send_sem, recv_sem), back = kind, (-way[0], -way[1])
        land = way if arriving else back
        return pltpu.make_async_remote_copy(
            src_ref=source_of(way),
            dst_ref=slot_of(land),
            send_sem=send_sem.at[WAYS.index(way)],
            recv_sem=recv_sem.at[WAYS.index(land)],
            device_id=device_at(row + way[0], strip + way[1]),
            device_id_type=MESH,
        )

    def start_border(kind, way):
        @pl.when(there(way))
        def _():
            border(kind, way).start()

    def clear_border(kind, way):
        @pl.when(jnp.logical_not(there(way)))
        def _():
            slot = kind[1](way)
            slot[...] = jnp.zeros(slot.shape, slot.dtype)

    def end_border(kind, way):
        @pl.when(there(way))
        def _():
            border(kind, way, True).wait_recv()

    def sent_border(kind, way):
        @pl.when(there(way))
        def _():
            border(kind, way).wait_send()

    def slots(side_slots, row_slots, corner_slots):
        def slot_of(way):
            side, top = corner_of(way)
            if way[0] == 0:
                return side_slots.at[side]
            if way[1] == 0:
                return row_slots.at[top]
            return corner_slots.at[2 * top + side]

        return slot_of

    def cell_source(way):
        side = corner_of(way)[0]
        if way[0] == 0:
            return edges.at[side]
        if way[1] == 0:
            return own.at[pl.ds(0 if way[0] < 0 else (band - 1) * width2, width2)]
        return edges.at[side, pl.ds(0 if way[0] < 0 else edge_rows - 16, 16)]

    def rim_source(way):
        side, top = corner_of(way)
        return rim_rows.at[top] if way[1] == 0 else rims.at[side]

    cell_kind = (cell_source, slots(from_side, from_row, from_corner), a_send, a_recv)
    rim_kind = (rim_source, slots(rim_side, rim_row, rim_corner), e_send, e_recv)

    def up_border(side, arriving=False):
        land = side if arriving else 1 - side
        return pltpu.make_async_remote_copy(
            src_ref=up_in.at[pl.ds(0 if side == 0 else up_in.shape[0] - up_edge, up_edge)],
            dst_ref=from_up.at[land],
            send_sem=a_send.at[len(WAYS) + side],
            recv_sem=a_recv.at[len(WAYS) + land],
            device_id=device_at(row, strip + (-1, 1)[side]),
            device_id_type=MESH,
        )

    for way in WAYS:
        start_border(cell_kind, way)
    for way in WAYS:
        clear_border(cell_kind, way)
        clear_border(rim_kind, way)
    loads[1].wait()
    for side in range(2):
        @pl.when(there((0, (-1, 1)[side])))
        def _(side=side):
            up_border(side).start()

        @pl.when(jnp.logical_not(there((0, (-1, 1)[side]))))
        def _(side=side):
            from_up[side] = jnp.zeros(from_up.shape[1:], BF)

    loads[2].wait()
    zero = jnp.zeros((channels, channels), F32)
    nothing = jnp.zeros((channels, 128), BF)
    for i in range(3):
        a, b, c = [f1[3 * i + j].astype(F32) for j in range(3)]
        bc, ab, za, cz = [
            jnp.concatenate(two, 1).astype(BF) for two in ((b, c), (a, b), (zero, a), (c, zero))
        ]
        table = (
            (bc, nothing, za, nothing),
            (ab, cz, nothing, nothing),
            (za, bc, nothing, nothing),
            (nothing, ab, nothing, cz),
        )
        for p in range(4):
            for k in range(4):
                w1[pl.ds(p * channels, channels), pl.ds(i * 512 + k * 128, 128)] = table[p][k]
    for k in range(12):
        w1_down[pl.ds(k * 128, 128)] = w1[:, pl.ds(k * 128, 128)].astype(F32).T.astype(BF)

    def widen(line):
        here = tile[line]
        patches[line, :, pl.ds(0, quads)] = here.astype(BF)
        patches[line, :, pl.ds(quads, 128)] = pltpu.roll(here[:, quads - 128 :], 1, 0).astype(BF)
        patches[line, :, pl.ds(quads + 128, 128)] = pltpu.roll(here[:, :128], span - 1, 0).astype(BF)

    def silu(values):
        return values / (1.0 + jnp.exp(-values))

    def pool(h):
        total = (silu(pre[h]) + silu(pre[h + 1])) * 0.25
        upper = total.astype(BF)
        both = jnp.concatenate([upper, (total - upper.astype(F32)).astype(BF)], 0)
        both = dot(both, spread_one[pl.ds((h // 2) % 2 * quads, quads)])
        return both[:span] + both[span:]

    side_at = [pl.ds(0, EDGE), pl.ds(EDGE + width2, EDGE)]
    for way in WAYS[:2]:
        end_border(cell_kind, way)
    for side in range(2):
        edge = from_side[side].astype(F32)
        for h in range(band):
            tile[h + 1, side_at[side]] = edge[h * EDGE : (h + 1) * EDGE]
    for line in range(1, band + 1):
        widen(line)
    windows = jnp.concatenate(
        [patches[1 + i : band - 1 + i].reshape((band - 2) * span, 512) for i in range(3)], 1
    )
    pre[1 : band - 1] = dot(windows, w1_down[...]).reshape(band - 2, span, quads)
    halves = {h: pool(h) for h in range(2, band - 2, 2)}

    for way in WAYS[2:]:
        end_border(cell_kind, way)
    for top in range(2):
        line = 0 if top == 0 else band + 1
        tile[line, mid] = from_row[top].astype(F32)
        for side in range(2):
            corner = from_corner[2 * top + side].astype(F32)
            tile[line, side_at[side]] = corner[16 - EDGE :] if top == 0 else corner[:EDGE]
        widen(line)
    windows = jnp.concatenate(
        [jnp.concatenate([patches[i], patches[band - 1 + i]], 0) for i in range(3)], 1
    )
    ends = dot(windows, w1_down[...])
    pre[0] = ends[:span]
    pre[band - 1] = ends[span:]
    for h in (0, band - 2):
        halves[h] = pool(h)
    pooled = jnp.concatenate([halves[4 * u] + halves[4 * u + 2] for u in range(band2)], 0)
    at_col = strip * width2 - EDGE + iota((band2 * span, quads), 0) % span
    pooled = jnp.where((at_col >= 0) & (at_col < full2), pooled, 0.0)
    for u in range(band2):
        block_f[pl.ds(u * reach, reach)] = pooled[u * span + 2 : u * span + 2 + reach]
    pooled = block_f[: band2 * reach].astype(BF)
    block[...] = pooled
    start, finish = post(rows, row, far_first(rows, row), row_device, lambda peer: block, gathered, b_send, b_recv)
    start()
    gathered[row] = pooled

    for h in range(band):
        pre[h] = slope(pre[h]) * 0.25
    for side in range(2):
        @pl.when(there((0, (-1, 1)[side])))
        def _(side=side):
            up_border(side, True).wait_recv()
    up_wide[pl.ds(0, up_edge)] = from_up[0].astype(F32)
    up_wide[pl.ds(up_edge, width2 * height2)] = up_in[...].astype(F32)
    up_wide[pl.ds(up_edge + width2 * height2, up_edge)] = from_up[1].astype(F32)
    for u in range(height2):
        up[u, pl.ds(0, 2)] = jnp.zeros((2, filters), F32)
        up[u, pl.ds(2, width2 + 4)] = up_wide[pl.ds(u, width2 + 4, stride=height2), :]
        up[u, pl.ds(width2 + 6, 2)] = jnp.zeros((2, filters), F32)
    loads[3].wait()
    for t in range(9):
        f2_down[t // 3, pl.ds(t % 3 * quads, quads)] = f2[t].astype(F32).T.astype(BF)

    half, bands = height2 // 2, rows // 2
    near_band = jnp.where(row < bands, 0, bands)
    far_band = bands - near_band

    def forward(band_at):
        at = band_at * band2
        for d in range(half):
            k = d % band2
            pool_f[at + d, pl.ds(2, reach)] = gathered[band_at + d // band2].astype(F32)[
                k * reach : (k + 1) * reach
            ]
            wide = pool_f[at + d]
            pool3[at + d, :, pl.ds(0, quads)] = pltpu.roll(wide, 1, 0).astype(BF)
            pool3[at + d, :, pl.ds(quads, quads)] = wide.astype(BF)
            pool3[at + d, :, pl.ds(2 * quads, quads)] = pltpu.roll(wide, span - 1, 0).astype(BF)
            spot = pl.multiple_of((at + d) * width2, width2)
            pool_all[strip, pl.ds(spot, width2)] = wide[EDGE : EDGE + width2].astype(BF)
        windows = pool3[pl.ds(at, half)].reshape(half * span, 3 * quads)
        if filters % 128 == 0:
            sums = dot(windows, jnp.concatenate([f2_down[i] for i in range(3)], 1))
            sums = [sums[:, i * filters : (i + 1) * filters] for i in range(3)]
        else:
            sums = [dot(windows, f2_down[i]) for i in range(3)]
        for i in range(3):
            sum_two[pl.ds(at + 2 - i, half)] += sums[i].reshape(half, span, filters)

    finish(bands + 1, rows)
    forward(near_band)
    finish(1, bands + 1)
    def across(source, table, send_sem, recv_sem, step):
        return pltpu.make_async_remote_copy(
            src_ref=source,
            dst_ref=table.at[strip],
            send_sem=send_sem.at[step],
            recv_sem=recv_sem.at[strip],
            device_id=device_at(row, lax.rem(col + step, cols) * pairs + pair),
            device_id_type=MESH,
        )

    def onward(table, send_sem, recv_sem, column, step):
        slot = column * pairs + pair
        return pltpu.make_async_remote_copy(
            src_ref=table.at[slot],
            dst_ref=table.at[slot],
            send_sem=send_sem.at[column * pairs + step],
            recv_sem=recv_sem.at[slot],
            device_id=device_at(row, col * pairs + lax.rem(pair + step, pairs)),
            device_id_type=MESH,
        )

    def arrival(table, send_sem, recv_sem, slot):
        return pltpu.make_async_remote_copy(
            src_ref=table.at[slot],
            dst_ref=table.at[slot],
            send_sem=send_sem.at[0],
            recv_sem=recv_sem.at[slot],
            device_id=device_at(row, lax.rem(col + 1, cols) * pairs + pair),
            device_id_type=MESH,
        )

    def share(table, send_sem, on_sem, recv_sem):
        for step in range(1, cols):
            across(table.at[strip], table, send_sem, recv_sem, step).start()
        for step in range(1, pairs):
            onward(table, on_sem, recv_sem, col, step).start()

    def pass_on(table, send_sem, on_sem, recv_sem):
        for step in range(1, cols):
            column = lax.rem(col + step, cols)
            arrival(table, send_sem, recv_sem, column * pairs + pair).wait_recv()
            for other in range(1, pairs):
                onward(table, on_sem, recv_sem, column, other).start()

    def settle(table, send_sem, on_sem, recv_sem):
        for step in range(1, cols):
            across(table.at[strip], table, send_sem, recv_sem, step).wait_send()
        for step in range(cols):
            column = lax.rem(col + step, cols)
            for other in range(1, pairs):
                onward(table, on_sem, recv_sem, column, other).wait_send()
                slot = column * pairs + lax.rem(pair + other, pairs)
                arrival(table, send_sem, recv_sem, slot).wait_recv()

    forward(far_band)
    pool_sems = (p_send, p_on, p_recv)
    share(pool_all, *pool_sems)
    spots = height2 * span
    pre_two = sum_two[1 : height2 + 1].reshape(spots, filters)
    near = up[0:height2].reshape(spots, filters) * slope(pre_two)
    near3[0, 1 : height2 + 1] = pltpu.roll(near, spots - 1, 0).astype(BF).reshape(height2, span, filters)
    near3[1, 1 : height2 + 1] = near.astype(BF).reshape(height2, span, filters)
    near3[2, 1 : height2 + 1] = pltpu.roll(near, 1, 0).astype(BF).reshape(height2, span, filters)

    def backward(band_at):
        at = band_at * band2
        windows = [
            near3[j, pl.ds(at + 2 - i, half)].reshape(half * span, filters) for i in range(3) for j in range(3)
        ]
        if filters % 128 == 0:
            total = dot(jnp.concatenate(windows, 1), f2[...].reshape(9 * filters, quads))
        else:
            total = jnp.zeros((half * span, quads), F32)
            for t in range(9):
                total += dot(windows[t], f2[t])
        for d in range(half):
            blocks[band_at + d // band2, pl.ds(d % band2 * width2, width2)] = total[
                d * span + EDGE : d * span + EDGE + width2
            ].astype(BF)

    start, finish = post(
        rows, row, far_first(rows, row), row_device, lambda peer: blocks.at[peer], landed, c_send, c_recv
    )
    backward(far_band)
    start(1, bands + 1)
    backward(near_band)
    start(bands + 1, rows)
    landed[row] = blocks[row]
    for u in range(height2):
        near_all[strip, pl.ds(u * width2, width2)] = near[
            u * span + EDGE : u * span + EDGE + width2
        ].astype(BF)
    near_sems = (n_send, n_on, n_recv)
    share(near_all, *near_sems)
    finish()
    parts = total_of(rows, landed).astype(BF)
    parts = dot(parts, spread_back[...])

    for h in range(band):
        k, i = h // 4, (h // 2) % 2
        body = parts[k * width2 : (k + 1) * width2, i * quads : (i + 1) * quads] * pre[h, mid]
        grad_f[h + 1, mid] = body
        grad_own[h] = grad_f[h + 1].astype(BF)
        rims_f[0, pl.ds(h, 1)] = body[:1]
        rims_f[1, pl.ds(h, 1)] = body[width2 - 1 :]
        if h in (0, band - 1):
            rim_rows[h // (band - 1)] = body.astype(BF)
    rims[...] = rims_f[...].astype(BF)
    for way in WAYS:
        start_border(rim_kind, way)

    low = iota((channels, 128), 1) < channels
    halves, ends = [], []
    own_spots = band * span
    windows = jnp.concatenate([patches[i : i + band].reshape(own_spots, 512) for i in range(3)], 1)
    taps = dot(grad_own[...].reshape(own_spots, quads), windows, BY_ROWS)

    def cut(i, p, k):
        return taps[p * channels : (p + 1) * channels, i * 512 + k * 128 : i * 512 + (k + 1) * 128]

    for i in range(3):
        bc = pltpu.roll(cut(i, 0, 0) + cut(i, 2, 1), 64, 1)
        ab = cut(i, 1, 0) + cut(i, 3, 1)
        za = pltpu.roll(cut(i, 0, 2) + cut(i, 2, 0), 64, 1)
        cz = cut(i, 1, 1) + cut(i, 3, 3)
        halves.append(ab + jnp.where(low, za, bc))
        ends.append(cz + bc)
    packed = halves + [jnp.where(low, ends[0], pltpu.roll(ends[1], 64, 1)), jnp.where(low, ends[2], 0.0)]
    packed = jnp.concatenate(packed, 0).astype(BF)
    piece = mine_blocks.shape[1]
    for s in range(strips):
        start, stop = s * piece, min((s + 1) * piece, packed.shape[0])
        if stop > start:
            mine_blocks[s, pl.ds(0, stop - start)] = packed[start:stop]
        if stop - start < piece:
            begin = max(stop - start, 0)
            mine_blocks[s, pl.ds(begin, piece - begin)] = jnp.zeros((piece - begin, 128), BF)
    start, finish = post(strips, strip, around(strips, strip), strip_device, lambda peer: mine_blocks.at[peer], one_landed, d1_send, d1_recv)
    start()
    one_landed[strip] = mine_blocks[strip]

    pass_on(pool_all, *pool_sems)
    pass_on(near_all, *near_sems)
    settle(pool_all, *pool_sems)
    settle(near_all, *near_sems)
    near_map[0] = jnp.zeros(near_map.shape[1:], BF)
    near_map[height2 + 1] = jnp.zeros(near_map.shape[1:], BF)
    at_lane = iota((filters, full2), 1)

    def assemble(u):
        at = u * width2
        if not isinstance(u, int):
            at = pl.multiple_of(at, width2)
        line = [near_all[s, pl.ds(at, width2)].astype(F32) for s in range(strips)]
        line = jnp.concatenate(line, 0).T
        after = jnp.where(at_lane < full2 - 1, pltpu.roll(line, full2 - 1, 1), 0.0)
        before = jnp.where(at_lane > 0, pltpu.roll(line, 1, 1), 0.0)
        for j, value in enumerate((after, line, before)):
            near_map[u + 1, pl.ds(j * filters, filters)] = value.astype(BF)
        for s in range(strips):
            pool_map[u, pl.ds(s * width2, width2)] = pool_all[s, pl.ds(at, width2)]

    chunk = max(1, 1024 // full2)
    steps = height2 // chunk
    if steps == 1:
        for u in range(height2):
            assemble(u)
    else:
        pl.loop(0, height2)(assemble)

    def filter_taps(i, step):
        at = step * chunk
        left = jnp.concatenate([near_map[at + k + 2 - i] for k in range(chunk)], 1)
        right = pool_map[pl.ds(at, chunk)].reshape(chunk * full2, quads)
        return scale_two * dot(left, right).reshape(3, filters, quads)

    def filter_gradient(i):
        g2_out[3 * i : 3 * i + 3] = filter_taps(i, 0)
        if steps > 1:
            @pl.loop(1, steps)
            def _(step):
                g2_out[3 * i : 3 * i + 3] += filter_taps(i, step)

    finish()
    part = total_of(strips, one_landed).astype(BF)
    one_part[...] = part
    start, finish = post(rows, row, far_first(rows, row), row_device, lambda peer: one_part, one_parts, d2_send, d2_recv)
    start()
    one_parts[row] = part

    for way in WAYS:
        end_border(rim_kind, way)
    for h in range(band):
        for side, at in ((0, EDGE - 1), (1, EDGE + width2)):
            grad_f[h + 1, pl.ds(at, 1)] = rim_side[side].astype(F32)[h : h + 1]
    for top, line, h in ((0, 0, band - 1), (1, band + 1, 0)):
        grad_f[line, mid] = rim_row[top].astype(F32)
        for side, at in ((0, EDGE - 1), (1, EDGE + width2)):
            grad_f[line, pl.ds(at, 1)] = rim_corner[2 * top + side].astype(F32)[h : h + 1]
    for line in range(band + 2):
        grad[line] = grad_f[line].astype(BF)
    cells = jnp.concatenate([grad[2 - i : 2 - i + band].reshape(own_spots, quads) for i in range(3)], 1)
    kernel = jnp.concatenate([w1[:, i * 512 : (i + 1) * 512] for i in range(3)], 0)
    total = dot(cells, kernel)
    before = pltpu.roll(total[:, quads : quads + 128], own_spots - 1, 0)
    after = pltpu.roll(total[:, quads + 128 :], 1, 0)
    sides = (total[:, :128] + after, total[:, 128:quads] + before)
    turned = []
    for h in range(band):
        lines_of = []
        for b in range(4):
            value = sides[b // 2][h * span + EDGE : h * span + EDGE + width2]
            lines_of.append(jnp.where(low_half == (b % 2 == 0), value, 0.0).astype(BF))
        turned.append(jnp.concatenate(lines_of, 0))
    turned = dot(jnp.concatenate(turned, 1), pick, BY_ROWS)
    for h in range(band):
        at = 2 * h * channels
        x_wide[pl.ds(h, channels, stride=band), :] = (
            turned[at : at + channels] + turned[at + channels : at + 2 * channels]
        )
    ig_out[...] = x_wide[...].astype(BF)

    filter_gradient(0)
    filter_gradient(1)
    finish()
    part = total_of(rows, one_parts).astype(BF)
    one_mine[...] = part
    start, finish = post(strips, strip, around(strips, strip), strip_device, lambda peer: one_mine, one_all, d3_send, d3_recv)
    start()
    one_all[strip] = part
    filter_gradient(2)
    for way in WAYS:
        sent_border(cell_kind, way)
        sent_border(rim_kind, way)
    for side in range(2):
        @pl.when(there((0, (-1, 1)[side])))
        def _(side=side):
            up_border(side).wait_send()
    finish()
    done = scale_one * one_all[...].astype(F32).reshape(strips * piece, 128)
    rolled = pltpu.roll(done, 64, 1)
    for i in range(3):
        for j in range(3):
            k = i if j < 2 else 3 + i // 2
            value = done if (j if j < 2 else i % 2) == 0 else rolled
            g1_out[3 * i + j] = value[k * channels : (k + 1) * channels, :channels]


def write_kernel(*refs):
    count = len(refs) // 2
    sources, targets, sem = refs[:count], refs[count:-1], refs[-1]
    copies = [pltpu.make_async_copy(sources[n], targets[n], sem.at[n]) for n in range(count)]
    for copy in copies:
        copy.start()
    for copy in copies:
        copy.wait()


def write_out(*arrays):
    arrays = [pltpu.with_memory_space_constraint(a, pltpu.VMEM) for a in arrays]
    return pl.pallas_call(
        write_kernel,
        out_shape=tuple(jax.ShapeDtypeStruct(a.shape, a.dtype) for a in arrays),
        in_specs=[VMEM] * len(arrays),
        out_specs=(HBM,) * len(arrays),
        scratch_shapes=[pltpu.SemaphoreType.DMA((len(arrays),))],
    )(*arrays)


def local(features_in, filters_one, filters_two, out_grad):
    channels, band, width = features_in.shape
    rows, strips = lax.axis_size("row"), lax.axis_size(STRIP)
    cols, pairs = lax.axis_size("col"), lax.axis_size("pair")
    filters = filters_two.shape[0]
    quads = 4 * channels
    height2 = out_grad.shape[2]
    width2, band2 = width // 4, band // 4
    span = width2 + 2 * EDGE
    full2 = width2 * strips
    spots = band2 * width2
    piece = -(-5 * channels // strips // 16) * 16

    def v(shape, kind=BF):
        return pltpu.VMEM(shape, kind)

    scratch = [
        v((channels * band, width)),
        v((9, channels, channels)),
        v((9, filters, quads)),
        v((width2 * height2, filters)),
        v((channels * band, width), F32),
        v((2 * channels * band, width)),
        v((band * width2, quads)),
        v((2, band * EDGE + 8, quads), F32),
        v((2, band * EDGE, quads)),
        v((2, band * EDGE, quads)),
        v((2, width2, quads)),
        v((4, 16, quads)),
        v((2, 2 * height2, filters)),
        v((band + 3, span, quads), F32),
        v((band + 2, span, 512)),
        v((quads, 3 * 512)),
        v((3 * 512, quads)),
        v((2 * quads, quads)),
        v((quads, 2 * quads)),
        v((3, 3 * quads, filters)),
        v((band + 1, span, quads), F32),
        v((band2 * (width2 + 4) + 8, quads), F32),
        v((band2 * (width2 + 4), quads)),
        v((rows, band2 * (width2 + 4), quads)),
        v((span * height2, filters), F32),
        v((height2 + 1, span, filters), F32),
        v((height2 + 1, span, quads), F32),
        v((height2, span, 3 * quads)),
        v((3, height2 + 2, span, filters)),
        v((height2 + 2, span, filters), F32),
        v((rows, spots, quads)),
        v((rows, spots, quads)),
        v((band + 3, span, quads), F32),
        v((band + 2, span, quads)),
        v((band, span, quads)),
        v((2, 16, quads), F32),
        v((2, 16, quads)),
        v((2, width2, quads)),
        v((2, 16, quads)),
        v((2, width2, quads)),
        v((4, 16, quads)),
        v((strips, height2 * width2, quads)),
        v((strips, height2 * width2, filters)),
        v((height2, full2, quads)),
        v((height2 + 2, 3 * filters, full2)),
        v((strips, piece, 128)),
        v((strips, piece, 128)),
        v((piece, 128)),
        v((rows, piece, 128)),
        v((piece, 128)),
        v((strips, piece, 128)),
        v((8, 128)),
        pltpu.SemaphoreType.DMA((4,)),
    ]
    scratch += sems(len(WAYS) + 2) + sems(len(WAYS)) + sems(rows) + sems(rows) + sems(strips) + sems(rows) + sems(strips)
    for _ in range(2):
        scratch += [
            pltpu.SemaphoreType.DMA((cols,)),
            pltpu.SemaphoreType.DMA((cols * pairs,)),
            pltpu.SemaphoreType.DMA((strips,)),
        ]
    arguments = (
        features_in.reshape(channels * band, width),
        jnp.transpose(filters_one, (1, 2, 0, 3)).reshape(9, channels, channels),
        jnp.transpose(filters_two, (1, 2, 0, 3)).reshape(9, filters, quads),
        jnp.transpose(out_grad, (1, 2, 0)).reshape(width2 * height2, filters),
    )
    arguments = [pltpu.with_memory_space_constraint(a, pltpu.HBM) for a in arguments]
    share = 1 if rows * strips <= 64 else 2
    scale_one = 1.0 / math.sqrt(band * rows * width * strips)
    scale_two = 1.0 / math.sqrt(height2 * full2)
    ig, g1, g2 = pl.pallas_call(
        functools.partial(whole_kernel, rows, strips, band, height2, scale_one, scale_two),
        out_shape=(
            jax.ShapeDtypeStruct((channels * band, width), BF),
            jax.ShapeDtypeStruct((9, channels, channels), F32),
            jax.ShapeDtypeStruct((9, filters, quads), F32),
        ),
        in_specs=[HBM] * 4,
        out_specs=(VMEM,) * 3,
        scratch_shapes=scratch,
        compiler_params=pltpu.CompilerParams(
            collective_id=0, has_side_effects=True, vmem_limit_bytes=share * 28 * 1024 * 1024
        ),
    )(*arguments)
    ig, g1, g2 = write_out(ig, g1, g2)
    grad_one = jnp.transpose(g1.reshape(3, 3, channels, channels), (2, 0, 1, 3))
    grad_two = jnp.transpose(g2.reshape(3, 3, filters, quads), (2, 0, 1, 3))
    return (ig.reshape(channels, band, width), grad_one, grad_two)


def solution(mesh):
    in_specs = (
        P("grp", "row", ("col", "pair")),
        P(),
        P("row", None, None, None),
        P(("grp", "row"), ("col", "pair"), None),
    )
    out_specs = (
        P("grp", "row", ("col", "pair")),
        P("grp", None, None, None),
        P(("grp", "row"), None, None, None),
    )
    return jax.shard_map(local, mesh=mesh, in_specs=in_specs, out_specs=out_specs, check_vma=False)
```

```python
import functools
import math

import jax
import jax.numpy as jnp
from jax import lax
from jax.experimental import pallas as pl
from jax.experimental.pallas import tpu as pltpu
from jax.sharding import PartitionSpec as P

MESH = pl.DeviceIdType.MESH
VMEM = pl.BlockSpec(memory_space=pltpu.VMEM)
HBM = pl.BlockSpec(memory_space=pltpu.HBM)
STRIP = ("col", "pair")
BF = jnp.bfloat16
F32 = jnp.float32

EDGE = 4

DIAGONALS = [(a, b) for a in (-1, 1) for b in (-1, 1)]
WAYS = [(0, -1), (0, 1), (-1, 0), (1, 0)] + DIAGONALS

BY_LANES = (((1,), (1,)), ((), ()))
BY_ROWS = (((0,), (0,)), ((), ()))


def place():
    return lax.axis_index("row"), lax.axis_index(STRIP)


def device_at(row, strip):
    pairs = lax.axis_size("pair")
    return (lax.axis_index("grp"), row, lax.div(strip, pairs), lax.rem(strip, pairs))


def sems(count):
    return [pltpu.SemaphoreType.DMA((count,)), pltpu.SemaphoreType.DMA((count,))]


def around(count, me):
    return lambda step: lax.rem(me + step, count)


def far_first(count, me):
    def peer(step):
        up = step - 1
        up += jnp.where(up >= me, 1, 0)
        down = count - step
        down -= jnp.where(down <= me, 1, 0)
        return jnp.where(me < count // 2, down, up)

    return peer


def post(count, me, order, device_of, source, landing, send_sem, recv_sem):
    def copy_of(step, slot):
        peer = order(step)
        return pltpu.make_async_remote_copy(
            src_ref=source(peer),
            dst_ref=landing.at[slot(peer)],
            send_sem=send_sem.at[step],
            recv_sem=recv_sem.at[slot(peer)],
            device_id=device_of(peer),
            device_id_type=MESH,
        )

    def start(low=1, high=count):
        @pl.loop(low, high)
        def _(step):
            copy_of(step, lambda peer: me).start()

    def finish(low=1, high=count):
        @pl.loop(low, high)
        def _(step):
            copy_of(step, lambda peer: me).wait_send()
            copy_of(step, lambda peer: peer).wait_recv()

    return start, finish


def iota(shape, dim):
    return lax.broadcasted_iota(jnp.int32, shape, dim)


def dot(a, b, numbers=(((1,), (0,)), ((), ()))):
    return lax.dot_general(a, b, numbers, preferred_element_type=F32)


def slope(values):
    s = 1.0 / (1.0 + jnp.exp(-values))
    return s * (1.0 + values * (1.0 - s))


def total_of(count, landing):
    value = landing[0].astype(F32)
    for i in range(1, count):
        value += landing[i].astype(F32)
    return value


def whole_kernel(
    rows, strips, band, height2, scale_one, scale_two,
    x_any, f1_any, f2_any, up_any,
    ig_out, g1_out, g2_out,
    x_in, f1, f2, up_in, x_wide, x_turned, own, edges_f, edges, from_side, from_row, from_corner, from_up,
    tile, patches, w1, w1_down, spread_one, spread_back, f2_down, pre, block_f, block, gathered, up_wide, up, pool_f, pool3, near3, sum_two,
    blocks, landed, grad_f, grad, grad_own, rims_f, rims, rim_rows, rim_side, rim_row, rim_corner, pool_all, near_all, pool_map, near_map,
    mine_blocks, one_landed, one_part, one_all,
    load_sem, a_send, a_recv, e_send, e_recv, b_send, b_recv, c_send, c_recv,
    d1_send, d1_recv, d2_send, d2_recv,
    p_send, p_on, p_recv, n_send, n_on, n_recv,
):
    row, strip = place()
    cols, pairs = lax.axis_size("col"), lax.axis_size("pair")
    col, pair = lax.axis_index("col"), lax.axis_index("pair")
    channels = f1.shape[1]
    filters = f2.shape[1]
    quads = 4 * channels
    width = x_in.shape[1]
    width2 = width // 4
    band2 = band // 4
    span = width2 + 2 * EDGE
    full2 = width2 * strips
    mid = pl.ds(EDGE, width2)
    reach = width2 + 4

    def row_device(i):
        return device_at(i, strip)

    def strip_device(i):
        return device_at(row, i)

    def there(way):
        a, b = row + way[0], strip + way[1]
        return (a >= 0) & (a < rows) & (b >= 0) & (b < strips)

    barrier = pltpu.get_barrier_semaphore()
    everyone = rows * strips
    for step in range(1, rows):
        pl.semaphore_signal(barrier, inc=1, device_id=row_device(lax.rem(row + step, rows)), device_id_type=MESH)
    for step in range(1, strips):
        pl.semaphore_signal(
            barrier, inc=1, device_id=strip_device(lax.rem(strip + step, strips)), device_id_type=MESH
        )
    for way in DIAGONALS:
        @pl.when(there(way))
        def _(way=way):
            pl.semaphore_signal(
                barrier, inc=1, device_id=device_at(row + way[0], strip + way[1]), device_id_type=MESH
            )
    loads = [
        pltpu.make_async_copy(source, target, load_sem.at[n])
        for n, (source, target) in enumerate([(x_any, x_in), (up_any, up_in), (f1_any, f1), (f2_any, f2)])
    ]
    for load in loads:
        load.start()

    shape = (width, width)
    pick = (iota(shape, 1) == 4 * (iota(shape, 0) % width2) + iota(shape, 0) // width2).astype(BF)
    low_half = iota((width2, 128), 1) < channels
    shape = (quads, quads)
    for i in range(2):
        target = 4 * (iota(shape, 0) % channels) + 2 * i + iota(shape, 0) // (2 * channels)
        spread_one[pl.ds(i * quads, quads)] = (iota(shape, 1) == target).astype(BF)
        target = 4 * (iota(shape, 1) % channels) + 2 * i + iota(shape, 1) // (2 * channels)
        spread_back[:, pl.ds(i * quads, quads)] = (iota(shape, 0) == target).astype(BF)
    grad_f[...] = jnp.zeros(grad_f.shape, F32)
    rims_f[...] = jnp.zeros(rims_f.shape, F32)
    sum_two[...] = jnp.zeros(sum_two.shape, F32)
    for u in range(height2):
        pool_f[u, pl.ds(0, 2)] = jnp.zeros((2, quads), F32)
        pool_f[u, pl.ds(2 + reach, 2)] = jnp.zeros((2, quads), F32)
    for j in range(3):
        near3[j, 0] = jnp.zeros(near3.shape[2:], BF)
        near3[j, height2 + 1] = jnp.zeros(near3.shape[2:], BF)
    loads[0].wait()
    x_wide[...] = x_in[...].astype(F32)
    for h in range(band):
        line = x_wide[pl.ds(h, channels, stride=band), :].astype(BF)
        x_turned[pl.ds(2 * h * channels, channels), :] = line
        x_turned[pl.ds((2 * h + 1) * channels, channels), :] = line
    turned = dot(pick, x_turned[...], BY_LANES)
    for h in range(band):
        lanes = slice(h * 128, (h + 1) * 128)
        for half in range(2):
            even = turned[2 * half * width2 : (2 * half + 1) * width2, lanes]
            odd = turned[(2 * half + 1) * width2 : (2 * half + 2) * width2, lanes]
            value = jnp.where(low_half, even, odd)
            tile[h + 1, mid, pl.ds(half * 128, 128)] = value
            own[pl.ds(h * width2, width2), pl.ds(half * 128, 128)] = value.astype(BF)
    for h in range(band):
        edges_f[0, pl.ds(h * EDGE, EDGE)] = tile[h + 1, pl.ds(EDGE, EDGE)]
        edges_f[1, pl.ds(h * EDGE, EDGE)] = tile[h + 1, pl.ds(width2, EDGE)]
    edges[...] = edges_f[:, : band * EDGE].astype(BF)

    diagonals = (jnp.where(row > 0, 1, 0) + jnp.where(row < rows - 1, 1, 0)) * (
        jnp.where(strip > 0, 1, 0) + jnp.where(strip < strips - 1, 1, 0)
    )
    pl.semaphore_wait(barrier, rows - 1 + strips - 1 + diagonals)
    edge_rows = band * EDGE
    up_edge = 2 * height2

    def corner_of(way):
        return (way[1] + 1) // 2, (way[0] + 1) // 2

    def border(kind, way, arriving=False):
        (source_of, slot_of, send_sem, recv_sem), back = kind, (-way[0], -way[1])
        land = way if arriving else back
        return pltpu.make_async_remote_copy(
            src_ref=source_of(way),
            dst_ref=slot_of(land),
            send_sem=send_sem.at[WAYS.index(way)],
            recv_sem=recv_sem.at[WAYS.index(land)],
            device_id=device_at(row + way[0], strip + way[1]),
            device_id_type=MESH,
        )

    def start_border(kind, way):
        @pl.when(there(way))
        def _():
            border(kind, way).start()

    def clear_border(kind, way):
        @pl.when(jnp.logical_not(there(way)))
        def _():
            slot = kind[1](way)
            slot[...] = jnp.zeros(slot.shape, slot.dtype)

    def end_border(kind, way):
        @pl.when(there(way))
        def _():
            border(kind, way, True).wait_recv()

    def sent_border(kind, way):
        @pl.when(there(way))
        def _():
            border(kind, way).wait_send()

    def slots(side_slots, row_slots, corner_slots):
        def slot_of(way):
            side, top = corner_of(way)
            if way[0] == 0:
                return side_slots.at[side]
            if way[1] == 0:
                return row_slots.at[top]
            return corner_slots.at[2 * top + side]

        return slot_of

    def cell_source(way):
        side = corner_of(way)[0]
        if way[0] == 0:
            return edges.at[side]
        if way[1] == 0:
            return own.at[pl.ds(0 if way[0] < 0 else (band - 1) * width2, width2)]
        return edges.at[side, pl.ds(0 if way[0] < 0 else edge_rows - 16, 16)]

    def rim_source(way):
        side, top = corner_of(way)
        return rim_rows.at[top] if way[1] == 0 else rims.at[side]

    cell_kind = (cell_source, slots(from_side, from_row, from_corner), a_send, a_recv)
    rim_kind = (rim_source, slots(rim_side, rim_row, rim_corner), e_send, e_recv)

    def up_border(side, arriving=False):
        land = side if arriving else 1 - side
        return pltpu.make_async_remote_copy(
            src_ref=up_in.at[pl.ds(0 if side == 0 else up_in.shape[0] - up_edge, up_edge)],
            dst_ref=from_up.at[land],
            send_sem=a_send.at[len(WAYS) + side],
            recv_sem=a_recv.at[len(WAYS) + land],
            device_id=device_at(row, strip + (-1, 1)[side]),
            device_id_type=MESH,
        )

    for way in WAYS:
        start_border(cell_kind, way)
    for way in WAYS:
        clear_border(cell_kind, way)
        clear_border(rim_kind, way)
    loads[1].wait()
    for side in range(2):
        @pl.when(there((0, (-1, 1)[side])))
        def _(side=side):
            up_border(side).start()

        @pl.when(jnp.logical_not(there((0, (-1, 1)[side]))))
        def _(side=side):
            from_up[side] = jnp.zeros(from_up.shape[1:], BF)

    loads[2].wait()
    zero = jnp.zeros((channels, channels), F32)
    nothing = jnp.zeros((channels, 128), BF)
    for i in range(3):
        a, b, c = [f1[3 * i + j].astype(F32) for j in range(3)]
        bc, ab, za, cz = [
            jnp.concatenate(two, 1).astype(BF) for two in ((b, c), (a, b), (zero, a), (c, zero))
        ]
        table = (
            (bc, nothing, za, nothing),
            (ab, cz, nothing, nothing),
            (za, bc, nothing, nothing),
            (nothing, ab, nothing, cz),
        )
        for p in range(4):
            for k in range(4):
                w1[pl.ds(p * channels, channels), pl.ds(i * 512 + k * 128, 128)] = table[p][k]
    for k in range(12):
        w1_down[pl.ds(k * 128, 128)] = w1[:, pl.ds(k * 128, 128)].astype(F32).T.astype(BF)

    def widen(line):
        here = tile[line]
        patches[line, :, pl.ds(0, quads)] = here.astype(BF)
        patches[line, :, pl.ds(quads, 128)] = pltpu.roll(here[:, quads - 128 :], 1, 0).astype(BF)
        patches[line, :, pl.ds(quads + 128, 128)] = pltpu.roll(here[:, :128], span - 1, 0).astype(BF)

    def silu(values):
        return values / (1.0 + jnp.exp(-values))

    def pool(h):
        total = (silu(pre[h]) + silu(pre[h + 1])) * 0.25
        upper = total.astype(BF)
        both = jnp.concatenate([upper, (total - upper.astype(F32)).astype(BF)], 0)
        both = dot(both, spread_one[pl.ds((h // 2) % 2 * quads, quads)])
        return both[:span] + both[span:]

    side_at = [pl.ds(0, EDGE), pl.ds(EDGE + width2, EDGE)]
    for way in WAYS[:2]:
        end_border(cell_kind, way)
    for side in range(2):
        edge = from_side[side].astype(F32)
        for h in range(band):
            tile[h + 1, side_at[side]] = edge[h * EDGE : (h + 1) * EDGE]
    for line in range(1, band + 1):
        widen(line)
    windows = jnp.concatenate(
        [patches[1 + i : band - 1 + i].reshape((band - 2) * span, 512) for i in range(3)], 1
    )
    pre[1 : band - 1] = dot(windows, w1_down[...]).reshape(band - 2, span, quads)
    halves = {h: pool(h) for h in range(2, band - 2, 2)}

    for way in WAYS[2:]:
        end_border(cell_kind, way)
    for top in range(2):
        line = 0 if top == 0 else band + 1
        tile[line, mid] = from_row[top].astype(F32)
        for side in range(2):
            corner = from_corner[2 * top + side].astype(F32)
            tile[line, side_at[side]] = corner[16 - EDGE :] if top == 0 else corner[:EDGE]
        widen(line)
    windows = jnp.concatenate(
        [jnp.concatenate([patches[i], patches[band - 1 + i]], 0) for i in range(3)], 1
    )
    ends = dot(windows, w1_down[...])
    pre[0] = ends[:span]
    pre[band - 1] = ends[span:]
    for h in (0, band - 2):
        halves[h] = pool(h)
    pooled = jnp.concatenate([halves[4 * u] + halves[4 * u + 2] for u in range(band2)], 0)
    at_col = strip * width2 - EDGE + iota((band2 * span, quads), 0) % span
    pooled = jnp.where((at_col >= 0) & (at_col < full2), pooled, 0.0)
    for u in range(band2):
        block_f[pl.ds(u * reach, reach)] = pooled[u * span + 2 : u * span + 2 + reach]
    pooled = block_f[: band2 * reach].astype(BF)
    block[...] = pooled
    start, finish = post(rows, row, far_first(rows, row), row_device, lambda peer: block, gathered, b_send, b_recv)
    start()
    gathered[row] = pooled

    for h in range(band):
        pre[h] = slope(pre[h]) * 0.25
    for side in range(2):
        @pl.when(there((0, (-1, 1)[side])))
        def _(side=side):
            up_border(side, True).wait_recv()
    up_wide[pl.ds(0, up_edge)] = from_up[0].astype(F32)
    up_wide[pl.ds(up_edge, width2 * height2)] = up_in[...].astype(F32)
    up_wide[pl.ds(up_edge + width2 * height2, up_edge)] = from_up[1].astype(F32)
    for u in range(height2):
        up[u, pl.ds(0, 2)] = jnp.zeros((2, filters), F32)
        up[u, pl.ds(2, width2 + 4)] = up_wide[pl.ds(u, width2 + 4, stride=height2), :]
        up[u, pl.ds(width2 + 6, 2)] = jnp.zeros((2, filters), F32)
    loads[3].wait()
    for t in range(9):
        f2_down[t // 3, pl.ds(t % 3 * quads, quads)] = f2[t].astype(F32).T.astype(BF)

    half, bands = height2 // 2, rows // 2
    near_band = jnp.where(row < bands, 0, bands)
    far_band = bands - near_band

    def forward(band_at):
        at = band_at * band2
        for d in range(half):
            k = d % band2
            pool_f[at + d, pl.ds(2, reach)] = gathered[band_at + d // band2].astype(F32)[
                k * reach : (k + 1) * reach
            ]
            wide = pool_f[at + d]
            pool3[at + d, :, pl.ds(0, quads)] = pltpu.roll(wide, 1, 0).astype(BF)
            pool3[at + d, :, pl.ds(quads, quads)] = wide.astype(BF)
            pool3[at + d, :, pl.ds(2 * quads, quads)] = pltpu.roll(wide, span - 1, 0).astype(BF)
            spot = pl.multiple_of((at + d) * width2, width2)
            pool_all[strip, pl.ds(spot, width2)] = wide[EDGE : EDGE + width2].astype(BF)
        windows = pool3[pl.ds(at, half)].reshape(half * span, 3 * quads)
        if filters % 128 == 0:
            sums = dot(windows, jnp.concatenate([f2_down[i] for i in range(3)], 1))
            sums = [sums[:, i * filters : (i + 1) * filters] for i in range(3)]
        else:
            sums = [dot(windows, f2_down[i]) for i in range(3)]
        for i in range(3):
            sum_two[pl.ds(at + 2 - i, half)] += sums[i].reshape(half, span, filters)

    finish(bands + 1, rows)
    forward(near_band)
    finish(1, bands + 1)
    def across(source, table, send_sem, recv_sem, step):
        return pltpu.make_async_remote_copy(
            src_ref=source,
            dst_ref=table.at[strip],
            send_sem=send_sem.at[step],
            recv_sem=recv_sem.at[strip],
            device_id=device_at(row, lax.rem(col + step, cols) * pairs + pair),
            device_id_type=MESH,
        )

    def onward(table, send_sem, recv_sem, column, step):
        slot = column * pairs + pair
        return pltpu.make_async_remote_copy(
            src_ref=table.at[slot],
            dst_ref=table.at[slot],
            send_sem=send_sem.at[column * pairs + step],
            recv_sem=recv_sem.at[slot],
            device_id=device_at(row, col * pairs + lax.rem(pair + step, pairs)),
            device_id_type=MESH,
        )

    def arrival(table, send_sem, recv_sem, slot):
        return pltpu.make_async_remote_copy(
            src_ref=table.at[slot],
            dst_ref=table.at[slot],
            send_sem=send_sem.at[0],
            recv_sem=recv_sem.at[slot],
            device_id=device_at(row, lax.rem(col + 1, cols) * pairs + pair),
            device_id_type=MESH,
        )

    def share(table, send_sem, on_sem, recv_sem):
        for step in range(1, cols):
            across(table.at[strip], table, send_sem, recv_sem, step).start()
        for step in range(1, pairs):
            onward(table, on_sem, recv_sem, col, step).start()

    def pass_on(table, send_sem, on_sem, recv_sem):
        for step in range(1, cols):
            column = lax.rem(col + step, cols)
            arrival(table, send_sem, recv_sem, column * pairs + pair).wait_recv()
            for other in range(1, pairs):
                onward(table, on_sem, recv_sem, column, other).start()

    def settle(table, send_sem, on_sem, recv_sem):
        for step in range(1, cols):
            across(table.at[strip], table, send_sem, recv_sem, step).wait_send()
        for step in range(cols):
            column = lax.rem(col + step, cols)
            for other in range(1, pairs):
                onward(table, on_sem, recv_sem, column, other).wait_send()
                slot = column * pairs + lax.rem(pair + other, pairs)
                arrival(table, send_sem, recv_sem, slot).wait_recv()

    forward(far_band)
    pool_sems = (p_send, p_on, p_recv)
    share(pool_all, *pool_sems)
    spots = height2 * span
    pre_two = sum_two[1 : height2 + 1].reshape(spots, filters)
    near = up[0:height2].reshape(spots, filters) * slope(pre_two)
    near3[0, 1 : height2 + 1] = pltpu.roll(near, spots - 1, 0).astype(BF).reshape(height2, span, filters)
    near3[1, 1 : height2 + 1] = near.astype(BF).reshape(height2, span, filters)
    near3[2, 1 : height2 + 1] = pltpu.roll(near, 1, 0).astype(BF).reshape(height2, span, filters)

    def backward(band_at):
        at = band_at * band2
        windows = [
            near3[j, pl.ds(at + 2 - i, half)].reshape(half * span, filters) for i in range(3) for j in range(3)
        ]
        if filters % 128 == 0:
            total = dot(jnp.concatenate(windows, 1), f2[...].reshape(9 * filters, quads))
        else:
            total = jnp.zeros((half * span, quads), F32)
            for t in range(9):
                total += dot(windows[t], f2[t])
        for d in range(half):
            blocks[band_at + d // band2, pl.ds(d % band2 * width2, width2)] = total[
                d * span + EDGE : d * span + EDGE + width2
            ].astype(BF)

    start, finish = post(
        rows, row, far_first(rows, row), row_device, lambda peer: blocks.at[peer], landed, c_send, c_recv
    )
    backward(far_band)
    start(1, bands + 1)
    backward(near_band)
    start(bands + 1, rows)
    landed[row] = blocks[row]
    for u in range(height2):
        near_all[strip, pl.ds(u * width2, width2)] = near[
            u * span + EDGE : u * span + EDGE + width2
        ].astype(BF)
    near_sems = (n_send, n_on, n_recv)
    share(near_all, *near_sems)
    finish()
    parts = total_of(rows, landed).astype(BF)
    parts = dot(parts, spread_back[...])

    for h in range(band):
        k, i = h // 4, (h // 2) % 2
        body = parts[k * width2 : (k + 1) * width2, i * quads : (i + 1) * quads] * pre[h, mid]
        grad_f[h + 1, mid] = body
        grad_own[h] = grad_f[h + 1].astype(BF)
        rims_f[0, pl.ds(h, 1)] = body[:1]
        rims_f[1, pl.ds(h, 1)] = body[width2 - 1 :]
        if h in (0, band - 1):
            rim_rows[h // (band - 1)] = body.astype(BF)
    rims[...] = rims_f[...].astype(BF)
    for way in WAYS:
        start_border(rim_kind, way)

    low = iota((channels, 128), 1) < channels
    halves, ends = [], []
    own_spots = band * span
    windows = jnp.concatenate([patches[i : i + band].reshape(own_spots, 512) for i in range(3)], 1)
    taps = dot(grad_own[...].reshape(own_spots, quads), windows, BY_ROWS)

    def cut(i, p, k):
        return taps[p * channels : (p + 1) * channels, i * 512 + k * 128 : i * 512 + (k + 1) * 128]

    for i in range(3):
        bc = pltpu.roll(cut(i, 0, 0) + cut(i, 2, 1), 64, 1)
        ab = cut(i, 1, 0) + cut(i, 3, 1)
        za = pltpu.roll(cut(i, 0, 2) + cut(i, 2, 0), 64, 1)
        cz = cut(i, 1, 1) + cut(i, 3, 3)
        halves.append(ab + jnp.where(low, za, bc))
        ends.append(cz + bc)
    short = channels // 2
    last = jnp.where(low[:short], ends[2][:short], pltpu.roll(ends[2][short:], 64, 1))
    packed = halves + [jnp.where(low, ends[0], pltpu.roll(ends[1], 64, 1)), last]
    packed = jnp.concatenate(packed, 0)
    owners, piece = mine_blocks.shape[:2]
    for o in range(owners):
        some = packed[o * piece : (o + 1) * piece]
        if some.shape[0] < piece:
            some = jnp.concatenate([some, jnp.zeros((piece - some.shape[0], 128), F32)], 0)
        mine_blocks[o] = some.astype(BF)

    me = row * strips + strip
    my_piece = strip * rows + row
    owning = my_piece < owners

    def target(step):
        z, s = step // strips, step % strips
        return jnp.where(row < rows // 2, rows - 1 - z, z), lax.rem(strip + strips - 1 - s, strips)

    def to_owner(step, arriving=False):
        r, s = target(step)
        other = r * strips + s
        return pltpu.make_async_remote_copy(
            src_ref=mine_blocks.at[my_piece if arriving else s * rows + r],
            dst_ref=one_landed.at[other if arriving else me],
            send_sem=d1_send.at[step],
            recv_sem=d1_recv.at[other if arriving else me],
            device_id=device_at(r, s),
            device_id_type=MESH,
        )

    def from_owner(step, arriving=False):
        r, s = target(step)
        slot = s * rows + r if arriving else my_piece
        return pltpu.make_async_remote_copy(
            src_ref=one_part,
            dst_ref=one_all.at[slot],
            send_sem=d2_send.at[step],
            recv_sem=d2_recv.at[slot],
            device_id=device_at(r, s),
            device_id_type=MESH,
        )

    def each_other(action):
        def one(step):
            r, s = target(step)

            @pl.when(r * strips + s != me)
            def _():
                action(step, s * rows + r < owners)

        if everyone > 16:
            pl.loop(0, everyone)(one)
        else:
            for step in range(everyone):
                one(step)

    def send_out(step, owner):
        @pl.when(owner)
        def _():
            to_owner(step).start()

    def settle_out(step, owner):
        @pl.when(owner)
        def _():
            to_owner(step).wait_send()

        @pl.when(owning)
        def _():
            to_owner(step, True).wait_recv()

    def send_back(step, owner):
        @pl.when(owning)
        def _():
            from_owner(step).start()

    def settle_back(step, owner):
        @pl.when(owning)
        def _():
            from_owner(step).wait_send()

        @pl.when(owner)
        def _():
            from_owner(step, True).wait_recv()

    each_other(send_out)

    @pl.when(owning)
    def _():
        one_landed[me] = mine_blocks[my_piece]

    pass_on(pool_all, *pool_sems)
    pass_on(near_all, *near_sems)
    settle(pool_all, *pool_sems)
    settle(near_all, *near_sems)
    near_map[0] = jnp.zeros(near_map.shape[1:], BF)
    near_map[height2 + 1] = jnp.zeros(near_map.shape[1:], BF)
    at_lane = iota((filters, full2), 1)

    def assemble(u):
        at = u * width2
        if not isinstance(u, int):
            at = pl.multiple_of(at, width2)
        line = [near_all[s, pl.ds(at, width2)].astype(F32) for s in range(strips)]
        line = jnp.concatenate(line, 0).T
        after = jnp.where(at_lane < full2 - 1, pltpu.roll(line, full2 - 1, 1), 0.0)
        before = jnp.where(at_lane > 0, pltpu.roll(line, 1, 1), 0.0)
        for j, value in enumerate((after, line, before)):
            near_map[u + 1, pl.ds(j * filters, filters)] = value.astype(BF)
        for s in range(strips):
            pool_map[u, pl.ds(s * width2, width2)] = pool_all[s, pl.ds(at, width2)]

    chunk = max(1, 1024 // full2)
    steps = height2 // chunk
    if steps == 1:
        for u in range(height2):
            assemble(u)
    else:
        pl.loop(0, height2)(assemble)

    def filter_taps(i, step):
        at = step * chunk
        left = jnp.concatenate([near_map[at + k + 2 - i] for k in range(chunk)], 1)
        right = pool_map[pl.ds(at, chunk)].reshape(chunk * full2, quads)
        return scale_two * dot(left, right).reshape(3, filters, quads)

    def filter_gradient(i):
        g2_out[3 * i : 3 * i + 3] = filter_taps(i, 0)
        if steps > 1:
            @pl.loop(1, steps)
            def _(step):
                g2_out[3 * i : 3 * i + 3] += filter_taps(i, step)

    for way in WAYS:
        end_border(rim_kind, way)
    for h in range(band):
        for side, at in ((0, EDGE - 1), (1, EDGE + width2)):
            grad_f[h + 1, pl.ds(at, 1)] = rim_side[side].astype(F32)[h : h + 1]
    for top, line, h in ((0, 0, band - 1), (1, band + 1, 0)):
        grad_f[line, mid] = rim_row[top].astype(F32)
        for side, at in ((0, EDGE - 1), (1, EDGE + width2)):
            grad_f[line, pl.ds(at, 1)] = rim_corner[2 * top + side].astype(F32)[h : h + 1]
    for line in range(band + 2):
        grad[line] = grad_f[line].astype(BF)
    cells = jnp.concatenate([grad[2 - i : 2 - i + band].reshape(own_spots, quads) for i in range(3)], 1)
    kernel = jnp.concatenate([w1[:, i * 512 : (i + 1) * 512] for i in range(3)], 0)
    total = dot(cells, kernel)
    before = pltpu.roll(total[:, quads : quads + 128], own_spots - 1, 0)
    after = pltpu.roll(total[:, quads + 128 :], 1, 0)
    sides = (total[:, :128] + after, total[:, 128:quads] + before)
    turned = []
    for h in range(band):
        lines_of = []
        for b in range(4):
            value = sides[b // 2][h * span + EDGE : h * span + EDGE + width2]
            lines_of.append(jnp.where(low_half == (b % 2 == 0), value, 0.0).astype(BF))
        turned.append(jnp.concatenate(lines_of, 0))
    turned = dot(jnp.concatenate(turned, 1), pick, BY_ROWS)
    for h in range(band):
        at = 2 * h * channels
        x_wide[pl.ds(h, channels, stride=band), :] = (
            turned[at : at + channels] + turned[at + channels : at + 2 * channels]
        )
    ig_out[...] = x_wide[...].astype(BF)

    each_other(settle_out)

    @pl.when(owning)
    def _():
        if everyone > 16:
            part = lax.fori_loop(
                1, everyone, lambda i, t: t + one_landed[i].astype(F32), one_landed[0].astype(F32)
            )
        else:
            part = total_of(everyone, one_landed)
        one_part[...] = part.astype(BF)
        one_all[my_piece] = part.astype(BF)

    each_other(send_back)
    for i in range(3):
        filter_gradient(i)
    for way in WAYS:
        sent_border(cell_kind, way)
        sent_border(rim_kind, way)
    for side in range(2):
        @pl.when(there((0, (-1, 1)[side])))
        def _(side=side):
            up_border(side).wait_send()
    each_other(settle_back)
    done = scale_one * one_all[...].astype(F32).reshape(owners * piece, 128)
    rolled = pltpu.roll(done, 64, 1)
    for i in range(3):
        for j in range(3):
            at = (i if j < 2 else 3 + i // 2) * channels
            if (i, j) == (2, 2):
                value = jnp.concatenate([done[at : at + short], rolled[at : at + short]], 0)
            else:
                value = (done if (j if j < 2 else i % 2) == 0 else rolled)[at : at + channels]
            g1_out[3 * i + j] = value[:, :channels]


def write_kernel(*refs):
    count = len(refs) // 2
    sources, targets, sem = refs[:count], refs[count:-1], refs[-1]
    copies = [pltpu.make_async_copy(sources[n], targets[n], sem.at[n]) for n in range(count)]
    for copy in copies:
        copy.start()
    for copy in copies:
        copy.wait()


def write_out(*arrays):
    arrays = [pltpu.with_memory_space_constraint(a, pltpu.VMEM) for a in arrays]
    return pl.pallas_call(
        write_kernel,
        out_shape=tuple(jax.ShapeDtypeStruct(a.shape, a.dtype) for a in arrays),
        in_specs=[VMEM] * len(arrays),
        out_specs=(HBM,) * len(arrays),
        scratch_shapes=[pltpu.SemaphoreType.DMA((len(arrays),))],
    )(*arrays)


def local(features_in, filters_one, filters_two, out_grad):
    channels, band, width = features_in.shape
    rows, strips = lax.axis_size("row"), lax.axis_size(STRIP)
    cols, pairs = lax.axis_size("col"), lax.axis_size("pair")
    filters = filters_two.shape[0]
    quads = 4 * channels
    height2 = out_grad.shape[2]
    width2, band2 = width // 4, band // 4
    span = width2 + 2 * EDGE
    full2 = width2 * strips
    spots = band2 * width2
    halves = 9 * channels // 2
    piece = -(-halves // (rows * strips) // 8) * 8
    owners = -(-halves // piece)

    def v(shape, kind=BF):
        return pltpu.VMEM(shape, kind)

    scratch = [
        v((channels * band, width)),
        v((9, channels, channels)),
        v((9, filters, quads)),
        v((width2 * height2, filters)),
        v((channels * band, width), F32),
        v((2 * channels * band, width)),
        v((band * width2, quads)),
        v((2, band * EDGE + 8, quads), F32),
        v((2, band * EDGE, quads)),
        v((2, band * EDGE, quads)),
        v((2, width2, quads)),
        v((4, 16, quads)),
        v((2, 2 * height2, filters)),
        v((band + 3, span, quads), F32),
        v((band + 2, span, 512)),
        v((quads, 3 * 512)),
        v((3 * 512, quads)),
        v((2 * quads, quads)),
        v((quads, 2 * quads)),
        v((3, 3 * quads, filters)),
        v((band + 1, span, quads), F32),
        v((band2 * (width2 + 4) + 8, quads), F32),
        v((band2 * (width2 + 4), quads)),
        v((rows, band2 * (width2 + 4), quads)),
        v((span * height2, filters), F32),
        v((height2 + 1, span, filters), F32),
        v((height2 + 1, span, quads), F32),
        v((height2, span, 3 * quads)),
        v((3, height2 + 2, span, filters)),
        v((height2 + 2, span, filters), F32),
        v((rows, spots, quads)),
        v((rows, spots, quads)),
        v((band + 3, span, quads), F32),
        v((band + 2, span, quads)),
        v((band, span, quads)),
        v((2, 16, quads), F32),
        v((2, 16, quads)),
        v((2, width2, quads)),
        v((2, 16, quads)),
        v((2, width2, quads)),
        v((4, 16, quads)),
        v((strips, height2 * width2, quads)),
        v((strips, height2 * width2, filters)),
        v((height2, full2, quads)),
        v((height2 + 2, 3 * filters, full2)),
        v((owners, piece, 128)),
        v((rows * strips, piece, 128)),
        v((piece, 128)),
        v((owners, piece, 128)),
        pltpu.SemaphoreType.DMA((4,)),
    ]
    scratch += sems(len(WAYS) + 2) + sems(len(WAYS)) + sems(rows) + sems(rows) + sems(rows * strips) + sems(rows * strips)
    for _ in range(2):
        scratch += [
            pltpu.SemaphoreType.DMA((cols,)),
            pltpu.SemaphoreType.DMA((cols * pairs,)),
            pltpu.SemaphoreType.DMA((strips,)),
        ]
    arguments = (
        features_in.reshape(channels * band, width),
        jnp.transpose(filters_one, (1, 2, 0, 3)).reshape(9, channels, channels),
        jnp.transpose(filters_two, (1, 2, 0, 3)).reshape(9, filters, quads),
        jnp.transpose(out_grad, (1, 2, 0)).reshape(width2 * height2, filters),
    )
    arguments = [pltpu.with_memory_space_constraint(a, pltpu.HBM) for a in arguments]
    share = 1 if rows * strips <= 64 else 2
    scale_one = 1.0 / math.sqrt(band * rows * width * strips)
    scale_two = 1.0 / math.sqrt(height2 * full2)
    ig, g1, g2 = pl.pallas_call(
        functools.partial(whole_kernel, rows, strips, band, height2, scale_one, scale_two),
        out_shape=(
            jax.ShapeDtypeStruct((channels * band, width), BF),
            jax.ShapeDtypeStruct((9, channels, channels), F32),
            jax.ShapeDtypeStruct((9, filters, quads), F32),
        ),
        in_specs=[HBM] * 4,
        out_specs=(VMEM,) * 3,
        scratch_shapes=scratch,
        compiler_params=pltpu.CompilerParams(
            collective_id=0, has_side_effects=True, vmem_limit_bytes=share * 28 * 1024 * 1024
        ),
    )(*arguments)
    ig, g1, g2 = write_out(ig, g1, g2)
    grad_one = jnp.transpose(g1.reshape(3, 3, channels, channels), (2, 0, 1, 3))
    grad_two = jnp.transpose(g2.reshape(3, 3, filters, quads), (2, 0, 1, 3))
    return (ig.reshape(channels, band, width), grad_one, grad_two)


def solution(mesh):
    in_specs = (
        P("grp", "row", ("col", "pair")),
        P(),
        P("row", None, None, None),
        P(("grp", "row"), ("col", "pair"), None),
    )
    out_specs = (
        P("grp", "row", ("col", "pair")),
        P("grp", None, None, None),
        P(("grp", "row"), None, None, None),
    )
    return jax.shard_map(local, mesh=mesh, in_specs=in_specs, out_specs=out_specs, check_vma=False)
```

```python
import functools
import math

import jax
import jax.numpy as jnp
from jax import lax
from jax.experimental import pallas as pl
from jax.experimental.pallas import tpu as pltpu
from jax.sharding import PartitionSpec as P

MESH = pl.DeviceIdType.MESH
VMEM = pl.BlockSpec(memory_space=pltpu.VMEM)
HBM = pl.BlockSpec(memory_space=pltpu.HBM)
STRIP = ("col", "pair")
BF = jnp.bfloat16
F32 = jnp.float32

EDGE = 4

DIAGONALS = [(a, b) for a in (-1, 1) for b in (-1, 1)]
WAYS = [(0, -1), (0, 1), (-1, 0), (1, 0)] + DIAGONALS

BY_LANES = (((1,), (1,)), ((), ()))
BY_ROWS = (((0,), (0,)), ((), ()))


def place():
    return lax.axis_index("row"), lax.axis_index(STRIP)


def device_at(row, strip):
    pairs = lax.axis_size("pair")
    return (lax.axis_index("grp"), row, lax.div(strip, pairs), lax.rem(strip, pairs))


def sems(count):
    return [pltpu.SemaphoreType.DMA((count,)), pltpu.SemaphoreType.DMA((count,))]


def around(count, me):
    return lambda step: lax.rem(me + step, count)


def far_first(count, me):
    def peer(step):
        up = step - 1
        up += jnp.where(up >= me, 1, 0)
        down = count - step
        down -= jnp.where(down <= me, 1, 0)
        return jnp.where(me < count // 2, down, up)

    return peer


def near_first(count, me):
    return lambda step: far_first(count, me)(count - step)


def post(count, me, order, device_of, source, landing, send_sem, recv_sem):
    def copy_of(step, slot):
        peer = order(step)
        return pltpu.make_async_remote_copy(
            src_ref=source(peer),
            dst_ref=landing.at[slot(peer)],
            send_sem=send_sem.at[step],
            recv_sem=recv_sem.at[slot(peer)],
            device_id=device_of(peer),
            device_id_type=MESH,
        )

    def start(low=1, high=count):
        @pl.loop(low, high)
        def _(step):
            copy_of(step, lambda peer: me).start()

    def arrive(low=1, high=count):
        @pl.loop(low, high)
        def _(step):
            copy_of(step, lambda peer: peer).wait_recv()

    def sent():
        @pl.loop(1, count)
        def _(step):
            copy_of(step, lambda peer: me).wait_send()

    return start, arrive, sent


def iota(shape, dim):
    return lax.broadcasted_iota(jnp.int32, shape, dim)


def dot(a, b, numbers=(((1,), (0,)), ((), ()))):
    return lax.dot_general(a, b, numbers, preferred_element_type=F32)


def slope(values):
    s = 1.0 / (1.0 + jnp.exp(-values))
    return s * (1.0 + values * (1.0 - s))


def total_of(count, landing):
    value = landing[0].astype(F32)
    for i in range(1, count):
        value += landing[i].astype(F32)
    return value


def whole_kernel(
    rows, strips, band, height2, scale_one, scale_two,
    x_any, f1_any, f2_any, up_any,
    ig_out, g1_out, g2_out,
    x_in, f1, f2, up_in, x_wide, x_turned, own, edges_f, edges, from_side, from_row, from_corner, from_up,
    tile, patches, inner, w1, w1_down, spread_one, spread_back, f2_down, pre, block_f, block, gathered, up_wide, up, pool_f, pool3, near3, sum_two,
    blocks, landed, grad_f, grad, grad_own, rims_f, rims, rim_rows, rim_side, rim_row, rim_corner, pool_all, near_all, pool_map, near_map,
    mine_blocks, one_landed, one_part, one_all,
    load_sem, a_send, a_recv, e_send, e_recv, b_send, b_recv, c_send, c_recv,
    d1_send, d1_recv, d2_send, d2_recv,
    p_send, p_on, p_recv, n_send, n_on, n_recv,
):
    row, strip = place()
    cols, pairs = lax.axis_size("col"), lax.axis_size("pair")
    col, pair = lax.axis_index("col"), lax.axis_index("pair")
    channels = f1.shape[1]
    filters = f2.shape[1]
    quads = 4 * channels
    width = x_in.shape[1]
    width2 = width // 4
    band2 = band // 4
    span = width2 + 2 * EDGE
    full2 = width2 * strips
    mid = pl.ds(EDGE, width2)
    reach = width2 + 4

    def row_device(i):
        return device_at(i, strip)

    def strip_device(i):
        return device_at(row, i)

    def there(way):
        a, b = row + way[0], strip + way[1]
        return (a >= 0) & (a < rows) & (b >= 0) & (b < strips)

    barrier = pltpu.get_barrier_semaphore()
    everyone = rows * strips
    for step in range(1, rows):
        pl.semaphore_signal(barrier, inc=1, device_id=row_device(lax.rem(row + step, rows)), device_id_type=MESH)
    for step in range(1, strips):
        pl.semaphore_signal(
            barrier, inc=1, device_id=strip_device(lax.rem(strip + step, strips)), device_id_type=MESH
        )
    for way in DIAGONALS:
        @pl.when(there(way))
        def _(way=way):
            pl.semaphore_signal(
                barrier, inc=1, device_id=device_at(row + way[0], strip + way[1]), device_id_type=MESH
            )
    loads = [
        pltpu.make_async_copy(source, target, load_sem.at[n])
        for n, (source, target) in enumerate([(x_any, x_in), (up_any, up_in), (f1_any, f1), (f2_any, f2)])
    ]
    for load in loads:
        load.start()

    shape = (width, width)
    pick = (iota(shape, 1) == 4 * (iota(shape, 0) % width2) + iota(shape, 0) // width2).astype(BF)
    low_half = iota((width2, 128), 1) < channels
    shape = (quads, quads)
    for i in range(2):
        target = 4 * (iota(shape, 0) % channels) + 2 * i + iota(shape, 0) // (2 * channels)
        spread_one[pl.ds(i * quads, quads)] = (iota(shape, 1) == target).astype(BF)
        target = 4 * (iota(shape, 1) % channels) + 2 * i + iota(shape, 1) // (2 * channels)
        spread_back[:, pl.ds(i * quads, quads)] = (iota(shape, 0) == target).astype(BF)
    grad_f[...] = jnp.zeros(grad_f.shape, F32)
    rims_f[...] = jnp.zeros(rims_f.shape, F32)
    sum_two[...] = jnp.zeros(sum_two.shape, F32)
    for line in (0, band + 1):
        patches[line] = jnp.zeros(patches.shape[1:], BF)
    for u in range(height2):
        pool_f[u, pl.ds(0, 2)] = jnp.zeros((2, quads), F32)
        pool_f[u, pl.ds(2 + reach, 2)] = jnp.zeros((2, quads), F32)
    for j in range(3):
        near3[j, 0] = jnp.zeros(near3.shape[2:], BF)
        near3[j, height2 + 1] = jnp.zeros(near3.shape[2:], BF)
    loads[0].wait()
    x_wide[...] = x_in[...].astype(F32)
    for h in range(band):
        line = x_wide[pl.ds(h, channels, stride=band), :].astype(BF)
        x_turned[pl.ds(2 * h * channels, channels), :] = line
        x_turned[pl.ds((2 * h + 1) * channels, channels), :] = line
    turned = dot(pick, x_turned[...], BY_LANES)
    for h in range(band):
        lanes = slice(h * 128, (h + 1) * 128)
        for half in range(2):
            even = turned[2 * half * width2 : (2 * half + 1) * width2, lanes]
            odd = turned[(2 * half + 1) * width2 : (2 * half + 2) * width2, lanes]
            value = jnp.where(low_half, even, odd)
            tile[h + 1, mid, pl.ds(half * 128, 128)] = value
            own[pl.ds(h * width2, width2), pl.ds(half * 128, 128)] = value.astype(BF)
    for h in range(band):
        edges_f[0, pl.ds(h * EDGE, EDGE)] = tile[h + 1, pl.ds(EDGE, EDGE)]
        edges_f[1, pl.ds(h * EDGE, EDGE)] = tile[h + 1, pl.ds(width2, EDGE)]
    edges[...] = edges_f[:, : band * EDGE].astype(BF)

    diagonals = (jnp.where(row > 0, 1, 0) + jnp.where(row < rows - 1, 1, 0)) * (
        jnp.where(strip > 0, 1, 0) + jnp.where(strip < strips - 1, 1, 0)
    )
    pl.semaphore_wait(barrier, rows - 1 + strips - 1 + diagonals)
    edge_rows = band * EDGE
    up_edge = 2 * height2

    def corner_of(way):
        return (way[1] + 1) // 2, (way[0] + 1) // 2

    def border(kind, way, arriving=False):
        (source_of, slot_of, send_sem, recv_sem), back = kind, (-way[0], -way[1])
        land = way if arriving else back
        return pltpu.make_async_remote_copy(
            src_ref=source_of(way),
            dst_ref=slot_of(land),
            send_sem=send_sem.at[WAYS.index(way)],
            recv_sem=recv_sem.at[WAYS.index(land)],
            device_id=device_at(row + way[0], strip + way[1]),
            device_id_type=MESH,
        )

    def start_border(kind, way):
        @pl.when(there(way))
        def _():
            border(kind, way).start()

    def clear_border(kind, way):
        @pl.when(jnp.logical_not(there(way)))
        def _():
            slot = kind[1](way)
            slot[...] = jnp.zeros(slot.shape, slot.dtype)

    def end_border(kind, way):
        @pl.when(there(way))
        def _():
            border(kind, way, True).wait_recv()

    def sent_border(kind, way):
        @pl.when(there(way))
        def _():
            border(kind, way).wait_send()

    def slots(side_slots, row_slots, corner_slots):
        def slot_of(way):
            side, top = corner_of(way)
            if way[0] == 0:
                return side_slots.at[side]
            if way[1] == 0:
                return row_slots.at[top]
            return corner_slots.at[2 * top + side]

        return slot_of

    def cell_source(way):
        side = corner_of(way)[0]
        if way[0] == 0:
            return edges.at[side]
        if way[1] == 0:
            return own.at[pl.ds(0 if way[0] < 0 else (band - 1) * width2, width2)]
        return edges.at[side, pl.ds(0 if way[0] < 0 else edge_rows - 16, 16)]

    def rim_source(way):
        side, top = corner_of(way)
        return rim_rows.at[top] if way[1] == 0 else rims.at[side]

    cell_kind = (cell_source, slots(from_side, from_row, from_corner), a_send, a_recv)
    rim_kind = (rim_source, slots(rim_side, rim_row, rim_corner), e_send, e_recv)

    def up_border(side, arriving=False):
        land = side if arriving else 1 - side
        return pltpu.make_async_remote_copy(
            src_ref=up_in.at[pl.ds(0 if side == 0 else up_in.shape[0] - up_edge, up_edge)],
            dst_ref=from_up.at[land],
            send_sem=a_send.at[len(WAYS) + side],
            recv_sem=a_recv.at[len(WAYS) + land],
            device_id=device_at(row, strip + (-1, 1)[side]),
            device_id_type=MESH,
        )

    for way in WAYS:
        start_border(cell_kind, way)
    for way in WAYS:
        clear_border(cell_kind, way)
        clear_border(rim_kind, way)
    loads[1].wait()
    for side in range(2):
        @pl.when(there((0, (-1, 1)[side])))
        def _(side=side):
            up_border(side).start()

        @pl.when(jnp.logical_not(there((0, (-1, 1)[side]))))
        def _(side=side):
            from_up[side] = jnp.zeros(from_up.shape[1:], BF)

    loads[2].wait()
    zero = jnp.zeros((channels, channels), F32)
    nothing = jnp.zeros((channels, 128), BF)
    for i in range(3):
        a, b, c = [f1[3 * i + j].astype(F32) for j in range(3)]
        bc, ab, za, cz = [
            jnp.concatenate(two, 1).astype(BF) for two in ((b, c), (a, b), (zero, a), (c, zero))
        ]
        table = (
            (bc, nothing, za, nothing),
            (ab, cz, nothing, nothing),
            (za, bc, nothing, nothing),
            (nothing, ab, nothing, cz),
        )
        for p in range(4):
            for k in range(4):
                w1[pl.ds(p * channels, channels), pl.ds(i * 512 + k * 128, 128)] = table[p][k]
    for k in range(12):
        w1_down[pl.ds(k * 128, 128)] = w1[:, pl.ds(k * 128, 128)].astype(F32).T.astype(BF)

    def widen(line):
        here = tile[line]
        patches[line, :, pl.ds(0, quads)] = here.astype(BF)
        patches[line, :, pl.ds(quads, 128)] = pltpu.roll(here[:, quads - 128 :], 1, 0).astype(BF)
        patches[line, :, pl.ds(quads + 128, 128)] = pltpu.roll(here[:, :128], span - 1, 0).astype(BF)

    def silu(values):
        return values / (1.0 + jnp.exp(-values))

    def pool(h):
        total = (silu(pre[h]) + silu(pre[h + 1])) * 0.25
        upper = total.astype(BF)
        both = jnp.concatenate([upper, (total - upper.astype(F32)).astype(BF)], 0)
        both = dot(both, spread_one[pl.ds((h // 2) % 2 * quads, quads)])
        return both[:span] + both[span:]

    side_at = [pl.ds(0, EDGE), pl.ds(EDGE + width2, EDGE)]
    for way in WAYS[:2]:
        end_border(cell_kind, way)
    for side in range(2):
        edge = from_side[side].astype(F32)
        for h in range(band):
            tile[h + 1, side_at[side]] = edge[h * EDGE : (h + 1) * EDGE]
    for line in range(1, band + 1):
        widen(line)
    windows = jnp.concatenate([patches[i : i + band].reshape(band * span, 512) for i in range(3)], 1)
    pre[0:band] = dot(windows, w1_down[...]).reshape(band, span, quads)
    halves = {h: pool(h) for h in range(2, band - 2, 2)}

    for way in WAYS[2:]:
        end_border(cell_kind, way)
    for top in range(2):
        line = 0 if top == 0 else band + 1
        tile[line, mid] = from_row[top].astype(F32)
        for side in range(2):
            corner = from_corner[2 * top + side].astype(F32)
            tile[line, side_at[side]] = corner[16 - EDGE :] if top == 0 else corner[:EDGE]
        widen(line)
    pre[0] += dot(patches[0], w1_down[pl.ds(0, 512)])
    pre[band - 1] += dot(patches[band + 1], w1_down[pl.ds(1024, 512)])
    for h in (0, band - 2):
        halves[h] = pool(h)
    pooled = jnp.concatenate([halves[4 * u] + halves[4 * u + 2] for u in range(band2)], 0)
    at_col = strip * width2 - EDGE + iota((band2 * span, quads), 0) % span
    pooled = jnp.where((at_col >= 0) & (at_col < full2), pooled, 0.0)
    for u in range(band2):
        block_f[pl.ds(u * reach, reach)] = pooled[u * span + 2 : u * span + 2 + reach]
    pooled = block_f[: band2 * reach].astype(BF)
    block[...] = pooled
    start, arrive, b_sent = post(
        rows, row, near_first(rows, row), row_device, lambda peer: block, gathered, b_send, b_recv
    )
    start()
    gathered[row] = pooled

    for h in range(band):
        pre[h] = slope(pre[h]) * 0.25
    for line in range(band + 2):
        inner[line, :, pl.ds(0, quads)] = tile[line, mid].astype(BF)
        inner[line, :, pl.ds(quads, 128)] = tile[line, pl.ds(EDGE - 1, width2), pl.ds(quads - 128, 128)].astype(BF)
        inner[line, :, pl.ds(quads + 128, 128)] = tile[line, pl.ds(EDGE + 1, width2), pl.ds(0, 128)].astype(BF)
    for side in range(2):
        @pl.when(there((0, (-1, 1)[side])))
        def _(side=side):
            up_border(side, True).wait_recv()
    up_wide[pl.ds(0, up_edge)] = from_up[0].astype(F32)
    up_wide[pl.ds(up_edge, width2 * height2)] = up_in[...].astype(F32)
    up_wide[pl.ds(up_edge + width2 * height2, up_edge)] = from_up[1].astype(F32)
    for u in range(height2):
        up[u, pl.ds(0, 2)] = jnp.zeros((2, filters), F32)
        up[u, pl.ds(2, width2 + 4)] = up_wide[pl.ds(u, width2 + 4, stride=height2), :]
        up[u, pl.ds(width2 + 6, 2)] = jnp.zeros((2, filters), F32)
    loads[3].wait()
    for t in range(9):
        f2_down[t // 3, pl.ds(t % 3 * quads, quads)] = f2[t].astype(F32).T.astype(BF)

    half, bands = height2 // 2, rows // 2
    near_band = jnp.where(row < bands, 0, bands)
    far_band = bands - near_band

    def forward(band_at):
        at = band_at * band2
        for d in range(half):
            k = d % band2
            pool_f[at + d, pl.ds(2, reach)] = gathered[band_at + d // band2].astype(F32)[
                k * reach : (k + 1) * reach
            ]
            wide = pool_f[at + d]
            pool3[at + d, :, pl.ds(0, quads)] = pltpu.roll(wide, 1, 0).astype(BF)
            pool3[at + d, :, pl.ds(quads, quads)] = wide.astype(BF)
            pool3[at + d, :, pl.ds(2 * quads, quads)] = pltpu.roll(wide, span - 1, 0).astype(BF)
            spot = pl.multiple_of((at + d) * width2, width2)
            pool_all[strip, pl.ds(spot, width2)] = wide[EDGE : EDGE + width2].astype(BF)
        windows = pool3[pl.ds(at, half)].reshape(half * span, 3 * quads)
        if filters % 128 == 0:
            sums = dot(windows, jnp.concatenate([f2_down[i] for i in range(3)], 1))
            sums = [sums[:, i * filters : (i + 1) * filters] for i in range(3)]
        else:
            sums = [dot(windows, f2_down[i]) for i in range(3)]
        for i in range(3):
            sum_two[pl.ds(at + 2 - i, half)] += sums[i].reshape(half, span, filters)

    arrive(1, rows - bands)
    forward(near_band)
    arrive(rows - bands, rows)
    def across(source, table, send_sem, recv_sem, step):
        return pltpu.make_async_remote_copy(
            src_ref=source,
            dst_ref=table.at[strip],
            send_sem=send_sem.at[step],
            recv_sem=recv_sem.at[strip],
            device_id=device_at(row, lax.rem(col + step, cols) * pairs + pair),
            device_id_type=MESH,
        )

    def onward(table, send_sem, recv_sem, column, step):
        slot = column * pairs + pair
        return pltpu.make_async_remote_copy(
            src_ref=table.at[slot],
            dst_ref=table.at[slot],
            send_sem=send_sem.at[column * pairs + step],
            recv_sem=recv_sem.at[slot],
            device_id=device_at(row, col * pairs + lax.rem(pair + step, pairs)),
            device_id_type=MESH,
        )

    def arrival(table, send_sem, recv_sem, slot):
        return pltpu.make_async_remote_copy(
            src_ref=table.at[slot],
            dst_ref=table.at[slot],
            send_sem=send_sem.at[0],
            recv_sem=recv_sem.at[slot],
            device_id=device_at(row, lax.rem(col + 1, cols) * pairs + pair),
            device_id_type=MESH,
        )

    def share(table, send_sem, on_sem, recv_sem):
        for step in range(1, cols):
            across(table.at[strip], table, send_sem, recv_sem, step).start()
        for step in range(1, pairs):
            onward(table, on_sem, recv_sem, col, step).start()

    def pass_on(table, send_sem, on_sem, recv_sem):
        for step in range(1, cols):
            column = lax.rem(col + step, cols)
            arrival(table, send_sem, recv_sem, column * pairs + pair).wait_recv()
            for other in range(1, pairs):
                onward(table, on_sem, recv_sem, column, other).start()

    def settle(table, send_sem, on_sem, recv_sem):
        for step in range(1, cols):
            across(table.at[strip], table, send_sem, recv_sem, step).wait_send()
        for step in range(cols):
            column = lax.rem(col + step, cols)
            for other in range(1, pairs):
                onward(table, on_sem, recv_sem, column, other).wait_send()
                slot = column * pairs + lax.rem(pair + other, pairs)
                arrival(table, send_sem, recv_sem, slot).wait_recv()

    forward(far_band)
    pool_sems = (p_send, p_on, p_recv)
    share(pool_all, *pool_sems)
    spots = height2 * span
    pre_two = sum_two[1 : height2 + 1].reshape(spots, filters)
    near = up[0:height2].reshape(spots, filters) * slope(pre_two)
    near3[0, 1 : height2 + 1] = pltpu.roll(near, spots - 1, 0).astype(BF).reshape(height2, span, filters)
    near3[1, 1 : height2 + 1] = near.astype(BF).reshape(height2, span, filters)
    near3[2, 1 : height2 + 1] = pltpu.roll(near, 1, 0).astype(BF).reshape(height2, span, filters)

    def backward(band_at):
        at = band_at * band2
        windows = [
            near3[j, pl.ds(at + 2 - i, half)].reshape(half * span, filters) for i in range(3) for j in range(3)
        ]
        if filters % 128 == 0:
            total = dot(jnp.concatenate(windows, 1), f2[...].reshape(9 * filters, quads))
        else:
            total = jnp.zeros((half * span, quads), F32)
            for t in range(9):
                total += dot(windows[t], f2[t])
        for d in range(half):
            blocks[band_at + d // band2, pl.ds(d % band2 * width2, width2)] = total[
                d * span + EDGE : d * span + EDGE + width2
            ].astype(BF)

    start, arrive, c_sent = post(
        rows, row, far_first(rows, row), row_device, lambda peer: blocks.at[peer], landed, c_send, c_recv
    )
    backward(far_band)
    start(1, bands + 1)
    backward(near_band)
    start(bands + 1, rows)
    landed[row] = blocks[row]
    for u in range(height2):
        near_all[strip, pl.ds(u * width2, width2)] = near[
            u * span + EDGE : u * span + EDGE + width2
        ].astype(BF)
    near_sems = (n_send, n_on, n_recv)
    share(near_all, *near_sems)
    arrive()
    parts = total_of(rows, landed).astype(BF)
    parts = dot(parts, spread_back[...])

    for h in range(band):
        k, i = h // 4, (h // 2) % 2
        body = parts[k * width2 : (k + 1) * width2, i * quads : (i + 1) * quads] * pre[h, mid]
        grad_f[h + 1, mid] = body
        grad_own[pl.ds(h * width2, width2)] = body.astype(BF)
        rims_f[0, pl.ds(h, 1)] = body[:1]
        rims_f[1, pl.ds(h, 1)] = body[width2 - 1 :]
        if h in (0, band - 1):
            rim_rows[h // (band - 1)] = body.astype(BF)

    low = iota((channels, 128), 1) < channels
    halves, ends = [], []
    own_spots = band * span
    windows = jnp.concatenate([inner[i : i + band].reshape(band * width2, 512) for i in range(3)], 1)
    taps = dot(grad_own[...], windows, BY_ROWS)

    def cut(i, p, k):
        return taps[p * channels : (p + 1) * channels, i * 512 + k * 128 : i * 512 + (k + 1) * 128]

    for i in range(3):
        bc = pltpu.roll(cut(i, 0, 0) + cut(i, 2, 1), 64, 1)
        ab = cut(i, 1, 0) + cut(i, 3, 1)
        za = pltpu.roll(cut(i, 0, 2) + cut(i, 2, 0), 64, 1)
        cz = cut(i, 1, 1) + cut(i, 3, 3)
        halves.append(ab + jnp.where(low, za, bc))
        ends.append(cz + bc)
    short = channels // 2
    last = jnp.where(low[:short], ends[2][:short], pltpu.roll(ends[2][short:], 64, 1))
    packed = halves + [jnp.where(low, ends[0], pltpu.roll(ends[1], 64, 1)), last]
    packed = jnp.concatenate(packed, 0)
    owners, piece = mine_blocks.shape[:2]
    for o in range(owners):
        some = packed[o * piece : (o + 1) * piece]
        if some.shape[0] < piece:
            some = jnp.concatenate([some, jnp.zeros((piece - some.shape[0], 128), F32)], 0)
        mine_blocks[o] = some.astype(BF)

    me = row * strips + strip
    low_row = rows // 2 - 1

    def piece_of(r, s):
        return 2 * s + r - low_row

    def owns(r, s):
        return (r >= low_row) & (r <= low_row + 1) & (piece_of(r, s) < owners)

    my_piece = piece_of(row, strip)
    owning = owns(row, strip)

    def target(step):
        z, s = step // strips, step % strips
        return jnp.where(row < rows // 2, rows - 1 - z, z), lax.rem(strip + strips - 1 - s, strips)

    def to_owner(step, arriving=False):
        r, s = target(step)
        other = r * strips + s
        return pltpu.make_async_remote_copy(
            src_ref=mine_blocks.at[my_piece if arriving else piece_of(r, s)],
            dst_ref=one_landed.at[other if arriving else me],
            send_sem=d1_send.at[step],
            recv_sem=d1_recv.at[other if arriving else me],
            device_id=device_at(r, s),
            device_id_type=MESH,
        )

    def from_owner(step, arriving=False):
        r, s = target(step)
        slot = piece_of(r, s) if arriving else my_piece
        return pltpu.make_async_remote_copy(
            src_ref=one_part,
            dst_ref=one_all.at[slot],
            send_sem=d2_send.at[step],
            recv_sem=d2_recv.at[slot],
            device_id=device_at(r, s),
            device_id_type=MESH,
        )

    def each_other(action):
        def one(step):
            r, s = target(step)

            @pl.when(r * strips + s != me)
            def _():
                action(step, owns(r, s))

        if everyone > 16:
            pl.loop(0, everyone)(one)
        else:
            for step in range(everyone):
                one(step)

    def send_out(step, owner):
        @pl.when(owner)
        def _():
            to_owner(step).start()

    def settle_out(step, owner):
        @pl.when(owner)
        def _():
            to_owner(step).wait_send()

        @pl.when(owning)
        def _():
            to_owner(step, True).wait_recv()

    def send_back(step, owner):
        @pl.when(owning)
        def _():
            from_owner(step).start()

    def settle_back(step, owner):
        @pl.when(owning)
        def _():
            from_owner(step).wait_send()

        @pl.when(owner)
        def _():
            from_owner(step, True).wait_recv()

    each_other(send_out)

    @pl.when(owning)
    def _():
        one_landed[me] = mine_blocks[my_piece]

    rims[...] = rims_f[...].astype(BF)
    for way in WAYS:
        start_border(rim_kind, way)

    pass_on(pool_all, *pool_sems)
    pass_on(near_all, *near_sems)
    each_other(settle_out)

    @pl.when(owning)
    def _():
        if everyone > 16:
            part = lax.fori_loop(
                1, everyone, lambda i, t: t + one_landed[i].astype(F32), one_landed[0].astype(F32)
            )
        else:
            part = total_of(everyone, one_landed)
        one_part[...] = part.astype(BF)
        one_all[my_piece] = part.astype(BF)

    each_other(send_back)

    settle(pool_all, *pool_sems)
    settle(near_all, *near_sems)
    near_map[0] = jnp.zeros(near_map.shape[1:], BF)
    near_map[height2 + 1] = jnp.zeros(near_map.shape[1:], BF)
    at_lane = iota((filters, full2), 1)

    def assemble(u):
        at = u * width2
        if not isinstance(u, int):
            at = pl.multiple_of(at, width2)
        line = [near_all[s, pl.ds(at, width2)].astype(F32) for s in range(strips)]
        line = jnp.concatenate(line, 0).T
        after = jnp.where(at_lane < full2 - 1, pltpu.roll(line, full2 - 1, 1), 0.0)
        before = jnp.where(at_lane > 0, pltpu.roll(line, 1, 1), 0.0)
        for j, value in enumerate((after, line, before)):
            near_map[u + 1, pl.ds(j * filters, filters)] = value.astype(BF)
        for s in range(strips):
            pool_map[u, pl.ds(s * width2, width2)] = pool_all[s, pl.ds(at, width2)]

    chunk = max(1, 1024 // full2)
    steps = height2 // chunk
    if steps == 1:
        for u in range(height2):
            assemble(u)
    else:
        pl.loop(0, height2)(assemble)

    def filter_taps(i, step):
        at = step * chunk
        left = jnp.concatenate([near_map[at + k + 2 - i] for k in range(chunk)], 1)
        right = pool_map[pl.ds(at, chunk)].reshape(chunk * full2, quads)
        return scale_two * dot(left, right).reshape(3, filters, quads)

    def filter_gradient(i):
        g2_out[3 * i : 3 * i + 3] = filter_taps(i, 0)
        if steps > 1:
            @pl.loop(1, steps)
            def _(step):
                g2_out[3 * i : 3 * i + 3] += filter_taps(i, step)

    for i in range(3):
        filter_gradient(i)

    for way in WAYS:
        end_border(rim_kind, way)
    for h in range(band):
        for side, at in ((0, EDGE - 1), (1, EDGE + width2)):
            grad_f[h + 1, pl.ds(at, 1)] = rim_side[side].astype(F32)[h : h + 1]
    for top, line, h in ((0, 0, band - 1), (1, band + 1, 0)):
        grad_f[line, mid] = rim_row[top].astype(F32)
        for side, at in ((0, EDGE - 1), (1, EDGE + width2)):
            grad_f[line, pl.ds(at, 1)] = rim_corner[2 * top + side].astype(F32)[h : h + 1]
    for line in range(band + 2):
        grad[line] = grad_f[line].astype(BF)
    cells = jnp.concatenate([grad[2 - i : 2 - i + band].reshape(own_spots, quads) for i in range(3)], 1)
    kernel = jnp.concatenate([w1[:, i * 512 : (i + 1) * 512] for i in range(3)], 0)
    total = dot(cells, kernel)
    before = pltpu.roll(total[:, quads : quads + 128], own_spots - 1, 0)
    after = pltpu.roll(total[:, quads + 128 :], 1, 0)
    sides = (total[:, :128] + after, total[:, 128:quads] + before)
    turned = []
    for h in range(band):
        lines_of = []
        for b in range(4):
            value = sides[b // 2][h * span + EDGE : h * span + EDGE + width2]
            lines_of.append(jnp.where(low_half == (b % 2 == 0), value, 0.0).astype(BF))
        turned.append(jnp.concatenate(lines_of, 0))
    turned = dot(jnp.concatenate(turned, 1), pick, BY_ROWS)
    for h in range(band):
        at = 2 * h * channels
        x_wide[pl.ds(h, channels, stride=band), :] = (
            turned[at : at + channels] + turned[at + channels : at + 2 * channels]
        )
    ig_out[...] = x_wide[...].astype(BF)

    b_sent()
    c_sent()
    for way in WAYS:
        sent_border(cell_kind, way)
        sent_border(rim_kind, way)
    for side in range(2):
        @pl.when(there((0, (-1, 1)[side])))
        def _(side=side):
            up_border(side).wait_send()
    each_other(settle_back)
    done = scale_one * one_all[...].astype(F32).reshape(owners * piece, 128)
    rolled = pltpu.roll(done, 64, 1)
    for i in range(3):
        for j in range(3):
            at = (i if j < 2 else 3 + i // 2) * channels
            if (i, j) == (2, 2):
                value = jnp.concatenate([done[at : at + short], rolled[at : at + short]], 0)
            else:
                value = (done if (j if j < 2 else i % 2) == 0 else rolled)[at : at + channels]
            g1_out[3 * i + j] = value[:, :channels]


def write_kernel(*refs):
    count = len(refs) // 2
    sources, targets, sem = refs[:count], refs[count:-1], refs[-1]
    copies = [pltpu.make_async_copy(sources[n], targets[n], sem.at[n]) for n in range(count)]
    for copy in copies:
        copy.start()
    for copy in copies:
        copy.wait()


def write_out(*arrays):
    arrays = [pltpu.with_memory_space_constraint(a, pltpu.VMEM) for a in arrays]
    return pl.pallas_call(
        write_kernel,
        out_shape=tuple(jax.ShapeDtypeStruct(a.shape, a.dtype) for a in arrays),
        in_specs=[VMEM] * len(arrays),
        out_specs=(HBM,) * len(arrays),
        scratch_shapes=[pltpu.SemaphoreType.DMA((len(arrays),))],
    )(*arrays)


def local(features_in, filters_one, filters_two, out_grad):
    channels, band, width = features_in.shape
    rows, strips = lax.axis_size("row"), lax.axis_size(STRIP)
    cols, pairs = lax.axis_size("col"), lax.axis_size("pair")
    filters = filters_two.shape[0]
    quads = 4 * channels
    height2 = out_grad.shape[2]
    width2, band2 = width // 4, band // 4
    span = width2 + 2 * EDGE
    full2 = width2 * strips
    spots = band2 * width2
    halves = 9 * channels // 2
    piece = -(-halves // (2 * strips) // 8) * 8
    owners = -(-halves // piece)

    def v(shape, kind=BF):
        return pltpu.VMEM(shape, kind)

    scratch = [
        v((channels * band, width)),
        v((9, channels, channels)),
        v((9, filters, quads)),
        v((width2 * height2, filters)),
        v((channels * band, width), F32),
        v((2 * channels * band, width)),
        v((band * width2, quads)),
        v((2, band * EDGE + 8, quads), F32),
        v((2, band * EDGE, quads)),
        v((2, band * EDGE, quads)),
        v((2, width2, quads)),
        v((4, 16, quads)),
        v((2, 2 * height2, filters)),
        v((band + 3, span, quads), F32),
        v((band + 2, span, 512)),
        v((band + 2, width2, 512)),
        v((quads, 3 * 512)),
        v((3 * 512, quads)),
        v((2 * quads, quads)),
        v((quads, 2 * quads)),
        v((3, 3 * quads, filters)),
        v((band + 1, span, quads), F32),
        v((band2 * (width2 + 4) + 8, quads), F32),
        v((band2 * (width2 + 4), quads)),
        v((rows, band2 * (width2 + 4), quads)),
        v((span * height2, filters), F32),
        v((height2 + 1, span, filters), F32),
        v((height2 + 1, span, quads), F32),
        v((height2, span, 3 * quads)),
        v((3, height2 + 2, span, filters)),
        v((height2 + 2, span, filters), F32),
        v((rows, spots, quads)),
        v((rows, spots, quads)),
        v((band + 3, span, quads), F32),
        v((band + 2, span, quads)),
        v((band * width2, quads)),
        v((2, 16, quads), F32),
        v((2, 16, quads)),
        v((2, width2, quads)),
        v((2, 16, quads)),
        v((2, width2, quads)),
        v((4, 16, quads)),
        v((strips, height2 * width2, quads)),
        v((strips, height2 * width2, filters)),
        v((height2, full2, quads)),
        v((height2 + 2, 3 * filters, full2)),
        v((owners, piece, 128)),
        v((rows * strips, piece, 128)),
        v((piece, 128)),
        v((owners, piece, 128)),
        pltpu.SemaphoreType.DMA((4,)),
    ]
    scratch += sems(len(WAYS) + 2) + sems(len(WAYS)) + sems(rows) + sems(rows) + sems(rows * strips) + sems(rows * strips)
    for _ in range(2):
        scratch += [
            pltpu.SemaphoreType.DMA((cols,)),
            pltpu.SemaphoreType.DMA((cols * pairs,)),
            pltpu.SemaphoreType.DMA((strips,)),
        ]
    arguments = (
        features_in.reshape(channels * band, width),
        jnp.transpose(filters_one, (1, 2, 0, 3)).reshape(9, channels, channels),
        jnp.transpose(filters_two, (1, 2, 0, 3)).reshape(9, filters, quads),
        jnp.transpose(out_grad, (1, 2, 0)).reshape(width2 * height2, filters),
    )
    arguments = [pltpu.with_memory_space_constraint(a, pltpu.HBM) for a in arguments]
    share = 1 if rows * strips <= 64 else 2
    scale_one = 1.0 / math.sqrt(band * rows * width * strips)
    scale_two = 1.0 / math.sqrt(height2 * full2)
    ig, g1, g2 = pl.pallas_call(
        functools.partial(whole_kernel, rows, strips, band, height2, scale_one, scale_two),
        out_shape=(
            jax.ShapeDtypeStruct((channels * band, width), BF),
            jax.ShapeDtypeStruct((9, channels, channels), F32),
            jax.ShapeDtypeStruct((9, filters, quads), F32),
        ),
        in_specs=[HBM] * 4,
        out_specs=(VMEM,) * 3,
        scratch_shapes=scratch,
        compiler_params=pltpu.CompilerParams(
            collective_id=0, has_side_effects=True, vmem_limit_bytes=share * 28 * 1024 * 1024
        ),
    )(*arguments)
    ig, g1, g2 = write_out(ig, g1, g2)
    grad_one = jnp.transpose(g1.reshape(3, 3, channels, channels), (2, 0, 1, 3))
    grad_two = jnp.transpose(g2.reshape(3, 3, filters, quads), (2, 0, 1, 3))
    return (ig.reshape(channels, band, width), grad_one, grad_two)


def solution(mesh):
    in_specs = (
        P("grp", "row", ("col", "pair")),
        P(),
        P("row", None, None, None),
        P(("grp", "row"), ("col", "pair"), None),
    )
    out_specs = (
        P("grp", "row", ("col", "pair")),
        P("grp", None, None, None),
        P(("grp", "row"), None, None, None),
    )
    return jax.shard_map(local, mesh=mesh, in_specs=in_specs, out_specs=out_specs, check_vma=False)
```

```python
import functools
import math

import jax
import jax.numpy as jnp
from jax import lax
from jax.experimental import pallas as pl
from jax.experimental.pallas import tpu as pltpu
from jax.sharding import PartitionSpec as P

MESH = pl.DeviceIdType.MESH
VMEM = pl.BlockSpec(memory_space=pltpu.VMEM)
HBM = pl.BlockSpec(memory_space=pltpu.HBM)
STRIP = ("col", "pair")
BF = jnp.bfloat16
F32 = jnp.float32

EDGE = 4

DIAGONALS = [(a, b) for a in (-1, 1) for b in (-1, 1)]
WAYS = [(0, -1), (0, 1), (-1, 0), (1, 0)] + DIAGONALS

BY_LANES = (((1,), (1,)), ((), ()))
BY_ROWS = (((0,), (0,)), ((), ()))


def place():
    return lax.axis_index("row"), lax.axis_index(STRIP)


def device_at(row, strip):
    pairs = lax.axis_size("pair")
    return (lax.axis_index("grp"), row, lax.div(strip, pairs), lax.rem(strip, pairs))


def sems(count):
    return [pltpu.SemaphoreType.DMA((count,)), pltpu.SemaphoreType.DMA((count,))]


def around(count, me):
    return lambda step: lax.rem(me + step, count)


def far_first(count, me):
    def peer(step):
        up = step - 1
        up += jnp.where(up >= me, 1, 0)
        down = count - step
        down -= jnp.where(down <= me, 1, 0)
        return jnp.where(me < count // 2, down, up)

    return peer


def near_first(count, me):
    return lambda step: far_first(count, me)(count - step)


def post(count, me, order, device_of, source, landing, send_sem, recv_sem):
    def copy_of(step, slot):
        peer = order(step)
        return pltpu.make_async_remote_copy(
            src_ref=source(peer),
            dst_ref=landing.at[slot(peer)],
            send_sem=send_sem.at[step],
            recv_sem=recv_sem.at[slot(peer)],
            device_id=device_of(peer),
            device_id_type=MESH,
        )

    def start(low=1, high=count):
        @pl.loop(low, high)
        def _(step):
            copy_of(step, lambda peer: me).start()

    def arrive(low=1, high=count):
        @pl.loop(low, high)
        def _(step):
            copy_of(step, lambda peer: peer).wait_recv()

    def sent():
        @pl.loop(1, count)
        def _(step):
            copy_of(step, lambda peer: me).wait_send()

    return start, arrive, sent


def iota(shape, dim):
    return lax.broadcasted_iota(jnp.int32, shape, dim)


def dot(a, b, numbers=(((1,), (0,)), ((), ()))):
    return lax.dot_general(a, b, numbers, preferred_element_type=F32)


def slope(values):
    s = 1.0 / (1.0 + jnp.exp(-values))
    return s * (1.0 + values * (1.0 - s))


def total_of(count, landing):
    value = landing[0].astype(F32)
    for i in range(1, count):
        value += landing[i].astype(F32)
    return value


def whole_kernel(
    rows, strips, band, height2, scale_one, scale_two,
    x_any, f1_any, f2_any, up_any,
    ig_out, g1_out, g2_out,
    x_in, f1, f2, up_in, x_wide, x_turned, own, edges_f, edges, from_side, from_row, from_corner, from_up,
    tile, patches, inner, w1, w1_down, reorder, f2_down, pre, block_f, block, gathered, up_wide, up, pool_f, pool3, near3, sum_two,
    blocks, landed, grad_f, grad, grad_own, rims_f, rims, rim_rows, rim_side, rim_row, rim_corner, pool_all, near_all, pool_map, near_map,
    mine_blocks, one_landed, one_part, one_all,
    load_sem, a_send, a_recv, e_send, e_recv, b_send, b_recv, c_send, c_recv,
    d1_send, d1_recv, d2_send, d2_recv,
    p_send, p_on, p_recv, n_send, n_on, n_recv,
):
    row, strip = place()
    cols, pairs = lax.axis_size("col"), lax.axis_size("pair")
    col, pair = lax.axis_index("col"), lax.axis_index("pair")
    channels = f1.shape[1]
    filters = f2.shape[1]
    quads = 4 * channels
    width = x_in.shape[1]
    width2 = width // 4
    band2 = band // 4
    span = width2 + 2 * EDGE
    full2 = width2 * strips
    mid = pl.ds(EDGE, width2)
    reach = width2 + 4

    def row_device(i):
        return device_at(i, strip)

    def strip_device(i):
        return device_at(row, i)

    def there(way):
        a, b = row + way[0], strip + way[1]
        return (a >= 0) & (a < rows) & (b >= 0) & (b < strips)

    barrier = pltpu.get_barrier_semaphore()
    everyone = rows * strips
    for step in range(1, rows):
        pl.semaphore_signal(barrier, inc=1, device_id=row_device(lax.rem(row + step, rows)), device_id_type=MESH)
    for step in range(1, strips):
        pl.semaphore_signal(
            barrier, inc=1, device_id=strip_device(lax.rem(strip + step, strips)), device_id_type=MESH
        )
    for way in DIAGONALS:
        @pl.when(there(way))
        def _(way=way):
            pl.semaphore_signal(
                barrier, inc=1, device_id=device_at(row + way[0], strip + way[1]), device_id_type=MESH
            )
    loads = [
        pltpu.make_async_copy(source, target, load_sem.at[n])
        for n, (source, target) in enumerate([(x_any, x_in), (up_any, up_in), (f1_any, f1), (f2_any, f2)])
    ]
    for load in loads:
        load.start()

    shape = (width, width)
    pick = (iota(shape, 1) == 4 * (iota(shape, 0) % width2) + iota(shape, 0) // width2).astype(BF)
    low_half = iota((width2, 128), 1) < channels
    shape = (quads, quads)
    for k in range(2):
        inside, outside = iota(shape, 1 - k), iota(shape, k)
        home = 4 * (inside % channels) + 2 * (inside // (2 * channels)) + inside // channels % 2
        reorder[k] = (outside == home).astype(BF)
    grad_f[...] = jnp.zeros(grad_f.shape, F32)
    rims_f[...] = jnp.zeros(rims_f.shape, F32)
    sum_two[...] = jnp.zeros(sum_two.shape, F32)
    for line in (0, band + 1):
        patches[line] = jnp.zeros(patches.shape[1:], BF)
    for u in range(height2):
        pool_f[u, pl.ds(0, 2)] = jnp.zeros((2, quads), F32)
        pool_f[u, pl.ds(2 + reach, 2)] = jnp.zeros((2, quads), F32)
    for j in range(3):
        near3[j, 0] = jnp.zeros(near3.shape[2:], BF)
        near3[j, height2 + 1] = jnp.zeros(near3.shape[2:], BF)
    loads[0].wait()
    x_wide[...] = x_in[...].astype(F32)
    for h in range(band):
        line = x_wide[pl.ds(h, channels, stride=band), :].astype(BF)
        x_turned[pl.ds(2 * h * channels, channels), :] = line
        x_turned[pl.ds((2 * h + 1) * channels, channels), :] = line
    turned = dot(pick, x_turned[...], BY_LANES)
    for h in range(band):
        lanes = slice(h * 128, (h + 1) * 128)
        for half in range(2):
            even = turned[2 * half * width2 : (2 * half + 1) * width2, lanes]
            odd = turned[(2 * half + 1) * width2 : (2 * half + 2) * width2, lanes]
            value = jnp.where(low_half, even, odd)
            tile[h + 1, mid, pl.ds(half * 128, 128)] = value
            own[pl.ds(h * width2, width2), pl.ds(half * 128, 128)] = value.astype(BF)
    for h in range(band):
        edges_f[0, pl.ds(h * EDGE, EDGE)] = tile[h + 1, pl.ds(EDGE, EDGE)]
        edges_f[1, pl.ds(h * EDGE, EDGE)] = tile[h + 1, pl.ds(width2, EDGE)]
    edges[...] = edges_f[:, : band * EDGE].astype(BF)

    diagonals = (jnp.where(row > 0, 1, 0) + jnp.where(row < rows - 1, 1, 0)) * (
        jnp.where(strip > 0, 1, 0) + jnp.where(strip < strips - 1, 1, 0)
    )
    pl.semaphore_wait(barrier, rows - 1 + strips - 1 + diagonals)
    edge_rows = band * EDGE
    up_edge = 2 * height2

    def corner_of(way):
        return (way[1] + 1) // 2, (way[0] + 1) // 2

    def border(kind, way, arriving=False):
        (source_of, slot_of, send_sem, recv_sem), back = kind, (-way[0], -way[1])
        land = way if arriving else back
        return pltpu.make_async_remote_copy(
            src_ref=source_of(way),
            dst_ref=slot_of(land),
            send_sem=send_sem.at[WAYS.index(way)],
            recv_sem=recv_sem.at[WAYS.index(land)],
            device_id=device_at(row + way[0], strip + way[1]),
            device_id_type=MESH,
        )

    def start_border(kind, way):
        @pl.when(there(way))
        def _():
            border(kind, way).start()

    def clear_border(kind, way):
        @pl.when(jnp.logical_not(there(way)))
        def _():
            slot = kind[1](way)
            slot[...] = jnp.zeros(slot.shape, slot.dtype)

    def end_border(kind, way):
        @pl.when(there(way))
        def _():
            border(kind, way, True).wait_recv()

    def sent_border(kind, way):
        @pl.when(there(way))
        def _():
            border(kind, way).wait_send()

    def slots(side_slots, row_slots, corner_slots):
        def slot_of(way):
            side, top = corner_of(way)
            if way[0] == 0:
                return side_slots.at[side]
            if way[1] == 0:
                return row_slots.at[top]
            return corner_slots.at[2 * top + side]

        return slot_of

    def cell_source(way):
        side = corner_of(way)[0]
        if way[0] == 0:
            return edges.at[side]
        if way[1] == 0:
            return own.at[pl.ds(0 if way[0] < 0 else (band - 1) * width2, width2)]
        return edges.at[side, pl.ds(0 if way[0] < 0 else edge_rows - 16, 16)]

    def rim_source(way):
        side, top = corner_of(way)
        return rim_rows.at[top] if way[1] == 0 else rims.at[side]

    cell_kind = (cell_source, slots(from_side, from_row, from_corner), a_send, a_recv)
    rim_kind = (rim_source, slots(rim_side, rim_row, rim_corner), e_send, e_recv)

    def up_border(side, arriving=False):
        land = side if arriving else 1 - side
        return pltpu.make_async_remote_copy(
            src_ref=up_in.at[pl.ds(0 if side == 0 else up_in.shape[0] - up_edge, up_edge)],
            dst_ref=from_up.at[land],
            send_sem=a_send.at[len(WAYS) + side],
            recv_sem=a_recv.at[len(WAYS) + land],
            device_id=device_at(row, strip + (-1, 1)[side]),
            device_id_type=MESH,
        )

    for way in WAYS[2:] + WAYS[:2]:
        start_border(cell_kind, way)
    for way in WAYS:
        clear_border(cell_kind, way)
        clear_border(rim_kind, way)
    loads[1].wait()
    for side in range(2):
        @pl.when(there((0, (-1, 1)[side])))
        def _(side=side):
            up_border(side).start()

        @pl.when(jnp.logical_not(there((0, (-1, 1)[side]))))
        def _(side=side):
            from_up[side] = jnp.zeros(from_up.shape[1:], BF)

    loads[2].wait()
    zero = jnp.zeros((channels, channels), F32)
    nothing = jnp.zeros((channels, 128), BF)
    for i in range(3):
        a, b, c = [f1[3 * i + j].astype(F32) for j in range(3)]
        bc, ab, za, cz = [
            jnp.concatenate(two, 1).astype(BF) for two in ((b, c), (a, b), (zero, a), (c, zero))
        ]
        table = (
            (bc, nothing, za, nothing),
            (ab, cz, nothing, nothing),
            (za, bc, nothing, nothing),
            (nothing, ab, nothing, cz),
        )
        for p in range(4):
            for k in range(4):
                w1[pl.ds(p * channels, channels), pl.ds(i * 512 + k * 128, 128)] = table[p][k]
    for k in range(12):
        w1_down[pl.ds(k * 128, 128)] = w1[:, pl.ds(k * 128, 128)].astype(F32).T.astype(BF)

    def widen(line):
        here = tile[line]
        patches[line, :, pl.ds(0, quads)] = here.astype(BF)
        patches[line, :, pl.ds(quads, 128)] = pltpu.roll(here[:, quads - 128 :], 1, 0).astype(BF)
        patches[line, :, pl.ds(quads + 128, 128)] = pltpu.roll(here[:, :128], span - 1, 0).astype(BF)

    def silu(values):
        return values / (1.0 + jnp.exp(-values))

    def pool(h):
        total = (silu(pre[h]) + silu(pre[h + 1])) * 0.25
        left, right = total[:, :128], total[:, 128:]
        left += pltpu.roll(left, 64, 1)
        right += pltpu.roll(right, 64, 1)
        return jnp.where(iota((span, 128), 1) < channels, left, right)

    side_at = [pl.ds(0, EDGE), pl.ds(EDGE + width2, EDGE)]
    for way in WAYS[:2]:
        end_border(cell_kind, way)
    for side in range(2):
        edge = from_side[side].astype(F32)
        for h in range(band):
            tile[h + 1, side_at[side]] = edge[h * EDGE : (h + 1) * EDGE]
    for line in range(1, band + 1):
        widen(line)
    windows = jnp.concatenate([patches[i : i + band].reshape(band * span, 512) for i in range(3)], 1)
    pre[0:band] = dot(windows, w1_down[...]).reshape(band, span, quads)
    halves = {h: pool(h) for h in range(2, band - 2, 2)}

    for way in WAYS[2:]:
        end_border(cell_kind, way)
    for top in range(2):
        line = 0 if top == 0 else band + 1
        tile[line, mid] = from_row[top].astype(F32)
        for side in range(2):
            corner = from_corner[2 * top + side].astype(F32)
            tile[line, side_at[side]] = corner[16 - EDGE :] if top == 0 else corner[:EDGE]
        widen(line)
    pre[0] += dot(patches[0], w1_down[pl.ds(0, 512)])
    pre[band - 1] += dot(patches[band + 1], w1_down[pl.ds(1024, 512)])
    for h in (0, band - 2):
        halves[h] = pool(h)
    pooled = [jnp.concatenate([halves[4 * u], halves[4 * u + 2]], 1) for u in range(band2)]
    pooled = jnp.concatenate(pooled, 0)
    at_col = strip * width2 - EDGE + iota((band2 * span, quads), 0) % span
    pooled = jnp.where((at_col >= 0) & (at_col < full2), pooled, 0.0)
    for u in range(band2):
        block_f[pl.ds(u * reach, reach)] = pooled[u * span + 2 : u * span + 2 + reach]
    pooled = block_f[: band2 * reach].astype(BF)
    block[...] = pooled
    start, arrive, b_sent = post(
        rows, row, near_first(rows, row), row_device, lambda peer: block, gathered, b_send, b_recv
    )
    start()
    gathered[row] = pooled

    for h in range(band):
        pre[h] = slope(pre[h]) * 0.25
    for line in range(band + 2):
        inner[line, :, pl.ds(0, quads)] = tile[line, mid].astype(BF)
        inner[line, :, pl.ds(quads, 128)] = tile[line, pl.ds(EDGE - 1, width2), pl.ds(quads - 128, 128)].astype(BF)
        inner[line, :, pl.ds(quads + 128, 128)] = tile[line, pl.ds(EDGE + 1, width2), pl.ds(0, 128)].astype(BF)
    for side in range(2):
        @pl.when(there((0, (-1, 1)[side])))
        def _(side=side):
            up_border(side, True).wait_recv()
    up_wide[pl.ds(0, up_edge)] = from_up[0].astype(F32)
    up_wide[pl.ds(up_edge, width2 * height2)] = up_in[...].astype(F32)
    up_wide[pl.ds(up_edge + width2 * height2, up_edge)] = from_up[1].astype(F32)
    for u in range(height2):
        up[u, pl.ds(0, 2)] = jnp.zeros((2, filters), F32)
        up[u, pl.ds(2, width2 + 4)] = up_wide[pl.ds(u, width2 + 4, stride=height2), :]
        up[u, pl.ds(width2 + 6, 2)] = jnp.zeros((2, filters), F32)
    loads[3].wait()
    f2[...] = dot(f2[...].reshape(9 * filters, quads), reorder[0]).astype(BF).reshape(9, filters, quads)
    for t in range(9):
        f2_down[t // 3, pl.ds(t % 3 * quads, quads)] = f2[t].astype(F32).T.astype(BF)

    half, bands = height2 // 2, rows // 2
    near_band = jnp.where(row < bands, 0, bands)
    far_band = bands - near_band

    def forward(band_at):
        at = band_at * band2
        for d in range(half):
            k = d % band2
            pool_f[at + d, pl.ds(2, reach)] = gathered[band_at + d // band2].astype(F32)[
                k * reach : (k + 1) * reach
            ]
            wide = pool_f[at + d]
            pool3[at + d, :, pl.ds(0, quads)] = pltpu.roll(wide, 1, 0).astype(BF)
            pool3[at + d, :, pl.ds(quads, quads)] = wide.astype(BF)
            pool3[at + d, :, pl.ds(2 * quads, quads)] = pltpu.roll(wide, span - 1, 0).astype(BF)
            spot = pl.multiple_of((at + d) * width2, width2)
            pool_all[strip, pl.ds(spot, width2)] = wide[EDGE : EDGE + width2].astype(BF)
        windows = pool3[pl.ds(at, half)].reshape(half * span, 3 * quads)
        if filters % 128 == 0:
            sums = dot(windows, jnp.concatenate([f2_down[i] for i in range(3)], 1))
            sums = [sums[:, i * filters : (i + 1) * filters] for i in range(3)]
        else:
            sums = [dot(windows, f2_down[i]) for i in range(3)]
        for i in range(3):
            sum_two[pl.ds(at + 2 - i, half)] += sums[i].reshape(half, span, filters)

    arrive(1, rows - bands)
    forward(near_band)
    arrive(rows - bands, rows)
    def across(source, table, send_sem, recv_sem, step):
        return pltpu.make_async_remote_copy(
            src_ref=source,
            dst_ref=table.at[strip],
            send_sem=send_sem.at[step],
            recv_sem=recv_sem.at[strip],
            device_id=device_at(row, lax.rem(col + step, cols) * pairs + pair),
            device_id_type=MESH,
        )

    def onward(table, send_sem, recv_sem, column, step):
        slot = column * pairs + pair
        return pltpu.make_async_remote_copy(
            src_ref=table.at[slot],
            dst_ref=table.at[slot],
            send_sem=send_sem.at[column * pairs + step],
            recv_sem=recv_sem.at[slot],
            device_id=device_at(row, col * pairs + lax.rem(pair + step, pairs)),
            device_id_type=MESH,
        )

    def arrival(table, send_sem, recv_sem, slot):
        return pltpu.make_async_remote_copy(
            src_ref=table.at[slot],
            dst_ref=table.at[slot],
            send_sem=send_sem.at[0],
            recv_sem=recv_sem.at[slot],
            device_id=device_at(row, lax.rem(col + 1, cols) * pairs + pair),
            device_id_type=MESH,
        )

    def share(table, send_sem, on_sem, recv_sem):
        for step in range(1, cols):
            across(table.at[strip], table, send_sem, recv_sem, step).start()
        for step in range(1, pairs):
            onward(table, on_sem, recv_sem, col, step).start()

    def pass_on(table, send_sem, on_sem, recv_sem):
        for step in range(1, cols):
            column = lax.rem(col + step, cols)
            arrival(table, send_sem, recv_sem, column * pairs + pair).wait_recv()
            for other in range(1, pairs):
                onward(table, on_sem, recv_sem, column, other).start()

    def settle(table, send_sem, on_sem, recv_sem):
        for step in range(1, cols):
            across(table.at[strip], table, send_sem, recv_sem, step).wait_send()
        for step in range(cols):
            column = lax.rem(col + step, cols)
            for other in range(1, pairs):
                onward(table, on_sem, recv_sem, column, other).wait_send()
                slot = column * pairs + lax.rem(pair + other, pairs)
                arrival(table, send_sem, recv_sem, slot).wait_recv()

    forward(far_band)
    pool_sems = (p_send, p_on, p_recv)
    share(pool_all, *pool_sems)
    spots = height2 * span
    pre_two = sum_two[1 : height2 + 1].reshape(spots, filters)
    near = up[0:height2].reshape(spots, filters) * slope(pre_two)
    near3[0, 1 : height2 + 1] = pltpu.roll(near, spots - 1, 0).astype(BF).reshape(height2, span, filters)
    near3[1, 1 : height2 + 1] = near.astype(BF).reshape(height2, span, filters)
    near3[2, 1 : height2 + 1] = pltpu.roll(near, 1, 0).astype(BF).reshape(height2, span, filters)

    def backward(band_at):
        at = band_at * band2
        windows = [
            near3[j, pl.ds(at + 2 - i, half)].reshape(half * span, filters) for i in range(3) for j in range(3)
        ]
        if filters % 128 == 0:
            total = dot(jnp.concatenate(windows, 1), f2[...].reshape(9 * filters, quads))
        else:
            total = jnp.zeros((half * span, quads), F32)
            for t in range(9):
                total += dot(windows[t], f2[t])
        for d in range(half):
            blocks[band_at + d // band2, pl.ds(d % band2 * width2, width2)] = total[
                d * span + EDGE : d * span + EDGE + width2
            ].astype(BF)

    start, arrive, c_sent = post(
        rows, row, far_first(rows, row), row_device, lambda peer: blocks.at[peer], landed, c_send, c_recv
    )
    backward(far_band)
    start(1, bands + 1)
    backward(near_band)
    start(bands + 1, rows)
    landed[row] = blocks[row]
    for u in range(height2):
        near_all[strip, pl.ds(u * width2, width2)] = near[
            u * span + EDGE : u * span + EDGE + width2
        ].astype(BF)
    near_sems = (n_send, n_on, n_recv)
    share(near_all, *near_sems)
    arrive()
    parts = total_of(rows, landed)
    wide = {}
    for k in range(band2):
        for i in range(2):
            some = parts[k * width2 : (k + 1) * width2, i * 128 : (i + 1) * 128]
            other = pltpu.roll(some, 64, 1)
            wide[k, i] = jnp.concatenate(
                [jnp.where(low_half, some, other), jnp.where(low_half, other, some)], 1
            )

    for h in range(band):
        k, i = h // 4, (h // 2) % 2
        body = wide[k, i] * pre[h, mid]
        grad_f[h + 1, mid] = body
        grad_own[pl.ds(h * width2, width2)] = body.astype(BF)
        rims_f[0, pl.ds(h, 1)] = body[:1]
        rims_f[1, pl.ds(h, 1)] = body[width2 - 1 :]
        if h in (0, band - 1):
            rim_rows[h // (band - 1)] = body.astype(BF)

    low = iota((channels, 128), 1) < channels
    halves, ends = [], []
    own_spots = band * span
    windows = jnp.concatenate([inner[i : i + band].reshape(band * width2, 512) for i in range(3)], 1)
    taps = dot(grad_own[...], windows, BY_ROWS)

    def cut(i, p, k):
        return taps[p * channels : (p + 1) * channels, i * 512 + k * 128 : i * 512 + (k + 1) * 128]

    for i in range(3):
        bc = pltpu.roll(cut(i, 0, 0) + cut(i, 2, 1), 64, 1)
        ab = cut(i, 1, 0) + cut(i, 3, 1)
        za = pltpu.roll(cut(i, 0, 2) + cut(i, 2, 0), 64, 1)
        cz = cut(i, 1, 1) + cut(i, 3, 3)
        halves.append(ab + jnp.where(low, za, bc))
        ends.append(cz + bc)
    short = channels // 2
    last = jnp.where(low[:short], ends[2][:short], pltpu.roll(ends[2][short:], 64, 1))
    packed = halves + [jnp.where(low, ends[0], pltpu.roll(ends[1], 64, 1)), last]
    packed = jnp.concatenate(packed, 0)
    owners, piece = mine_blocks.shape[:2]
    for o in range(owners):
        some = packed[o * piece : (o + 1) * piece]
        if some.shape[0] < piece:
            some = jnp.concatenate([some, jnp.zeros((piece - some.shape[0], 128), F32)], 0)
        mine_blocks[o] = some.astype(BF)

    me = row * strips + strip
    low_row = rows // 2 - 1

    def piece_of(r, s):
        return 2 * s + r - low_row

    def owns(r, s):
        return (r >= low_row) & (r <= low_row + 1) & (piece_of(r, s) < owners)

    my_piece = piece_of(row, strip)
    owning = owns(row, strip)

    def target(step):
        z, s = step % rows, step // rows
        return jnp.where(row < rows // 2, rows - 1 - z, z), lax.rem(col + cols - 1 - s // pairs, cols) * pairs + lax.rem(
            pair + pairs - 1 - s % pairs, pairs
        )

    def to_owner(step, arriving=False):
        r, s = target(step)
        other = r * strips + s
        return pltpu.make_async_remote_copy(
            src_ref=mine_blocks.at[my_piece if arriving else piece_of(r, s)],
            dst_ref=one_landed.at[other if arriving else me],
            send_sem=d1_send.at[step],
            recv_sem=d1_recv.at[other if arriving else me],
            device_id=device_at(r, s),
            device_id_type=MESH,
        )

    def from_owner(step, arriving=False):
        r, s = target(step)
        slot = piece_of(r, s) if arriving else my_piece
        return pltpu.make_async_remote_copy(
            src_ref=one_part,
            dst_ref=one_all.at[slot],
            send_sem=d2_send.at[step],
            recv_sem=d2_recv.at[slot],
            device_id=device_at(r, s),
            device_id_type=MESH,
        )

    def each_other(action):
        def one(step):
            r, s = target(step)

            @pl.when(r * strips + s != me)
            def _():
                action(step, owns(r, s))

        if everyone > 16:
            pl.loop(0, everyone)(one)
        else:
            for step in range(everyone):
                one(step)

    def send_out(step, owner):
        @pl.when(owner)
        def _():
            to_owner(step).start()

    def settle_out(step, owner):
        @pl.when(owner)
        def _():
            to_owner(step).wait_send()

        @pl.when(owning)
        def _():
            to_owner(step, True).wait_recv()

    def send_back(step, owner):
        @pl.when(owning)
        def _():
            from_owner(step).start()

    def settle_back(step, owner):
        @pl.when(owning)
        def _():
            from_owner(step).wait_send()

        @pl.when(owner)
        def _():
            from_owner(step, True).wait_recv()

    each_other(send_out)

    @pl.when(owning)
    def _():
        one_landed[me] = mine_blocks[my_piece]

    rims[...] = rims_f[...].astype(BF)
    for way in WAYS:
        start_border(rim_kind, way)

    pass_on(pool_all, *pool_sems)
    pass_on(near_all, *near_sems)
    each_other(settle_out)

    @pl.when(owning)
    def _():
        if everyone > 16:
            part = lax.fori_loop(
                1, everyone, lambda i, t: t + one_landed[i].astype(F32), one_landed[0].astype(F32)
            )
        else:
            part = total_of(everyone, one_landed)
        one_part[...] = part.astype(BF)
        one_all[my_piece] = part.astype(BF)

    each_other(send_back)

    settle(pool_all, *pool_sems)
    settle(near_all, *near_sems)
    near_map[0] = jnp.zeros(near_map.shape[1:], BF)
    near_map[height2 + 1] = jnp.zeros(near_map.shape[1:], BF)
    at_lane = iota((filters, full2), 1)

    def assemble(u):
        at = u * width2
        if not isinstance(u, int):
            at = pl.multiple_of(at, width2)
        line = [near_all[s, pl.ds(at, width2)].astype(F32) for s in range(strips)]
        line = jnp.concatenate(line, 0).T
        after = jnp.where(at_lane < full2 - 1, pltpu.roll(line, full2 - 1, 1), 0.0)
        before = jnp.where(at_lane > 0, pltpu.roll(line, 1, 1), 0.0)
        for j, value in enumerate((after, line, before)):
            near_map[u + 1, pl.ds(j * filters, filters)] = value.astype(BF)
        line = jnp.concatenate([pool_all[s, pl.ds(at, width2)] for s in range(strips)], 0)
        pool_map[u] = dot(line, reorder[1]).astype(BF)

    chunk = max(1, 1024 // full2)
    steps = height2 // chunk
    if steps == 1:
        for u in range(height2):
            assemble(u)
    else:
        pl.loop(0, height2)(assemble)

    def filter_taps(i, step):
        at = step * chunk
        left = jnp.concatenate([near_map[at + k + 2 - i] for k in range(chunk)], 1)
        right = pool_map[pl.ds(at, chunk)].reshape(chunk * full2, quads)
        return scale_two * dot(left, right).reshape(3, filters, quads)

    def filter_gradient(i):
        g2_out[3 * i : 3 * i + 3] = filter_taps(i, 0)
        if steps > 1:
            @pl.loop(1, steps)
            def _(step):
                g2_out[3 * i : 3 * i + 3] += filter_taps(i, step)

    for i in range(3):
        filter_gradient(i)

    for way in WAYS:
        end_border(rim_kind, way)
    for h in range(band):
        for side, at in ((0, EDGE - 1), (1, EDGE + width2)):
            grad_f[h + 1, pl.ds(at, 1)] = rim_side[side].astype(F32)[h : h + 1]
    for top, line, h in ((0, 0, band - 1), (1, band + 1, 0)):
        grad_f[line, mid] = rim_row[top].astype(F32)
        for side, at in ((0, EDGE - 1), (1, EDGE + width2)):
            grad_f[line, pl.ds(at, 1)] = rim_corner[2 * top + side].astype(F32)[h : h + 1]
    for line in range(band + 2):
        grad[line] = grad_f[line].astype(BF)
    cells = jnp.concatenate([grad[2 - i : 2 - i + band].reshape(own_spots, quads) for i in range(3)], 1)
    kernel = jnp.concatenate([w1[:, i * 512 : (i + 1) * 512] for i in range(3)], 0)
    total = dot(cells, kernel)
    before = pltpu.roll(total[:, quads : quads + 128], own_spots - 1, 0)
    after = pltpu.roll(total[:, quads + 128 :], 1, 0)
    sides = (total[:, :128] + after, total[:, 128:quads] + before)
    turned = []
    for h in range(band):
        lines_of = []
        for b in range(4):
            value = sides[b // 2][h * span + EDGE : h * span + EDGE + width2]
            lines_of.append(jnp.where(low_half == (b % 2 == 0), value, 0.0).astype(BF))
        turned.append(jnp.concatenate(lines_of, 0))
    turned = dot(jnp.concatenate(turned, 1), pick, BY_ROWS)
    for h in range(band):
        at = 2 * h * channels
        x_wide[pl.ds(h, channels, stride=band), :] = (
            turned[at : at + channels] + turned[at + channels : at + 2 * channels]
        )
    ig_out[...] = x_wide[...].astype(BF)

    b_sent()
    c_sent()
    for way in WAYS:
        sent_border(cell_kind, way)
        sent_border(rim_kind, way)
    for side in range(2):
        @pl.when(there((0, (-1, 1)[side])))
        def _(side=side):
            up_border(side).wait_send()
    each_other(settle_back)
    done = scale_one * one_all[...].astype(F32).reshape(owners * piece, 128)
    rolled = pltpu.roll(done, 64, 1)
    for i in range(3):
        for j in range(3):
            at = (i if j < 2 else 3 + i // 2) * channels
            if (i, j) == (2, 2):
                value = jnp.concatenate([done[at : at + short], rolled[at : at + short]], 0)
            else:
                value = (done if (j if j < 2 else i % 2) == 0 else rolled)[at : at + channels]
            g1_out[3 * i + j] = value[:, :channels]


def write_kernel(*refs):
    count = len(refs) // 2
    sources, targets, sem = refs[:count], refs[count:-1], refs[-1]
    copies = [pltpu.make_async_copy(sources[n], targets[n], sem.at[n]) for n in range(count)]
    for copy in copies:
        copy.start()
    for copy in copies:
        copy.wait()


def write_out(*arrays):
    arrays = [pltpu.with_memory_space_constraint(a, pltpu.VMEM) for a in arrays]
    return pl.pallas_call(
        write_kernel,
        out_shape=tuple(jax.ShapeDtypeStruct(a.shape, a.dtype) for a in arrays),
        in_specs=[VMEM] * len(arrays),
        out_specs=(HBM,) * len(arrays),
        scratch_shapes=[pltpu.SemaphoreType.DMA((len(arrays),))],
    )(*arrays)


def local(features_in, filters_one, filters_two, out_grad):
    channels, band, width = features_in.shape
    rows, strips = lax.axis_size("row"), lax.axis_size(STRIP)
    cols, pairs = lax.axis_size("col"), lax.axis_size("pair")
    filters = filters_two.shape[0]
    quads = 4 * channels
    height2 = out_grad.shape[2]
    width2, band2 = width // 4, band // 4
    span = width2 + 2 * EDGE
    full2 = width2 * strips
    spots = band2 * width2
    halves = 9 * channels // 2
    piece = -(-halves // (2 * strips) // 8) * 8
    owners = -(-halves // piece)

    def v(shape, kind=BF):
        return pltpu.VMEM(shape, kind)

    scratch = [
        v((channels * band, width)),
        v((9, channels, channels)),
        v((9, filters, quads)),
        v((width2 * height2, filters)),
        v((channels * band, width), F32),
        v((2 * channels * band, width)),
        v((band * width2, quads)),
        v((2, band * EDGE + 8, quads), F32),
        v((2, band * EDGE, quads)),
        v((2, band * EDGE, quads)),
        v((2, width2, quads)),
        v((4, 16, quads)),
        v((2, 2 * height2, filters)),
        v((band + 3, span, quads), F32),
        v((band + 2, span, 512)),
        v((band + 2, width2, 512)),
        v((quads, 3 * 512)),
        v((3 * 512, quads)),
        v((2, quads, quads)),
        v((3, 3 * quads, filters)),
        v((band + 1, span, quads), F32),
        v((band2 * (width2 + 4) + 8, quads), F32),
        v((band2 * (width2 + 4), quads)),
        v((rows, band2 * (width2 + 4), quads)),
        v((span * height2, filters), F32),
        v((height2 + 1, span, filters), F32),
        v((height2 + 1, span, quads), F32),
        v((height2, span, 3 * quads)),
        v((3, height2 + 2, span, filters)),
        v((height2 + 2, span, filters), F32),
        v((rows, spots, quads)),
        v((rows, spots, quads)),
        v((band + 3, span, quads), F32),
        v((band + 2, span, quads)),
        v((band * width2, quads)),
        v((2, 16, quads), F32),
        v((2, 16, quads)),
        v((2, width2, quads)),
        v((2, 16, quads)),
        v((2, width2, quads)),
        v((4, 16, quads)),
        v((strips, height2 * width2, quads)),
        v((strips, height2 * width2, filters)),
        v((height2, full2, quads)),
        v((height2 + 2, 3 * filters, full2)),
        v((owners, piece, 128)),
        v((rows * strips, piece, 128)),
        v((piece, 128)),
        v((owners, piece, 128)),
        pltpu.SemaphoreType.DMA((4,)),
    ]
    scratch += sems(len(WAYS) + 2) + sems(len(WAYS)) + sems(rows) + sems(rows) + sems(rows * strips) + sems(rows * strips)
    for _ in range(2):
        scratch += [
            pltpu.SemaphoreType.DMA((cols,)),
            pltpu.SemaphoreType.DMA((cols * pairs,)),
            pltpu.SemaphoreType.DMA((strips,)),
        ]
    arguments = (
        features_in.reshape(channels * band, width),
        jnp.transpose(filters_one, (1, 2, 0, 3)).reshape(9, channels, channels),
        jnp.transpose(filters_two, (1, 2, 0, 3)).reshape(9, filters, quads),
        jnp.transpose(out_grad, (1, 2, 0)).reshape(width2 * height2, filters),
    )
    arguments = [pltpu.with_memory_space_constraint(a, pltpu.HBM) for a in arguments]
    share = 1 if rows * strips <= 64 else 2
    scale_one = 1.0 / math.sqrt(band * rows * width * strips)
    scale_two = 1.0 / math.sqrt(height2 * full2)
    ig, g1, g2 = pl.pallas_call(
        functools.partial(whole_kernel, rows, strips, band, height2, scale_one, scale_two),
        out_shape=(
            jax.ShapeDtypeStruct((channels * band, width), BF),
            jax.ShapeDtypeStruct((9, channels, channels), F32),
            jax.ShapeDtypeStruct((9, filters, quads), F32),
        ),
        in_specs=[HBM] * 4,
        out_specs=(VMEM,) * 3,
        scratch_shapes=scratch,
        compiler_params=pltpu.CompilerParams(
            collective_id=0, has_side_effects=True, vmem_limit_bytes=share * 28 * 1024 * 1024
        ),
    )(*arguments)
    ig, g1, g2 = write_out(ig, g1, g2)
    grad_one = jnp.transpose(g1.reshape(3, 3, channels, channels), (2, 0, 1, 3))
    grad_two = jnp.transpose(g2.reshape(3, 3, filters, quads), (2, 0, 1, 3))
    return (ig.reshape(channels, band, width), grad_one, grad_two)


def solution(mesh):
    in_specs = (
        P("grp", "row", ("col", "pair")),
        P(),
        P("row", None, None, None),
        P(("grp", "row"), ("col", "pair"), None),
    )
    out_specs = (
        P("grp", "row", ("col", "pair")),
        P("grp", None, None, None),
        P(("grp", "row"), None, None, None),
    )
    return jax.shard_map(local, mesh=mesh, in_specs=in_specs, out_specs=out_specs, check_vma=False)
```

```python
import functools
import math

import jax
import jax.numpy as jnp
from jax import lax
from jax.experimental import pallas as pl
from jax.experimental.pallas import tpu as pltpu
from jax.sharding import PartitionSpec as P

MESH = pl.DeviceIdType.MESH
VMEM = pl.BlockSpec(memory_space=pltpu.VMEM)
HBM = pl.BlockSpec(memory_space=pltpu.HBM)
STRIP = ("col", "pair")
BF = jnp.bfloat16
F32 = jnp.float32

EDGE = 4

DIAGONALS = [(a, b) for a in (-1, 1) for b in (-1, 1)]
WAYS = [(0, -1), (0, 1), (-1, 0), (1, 0)] + DIAGONALS

BY_LANES = (((1,), (1,)), ((), ()))
BY_ROWS = (((0,), (0,)), ((), ()))


def place():
    return lax.axis_index("row"), lax.axis_index(STRIP)


def device_at(row, strip):
    pairs = lax.axis_size("pair")
    return (lax.axis_index("grp"), row, lax.div(strip, pairs), lax.rem(strip, pairs))


def sems(count):
    return [pltpu.SemaphoreType.DMA((count,)), pltpu.SemaphoreType.DMA((count,))]


def around(count, me):
    return lambda step: lax.rem(me + step, count)


def far_first(count, me):
    def peer(step):
        up = step - 1
        up += jnp.where(up >= me, 1, 0)
        down = count - step
        down -= jnp.where(down <= me, 1, 0)
        return jnp.where(me < count // 2, down, up)

    return peer


def near_first(count, me):
    return lambda step: far_first(count, me)(count - step)


def post(count, me, order, device_of, source, landing, send_sem, recv_sem):
    def copy_of(step, slot):
        peer = order(step)
        return pltpu.make_async_remote_copy(
            src_ref=source(peer),
            dst_ref=landing.at[slot(peer)],
            send_sem=send_sem.at[step],
            recv_sem=recv_sem.at[slot(peer)],
            device_id=device_of(peer),
            device_id_type=MESH,
        )

    def start(low=1, high=count):
        @pl.loop(low, high)
        def _(step):
            copy_of(step, lambda peer: me).start()

    def arrive(low=1, high=count):
        @pl.loop(low, high)
        def _(step):
            copy_of(step, lambda peer: peer).wait_recv()

    def sent():
        @pl.loop(1, count)
        def _(step):
            copy_of(step, lambda peer: me).wait_send()

    return start, arrive, sent


def iota(shape, dim):
    return lax.broadcasted_iota(jnp.int32, shape, dim)


def dot(a, b, numbers=(((1,), (0,)), ((), ()))):
    return lax.dot_general(a, b, numbers, preferred_element_type=F32)


def slope(values):
    s = 1.0 / (1.0 + jnp.exp(-values))
    return s * (1.0 + values * (1.0 - s))


def total_of(count, landing):
    value = landing[0].astype(F32)
    for i in range(1, count):
        value += landing[i].astype(F32)
    return value


def whole_kernel(
    rows, strips, band, height2, scale_one, scale_two,
    x_any, f1_any, f2_any, up_any,
    ig_out, g1_out, g2_out,
    x_in, f1, f2, up_in, x_wide, x_turned, own, edges_f, edges, from_side, from_row, from_corner, from_up,
    tile, patches, inner, w1, w1_down, reorder, f2_down, pre, block_f, block, gathered, up_wide, up, pool_f, pool3, near3, sum_two,
    blocks, landed, grad_f, grad, grad_own, rims_f, rims, rim_rows, rim_side, rim_row, rim_corner, pool_all, near_all, pool_map, near_map,
    mine_blocks, one_landed, one_part, one_all,
    load_sem, a_send, a_recv, e_send, e_recv, b_send, b_recv, c_send, c_recv,
    d1_send, d1_recv, d2_send, d2_recv,
    p_send, p_on, p_recv, n_send, n_on, n_recv,
):
    row, strip = place()
    cols, pairs = lax.axis_size("col"), lax.axis_size("pair")
    col, pair = lax.axis_index("col"), lax.axis_index("pair")
    channels = f1.shape[1]
    filters = f2.shape[1]
    quads = 4 * channels
    width = x_in.shape[1]
    width2 = width // 4
    band2 = band // 4
    span = width2 + 2 * EDGE
    full2 = width2 * strips
    mid = pl.ds(EDGE, width2)
    reach = width2 + 4

    def row_device(i):
        return device_at(i, strip)

    def strip_device(i):
        return device_at(row, i)

    def there(way):
        a, b = row + way[0], strip + way[1]
        return (a >= 0) & (a < rows) & (b >= 0) & (b < strips)

    barrier = pltpu.get_barrier_semaphore()
    everyone = rows * strips
    for step in range(1, rows):
        pl.semaphore_signal(barrier, inc=1, device_id=row_device(lax.rem(row + step, rows)), device_id_type=MESH)
    for step in range(1, strips):
        pl.semaphore_signal(
            barrier, inc=1, device_id=strip_device(lax.rem(strip + step, strips)), device_id_type=MESH
        )
    for way in DIAGONALS:
        @pl.when(there(way))
        def _(way=way):
            pl.semaphore_signal(
                barrier, inc=1, device_id=device_at(row + way[0], strip + way[1]), device_id_type=MESH
            )
    loads = [
        pltpu.make_async_copy(source, target, load_sem.at[n])
        for n, (source, target) in enumerate([(x_any, x_in), (up_any, up_in), (f1_any, f1), (f2_any, f2)])
    ]
    for load in loads:
        load.start()

    shape = (width, width)
    pick = (iota(shape, 1) == 4 * (iota(shape, 0) % width2) + iota(shape, 0) // width2).astype(BF)
    low_half = iota((width2, 128), 1) < channels
    shape = (quads, quads)
    for k in range(2):
        inside, outside = iota(shape, 1 - k), iota(shape, k)
        home = 4 * (inside % channels) + 2 * (inside // (2 * channels)) + inside // channels % 2
        reorder[k] = (outside == home).astype(BF)
    grad_f[...] = jnp.zeros(grad_f.shape, F32)
    rims_f[...] = jnp.zeros(rims_f.shape, F32)
    sum_two[...] = jnp.zeros(sum_two.shape, F32)
    for line in (0, band + 1):
        patches[line] = jnp.zeros(patches.shape[1:], BF)
    for u in range(height2):
        pool_f[u, pl.ds(0, 2)] = jnp.zeros((2, quads), F32)
        pool_f[u, pl.ds(2 + reach, 2)] = jnp.zeros((2, quads), F32)
    for j in range(3):
        near3[j, 0] = jnp.zeros(near3.shape[2:], BF)
        near3[j, height2 + 1] = jnp.zeros(near3.shape[2:], BF)
    loads[0].wait()
    x_wide[...] = x_in[...].astype(F32)
    for h in range(band):
        line = x_wide[pl.ds(h, channels, stride=band), :].astype(BF)
        x_turned[pl.ds(2 * h * channels, channels), :] = line
        x_turned[pl.ds((2 * h + 1) * channels, channels), :] = line
    turned = dot(pick, x_turned[...], BY_LANES)
    for h in range(band):
        lanes = slice(h * 128, (h + 1) * 128)
        for half in range(2):
            even = turned[2 * half * width2 : (2 * half + 1) * width2, lanes]
            odd = turned[(2 * half + 1) * width2 : (2 * half + 2) * width2, lanes]
            value = jnp.where(low_half, even, odd)
            tile[h + 1, mid, pl.ds(half * 128, 128)] = value
            own[pl.ds(h * width2, width2), pl.ds(half * 128, 128)] = value.astype(BF)
    for h in range(band):
        edges_f[0, pl.ds(h * EDGE, EDGE)] = tile[h + 1, pl.ds(EDGE, EDGE)]
        edges_f[1, pl.ds(h * EDGE, EDGE)] = tile[h + 1, pl.ds(width2, EDGE)]
    edges[...] = edges_f[:, : band * EDGE].astype(BF)

    diagonals = (jnp.where(row > 0, 1, 0) + jnp.where(row < rows - 1, 1, 0)) * (
        jnp.where(strip > 0, 1, 0) + jnp.where(strip < strips - 1, 1, 0)
    )
    pl.semaphore_wait(barrier, rows - 1 + strips - 1 + diagonals)
    edge_rows = band * EDGE
    up_edge = 2 * height2

    def corner_of(way):
        return (way[1] + 1) // 2, (way[0] + 1) // 2

    def border(kind, way, arriving=False):
        (source_of, slot_of, send_sem, recv_sem), back = kind, (-way[0], -way[1])
        land = way if arriving else back
        return pltpu.make_async_remote_copy(
            src_ref=source_of(way),
            dst_ref=slot_of(land),
            send_sem=send_sem.at[WAYS.index(way)],
            recv_sem=recv_sem.at[WAYS.index(land)],
            device_id=device_at(row + way[0], strip + way[1]),
            device_id_type=MESH,
        )

    def start_border(kind, way):
        @pl.when(there(way))
        def _():
            border(kind, way).start()

    def clear_border(kind, way):
        @pl.when(jnp.logical_not(there(way)))
        def _():
            slot = kind[1](way)
            slot[...] = jnp.zeros(slot.shape, slot.dtype)

    def end_border(kind, way):
        @pl.when(there(way))
        def _():
            border(kind, way, True).wait_recv()

    def sent_border(kind, way):
        @pl.when(there(way))
        def _():
            border(kind, way).wait_send()

    def slots(side_slots, row_slots, corner_slots):
        def slot_of(way):
            side, top = corner_of(way)
            if way[0] == 0:
                return side_slots.at[side]
            if way[1] == 0:
                return row_slots.at[top]
            return corner_slots.at[2 * top + side]

        return slot_of

    def cell_source(way):
        side = corner_of(way)[0]
        if way[0] == 0:
            return edges.at[side]
        if way[1] == 0:
            return own.at[pl.ds(0 if way[0] < 0 else (band - 1) * width2, width2)]
        return edges.at[side, pl.ds(0 if way[0] < 0 else edge_rows - 16, 16)]

    def rim_source(way):
        side, top = corner_of(way)
        return rim_rows.at[top] if way[1] == 0 else rims.at[side]

    cell_kind = (cell_source, slots(from_side, from_row, from_corner), a_send, a_recv)
    rim_kind = (rim_source, slots(rim_side, rim_row, rim_corner), e_send, e_recv)

    def up_border(side, arriving=False):
        land = side if arriving else 1 - side
        return pltpu.make_async_remote_copy(
            src_ref=up_in.at[pl.ds(0 if side == 0 else up_in.shape[0] - up_edge, up_edge)],
            dst_ref=from_up.at[land],
            send_sem=a_send.at[len(WAYS) + side],
            recv_sem=a_recv.at[len(WAYS) + land],
            device_id=device_at(row, strip + (-1, 1)[side]),
            device_id_type=MESH,
        )

    for way in WAYS[2:] + WAYS[:2]:
        start_border(cell_kind, way)
    for way in WAYS:
        clear_border(cell_kind, way)
        clear_border(rim_kind, way)
    loads[1].wait()
    for side in range(2):
        @pl.when(there((0, (-1, 1)[side])))
        def _(side=side):
            up_border(side).start()

        @pl.when(jnp.logical_not(there((0, (-1, 1)[side]))))
        def _(side=side):
            from_up[side] = jnp.zeros(from_up.shape[1:], BF)

    loads[2].wait()
    zero = jnp.zeros((channels, channels), F32)
    nothing = jnp.zeros((channels, 128), BF)
    for i in range(3):
        a, b, c = [f1[3 * i + j].astype(F32) for j in range(3)]
        bc, ab, za, cz = [
            jnp.concatenate(two, 1).astype(BF) for two in ((b, c), (a, b), (zero, a), (c, zero))
        ]
        table = (
            (bc, nothing, za, nothing),
            (ab, cz, nothing, nothing),
            (za, bc, nothing, nothing),
            (nothing, ab, nothing, cz),
        )
        for p in range(4):
            for k in range(4):
                w1[pl.ds(p * channels, channels), pl.ds(i * 512 + k * 128, 128)] = table[p][k]
    for k in range(12):
        w1_down[pl.ds(k * 128, 128)] = w1[:, pl.ds(k * 128, 128)].astype(F32).T.astype(BF)

    def widen(line):
        here = tile[line]
        patches[line, :, pl.ds(0, quads)] = here.astype(BF)
        patches[line, :, pl.ds(quads, 128)] = pltpu.roll(here[:, quads - 128 :], 1, 0).astype(BF)
        patches[line, :, pl.ds(quads + 128, 128)] = pltpu.roll(here[:, :128], span - 1, 0).astype(BF)

    def silu(values):
        return values / (1.0 + jnp.exp(-values))

    def pool(h):
        total = (silu(pre[h]) + silu(pre[h + 1])) * 0.25
        left, right = total[:, :128], total[:, 128:]
        left += pltpu.roll(left, 64, 1)
        right += pltpu.roll(right, 64, 1)
        return jnp.where(iota((span, 128), 1) < channels, left, right)

    side_at = [pl.ds(0, EDGE), pl.ds(EDGE + width2, EDGE)]
    for way in WAYS[:2]:
        end_border(cell_kind, way)
    for side in range(2):
        edge = from_side[side].astype(F32)
        for h in range(band):
            tile[h + 1, side_at[side]] = edge[h * EDGE : (h + 1) * EDGE]
    for line in range(1, band + 1):
        widen(line)
    windows = jnp.concatenate([patches[i : i + band].reshape(band * span, 512) for i in range(3)], 1)
    pre[0:band] = dot(windows, w1_down[...]).reshape(band, span, quads)
    halves = {h: pool(h) for h in range(2, band - 2, 2)}

    for way in WAYS[2:]:
        end_border(cell_kind, way)
    for top in range(2):
        line = 0 if top == 0 else band + 1
        tile[line, mid] = from_row[top].astype(F32)
        for side in range(2):
            corner = from_corner[2 * top + side].astype(F32)
            tile[line, side_at[side]] = corner[16 - EDGE :] if top == 0 else corner[:EDGE]
        widen(line)
    pre[0] += dot(patches[0], w1_down[pl.ds(0, 512)])
    pre[band - 1] += dot(patches[band + 1], w1_down[pl.ds(1024, 512)])
    for h in (0, band - 2):
        halves[h] = pool(h)
    pooled = [jnp.concatenate([halves[4 * u], halves[4 * u + 2]], 1) for u in range(band2)]
    pooled = jnp.concatenate(pooled, 0)
    at_col = strip * width2 - EDGE + iota((band2 * span, quads), 0) % span
    pooled = jnp.where((at_col >= 0) & (at_col < full2), pooled, 0.0)
    for u in range(band2):
        block_f[pl.ds(u * reach, reach)] = pooled[u * span + 2 : u * span + 2 + reach]
    pooled = block_f[: band2 * reach].astype(BF)
    block[...] = pooled
    start, arrive, b_sent = post(
        rows, row, near_first(rows, row), row_device, lambda peer: block, gathered, b_send, b_recv
    )
    start()
    gathered[row] = pooled

    for h in range(band):
        pre[h] = slope(pre[h]) * 0.25
    for line in range(band + 2):
        inner[line, :, pl.ds(0, quads)] = tile[line, mid].astype(BF)
        inner[line, :, pl.ds(quads, 128)] = tile[line, pl.ds(EDGE - 1, width2), pl.ds(quads - 128, 128)].astype(BF)
        inner[line, :, pl.ds(quads + 128, 128)] = tile[line, pl.ds(EDGE + 1, width2), pl.ds(0, 128)].astype(BF)
    for side in range(2):
        @pl.when(there((0, (-1, 1)[side])))
        def _(side=side):
            up_border(side, True).wait_recv()
    up_wide[pl.ds(0, up_edge)] = from_up[0].astype(F32)
    up_wide[pl.ds(up_edge, width2 * height2)] = up_in[...].astype(F32)
    up_wide[pl.ds(up_edge + width2 * height2, up_edge)] = from_up[1].astype(F32)
    for u in range(height2):
        up[u, pl.ds(0, 2)] = jnp.zeros((2, filters), F32)
        up[u, pl.ds(2, width2 + 4)] = up_wide[pl.ds(u, width2 + 4, stride=height2), :]
        up[u, pl.ds(width2 + 6, 2)] = jnp.zeros((2, filters), F32)
    loads[3].wait()
    f2[...] = dot(f2[...].reshape(9 * filters, quads), reorder[0]).astype(BF).reshape(9, filters, quads)
    for t in range(9):
        f2_down[t // 3, pl.ds(t % 3 * quads, quads)] = f2[t].astype(F32).T.astype(BF)

    half, bands = height2 // 2, rows // 2
    near_band = jnp.where(row < bands, 0, bands)
    far_band = bands - near_band

    def forward(band_at):
        at = band_at * band2
        for d in range(half):
            k = d % band2
            pool_f[at + d, pl.ds(2, reach)] = gathered[band_at + d // band2].astype(F32)[
                k * reach : (k + 1) * reach
            ]
            wide = pool_f[at + d]
            pool3[at + d, :, pl.ds(0, quads)] = pltpu.roll(wide, 1, 0).astype(BF)
            pool3[at + d, :, pl.ds(quads, quads)] = wide.astype(BF)
            pool3[at + d, :, pl.ds(2 * quads, quads)] = pltpu.roll(wide, span - 1, 0).astype(BF)
            spot = pl.multiple_of((at + d) * width2, width2)
            pool_all[strip, pl.ds(spot, width2)] = wide[EDGE : EDGE + width2].astype(BF)
        windows = pool3[pl.ds(at, half)].reshape(half * span, 3 * quads)
        if filters % 128 == 0:
            sums = dot(windows, jnp.concatenate([f2_down[i] for i in range(3)], 1))
            sums = [sums[:, i * filters : (i + 1) * filters] for i in range(3)]
        else:
            sums = [dot(windows, f2_down[i]) for i in range(3)]
        for i in range(3):
            sum_two[pl.ds(at + 2 - i, half)] += sums[i].reshape(half, span, filters)

    arrive(1, rows - bands)
    forward(near_band)
    arrive(rows - bands, rows)
    def across(source, table, send_sem, recv_sem, step):
        return pltpu.make_async_remote_copy(
            src_ref=source,
            dst_ref=table.at[strip],
            send_sem=send_sem.at[step],
            recv_sem=recv_sem.at[strip],
            device_id=device_at(row, lax.rem(col + step, cols) * pairs + pair),
            device_id_type=MESH,
        )

    def onward(table, send_sem, recv_sem, column, step):
        slot = column * pairs + pair
        return pltpu.make_async_remote_copy(
            src_ref=table.at[slot],
            dst_ref=table.at[slot],
            send_sem=send_sem.at[column * pairs + step],
            recv_sem=recv_sem.at[slot],
            device_id=device_at(row, col * pairs + lax.rem(pair + step, pairs)),
            device_id_type=MESH,
        )

    def arrival(table, send_sem, recv_sem, slot):
        return pltpu.make_async_remote_copy(
            src_ref=table.at[slot],
            dst_ref=table.at[slot],
            send_sem=send_sem.at[0],
            recv_sem=recv_sem.at[slot],
            device_id=device_at(row, lax.rem(col + 1, cols) * pairs + pair),
            device_id_type=MESH,
        )

    def share(table, send_sem, on_sem, recv_sem):
        for step in range(1, cols):
            across(table.at[strip], table, send_sem, recv_sem, step).start()
        for step in range(1, pairs):
            onward(table, on_sem, recv_sem, col, step).start()

    def pass_on(table, send_sem, on_sem, recv_sem):
        for step in range(1, cols):
            column = lax.rem(col + step, cols)
            arrival(table, send_sem, recv_sem, column * pairs + pair).wait_recv()
            for other in range(1, pairs):
                onward(table, on_sem, recv_sem, column, other).start()

    def settle(table, send_sem, on_sem, recv_sem):
        for step in range(1, cols):
            across(table.at[strip], table, send_sem, recv_sem, step).wait_send()
        for step in range(cols):
            column = lax.rem(col + step, cols)
            for other in range(1, pairs):
                onward(table, on_sem, recv_sem, column, other).wait_send()
                slot = column * pairs + lax.rem(pair + other, pairs)
                arrival(table, send_sem, recv_sem, slot).wait_recv()

    forward(far_band)
    pool_sems = (p_send, p_on, p_recv)
    share(pool_all, *pool_sems)
    spots = height2 * span
    pre_two = sum_two[1 : height2 + 1].reshape(spots, filters)
    near = up[0:height2].reshape(spots, filters) * slope(pre_two)
    near3[0, 1 : height2 + 1] = pltpu.roll(near, spots - 1, 0).astype(BF).reshape(height2, span, filters)
    near3[1, 1 : height2 + 1] = near.astype(BF).reshape(height2, span, filters)
    near3[2, 1 : height2 + 1] = pltpu.roll(near, 1, 0).astype(BF).reshape(height2, span, filters)

    def backward(band_at):
        at = band_at * band2
        windows = [
            near3[j, pl.ds(at + 2 - i, half)].reshape(half * span, filters) for i in range(3) for j in range(3)
        ]
        if filters % 128 == 0:
            total = dot(jnp.concatenate(windows, 1), f2[...].reshape(9 * filters, quads))
        else:
            total = jnp.zeros((half * span, quads), F32)
            for t in range(9):
                total += dot(windows[t], f2[t])
        for d in range(half):
            blocks[band_at + d // band2, pl.ds(d % band2 * width2, width2)] = total[
                d * span + EDGE : d * span + EDGE + width2
            ].astype(BF)

    start, arrive, c_sent = post(
        rows, row, far_first(rows, row), row_device, lambda peer: blocks.at[peer], landed, c_send, c_recv
    )
    backward(far_band)
    start(1, bands + 1)
    backward(near_band)
    start(bands + 1, rows)
    landed[row] = blocks[row]
    for u in range(height2):
        near_all[strip, pl.ds(u * width2, width2)] = near[
            u * span + EDGE : u * span + EDGE + width2
        ].astype(BF)
    near_sems = (n_send, n_on, n_recv)
    share(near_all, *near_sems)
    arrive()
    parts = total_of(rows, landed)
    wide = {}
    for k in range(band2):
        for i in range(2):
            some = parts[k * width2 : (k + 1) * width2, i * 128 : (i + 1) * 128]
            other = pltpu.roll(some, 64, 1)
            wide[k, i] = jnp.concatenate(
                [jnp.where(low_half, some, other), jnp.where(low_half, other, some)], 1
            )

    for h in range(band):
        k, i = h // 4, (h // 2) % 2
        body = wide[k, i] * pre[h, mid]
        grad_f[h + 1, mid] = body
        grad_own[pl.ds(h * width2, width2)] = body.astype(BF)
        rims_f[0, pl.ds(h, 1)] = body[:1]
        rims_f[1, pl.ds(h, 1)] = body[width2 - 1 :]
        if h in (0, band - 1):
            rim_rows[h // (band - 1)] = body.astype(BF)

    low = iota((channels, 128), 1) < channels
    halves, ends = [], []
    own_spots = band * span
    windows = [inner[i : i + band].reshape(band * width2, 512) for i in range(3)]
    turned = grad_own[...].astype(F32).T.astype(BF)
    taps = dot(turned, jnp.concatenate([window[:, :quads] for window in windows], 1))
    outer = jnp.concatenate([turned[:channels], turned[3 * channels :]], 0)
    outer = dot(outer, jnp.concatenate([window[:, quads:] for window in windows], 1))

    def cut(i, p, k):
        if k < 2:
            return taps[p * channels : (p + 1) * channels, i * quads + k * 128 : i * quads + (k + 1) * 128]
        half = channels * (p // 3)
        return outer[half : half + channels, i * quads + (k - 2) * 128 : i * quads + (k - 1) * 128]

    for i in range(3):
        bc = pltpu.roll(cut(i, 0, 0) + cut(i, 2, 1), 64, 1)
        ab = cut(i, 1, 0) + cut(i, 3, 1)
        za = pltpu.roll(cut(i, 0, 2) + cut(i, 2, 0), 64, 1)
        cz = cut(i, 1, 1) + cut(i, 3, 3)
        halves.append(ab + jnp.where(low, za, bc))
        ends.append(cz + bc)
    short = channels // 2
    last = jnp.where(low[:short], ends[2][:short], pltpu.roll(ends[2][short:], 64, 1))
    packed = halves + [jnp.where(low, ends[0], pltpu.roll(ends[1], 64, 1)), last]
    packed = jnp.concatenate(packed, 0)
    owners, piece = mine_blocks.shape[:2]
    for o in range(owners):
        some = packed[o * piece : (o + 1) * piece]
        if some.shape[0] < piece:
            some = jnp.concatenate([some, jnp.zeros((piece - some.shape[0], 128), F32)], 0)
        mine_blocks[o] = some.astype(BF)

    me = row * strips + strip
    low_row = rows // 2 - 1

    def piece_of(r, s):
        return 2 * s + r - low_row

    def owns(r, s):
        return (r >= low_row) & (r <= low_row + 1) & (piece_of(r, s) < owners)

    my_piece = piece_of(row, strip)
    owning = owns(row, strip)

    def target(step):
        z, s = step // strips, step % strips
        return jnp.where(row < rows // 2, rows - 1 - z, z), lax.rem(col + cols - 1 - s // pairs, cols) * pairs + lax.rem(
            pair + pairs - 1 - s % pairs, pairs
        )

    def to_owner(step, arriving=False):
        r, s = target(step)
        other = r * strips + s
        return pltpu.make_async_remote_copy(
            src_ref=mine_blocks.at[my_piece if arriving else piece_of(r, s)],
            dst_ref=one_landed.at[other if arriving else me],
            send_sem=d1_send.at[step],
            recv_sem=d1_recv.at[other if arriving else me],
            device_id=device_at(r, s),
            device_id_type=MESH,
        )

    def from_owner(step, arriving=False):
        r, s = target(step)
        slot = piece_of(r, s) if arriving else my_piece
        return pltpu.make_async_remote_copy(
            src_ref=one_part,
            dst_ref=one_all.at[slot],
            send_sem=d2_send.at[step],
            recv_sem=d2_recv.at[slot],
            device_id=device_at(r, s),
            device_id_type=MESH,
        )

    def each_other(action):
        def one(step):
            r, s = target(step)

            @pl.when(r * strips + s != me)
            def _():
                action(step, owns(r, s))

        if everyone > 16:
            pl.loop(0, everyone)(one)
        else:
            for step in range(everyone):
                one(step)

    def send_out(step, owner):
        @pl.when(owner)
        def _():
            to_owner(step).start()

    def settle_out(step, owner):
        @pl.when(owner)
        def _():
            to_owner(step).wait_send()

        @pl.when(owning)
        def _():
            to_owner(step, True).wait_recv()

    def send_back(step, owner):
        @pl.when(owning)
        def _():
            from_owner(step).start()

    def settle_back(step, owner):
        @pl.when(owning)
        def _():
            from_owner(step).wait_send()

        @pl.when(owner)
        def _():
            from_owner(step, True).wait_recv()

    each_other(send_out)

    @pl.when(owning)
    def _():
        one_landed[me] = mine_blocks[my_piece]

    rims[...] = rims_f[...].astype(BF)
    for way in WAYS:
        start_border(rim_kind, way)

    pass_on(pool_all, *pool_sems)
    pass_on(near_all, *near_sems)
    each_other(settle_out)

    @pl.when(owning)
    def _():
        if everyone > 16:
            part = lax.fori_loop(
                1, everyone, lambda i, t: t + one_landed[i].astype(F32), one_landed[0].astype(F32)
            )
        else:
            part = total_of(everyone, one_landed)
        one_part[...] = part.astype(BF)
        one_all[my_piece] = part.astype(BF)

    each_other(send_back)

    settle(pool_all, *pool_sems)
    settle(near_all, *near_sems)
    near_map[0] = jnp.zeros(near_map.shape[1:], BF)
    near_map[height2 + 1] = jnp.zeros(near_map.shape[1:], BF)
    at_lane = iota((filters, full2), 1)

    def assemble(u):
        at = u * width2
        if not isinstance(u, int):
            at = pl.multiple_of(at, width2)
        line = [near_all[s, pl.ds(at, width2)].astype(F32) for s in range(strips)]
        line = jnp.concatenate(line, 0).T
        after = jnp.where(at_lane < full2 - 1, pltpu.roll(line, full2 - 1, 1), 0.0)
        before = jnp.where(at_lane > 0, pltpu.roll(line, 1, 1), 0.0)
        for j, value in enumerate((after, line, before)):
            near_map[u + 1, pl.ds(j * filters, filters)] = value.astype(BF)
        line = jnp.concatenate([pool_all[s, pl.ds(at, width2)] for s in range(strips)], 0)
        pool_map[u] = dot(line, reorder[1]).astype(BF)

    chunk = max(1, 1024 // full2)
    steps = height2 // chunk
    if steps == 1:
        for u in range(height2):
            assemble(u)
    else:
        pl.loop(0, height2)(assemble)

    def filter_taps(i, step):
        at = step * chunk
        left = jnp.concatenate([near_map[at + k + 2 - i] for k in range(chunk)], 1)
        right = pool_map[pl.ds(at, chunk)].reshape(chunk * full2, quads)
        return scale_two * dot(left, right).reshape(3, filters, quads)

    def filter_gradient(i):
        g2_out[3 * i : 3 * i + 3] = filter_taps(i, 0)
        if steps > 1:
            @pl.loop(1, steps)
            def _(step):
                g2_out[3 * i : 3 * i + 3] += filter_taps(i, step)

    for i in range(3):
        filter_gradient(i)

    for way in WAYS:
        end_border(rim_kind, way)
    for h in range(band):
        for side, at in ((0, EDGE - 1), (1, EDGE + width2)):
            grad_f[h + 1, pl.ds(at, 1)] = rim_side[side].astype(F32)[h : h + 1]
    for top, line, h in ((0, 0, band - 1), (1, band + 1, 0)):
        grad_f[line, mid] = rim_row[top].astype(F32)
        for side, at in ((0, EDGE - 1), (1, EDGE + width2)):
            grad_f[line, pl.ds(at, 1)] = rim_corner[2 * top + side].astype(F32)[h : h + 1]
    for line in range(band + 2):
        grad[line] = grad_f[line].astype(BF)
    cells = jnp.concatenate([grad[2 - i : 2 - i + band].reshape(own_spots, quads) for i in range(3)], 1)
    kernel = jnp.concatenate([w1[:, i * 512 : (i + 1) * 512] for i in range(3)], 0)
    total = dot(cells, kernel)
    before = pltpu.roll(total[:, quads : quads + 128], own_spots - 1, 0)
    after = pltpu.roll(total[:, quads + 128 :], 1, 0)
    sides = (total[:, :128] + after, total[:, 128:quads] + before)
    turned = []
    for h in range(band):
        lines_of = []
        for b in range(4):
            value = sides[b // 2][h * span + EDGE : h * span + EDGE + width2]
            lines_of.append(jnp.where(low_half == (b % 2 == 0), value, 0.0).astype(BF))
        turned.append(jnp.concatenate(lines_of, 0))
    turned = dot(jnp.concatenate(turned, 1), pick, BY_ROWS)
    for h in range(band):
        at = 2 * h * channels
        x_wide[pl.ds(h, channels, stride=band), :] = (
            turned[at : at + channels] + turned[at + channels : at + 2 * channels]
        )
    ig_out[...] = x_wide[...].astype(BF)

    b_sent()
    c_sent()
    for way in WAYS:
        sent_border(cell_kind, way)
        sent_border(rim_kind, way)
    for side in range(2):
        @pl.when(there((0, (-1, 1)[side])))
        def _(side=side):
            up_border(side).wait_send()
    each_other(settle_back)
    done = scale_one * one_all[...].astype(F32).reshape(owners * piece, 128)
    rolled = pltpu.roll(done, 64, 1)
    for i in range(3):
        for j in range(3):
            at = (i if j < 2 else 3 + i // 2) * channels
            if (i, j) == (2, 2):
                value = jnp.concatenate([done[at : at + short], rolled[at : at + short]], 0)
            else:
                value = (done if (j if j < 2 else i % 2) == 0 else rolled)[at : at + channels]
            g1_out[3 * i + j] = value[:, :channels]


def write_kernel(*refs):
    count = len(refs) // 2
    sources, targets, sem = refs[:count], refs[count:-1], refs[-1]
    copies = [pltpu.make_async_copy(sources[n], targets[n], sem.at[n]) for n in range(count)]
    for copy in copies:
        copy.start()
    for copy in copies:
        copy.wait()


def write_out(*arrays):
    arrays = [pltpu.with_memory_space_constraint(a, pltpu.VMEM) for a in arrays]
    return pl.pallas_call(
        write_kernel,
        out_shape=tuple(jax.ShapeDtypeStruct(a.shape, a.dtype) for a in arrays),
        in_specs=[VMEM] * len(arrays),
        out_specs=(HBM,) * len(arrays),
        scratch_shapes=[pltpu.SemaphoreType.DMA((len(arrays),))],
    )(*arrays)


def local(features_in, filters_one, filters_two, out_grad):
    channels, band, width = features_in.shape
    rows, strips = lax.axis_size("row"), lax.axis_size(STRIP)
    cols, pairs = lax.axis_size("col"), lax.axis_size("pair")
    filters = filters_two.shape[0]
    quads = 4 * channels
    height2 = out_grad.shape[2]
    width2, band2 = width // 4, band // 4
    span = width2 + 2 * EDGE
    full2 = width2 * strips
    spots = band2 * width2
    halves = 9 * channels // 2
    piece = -(-halves // (2 * strips) // 8) * 8
    owners = -(-halves // piece)

    def v(shape, kind=BF):
        return pltpu.VMEM(shape, kind)

    scratch = [
        v((channels * band, width)),
        v((9, channels, channels)),
        v((9, filters, quads)),
        v((width2 * height2, filters)),
        v((channels * band, width), F32),
        v((2 * channels * band, width)),
        v((band * width2, quads)),
        v((2, band * EDGE + 8, quads), F32),
        v((2, band * EDGE, quads)),
        v((2, band * EDGE, quads)),
        v((2, width2, quads)),
        v((4, 16, quads)),
        v((2, 2 * height2, filters)),
        v((band + 3, span, quads), F32),
        v((band + 2, span, 512)),
        v((band + 2, width2, 512)),
        v((quads, 3 * 512)),
        v((3 * 512, quads)),
        v((2, quads, quads)),
        v((3, 3 * quads, filters)),
        v((band + 1, span, quads), F32),
        v((band2 * (width2 + 4) + 8, quads), F32),
        v((band2 * (width2 + 4), quads)),
        v((rows, band2 * (width2 + 4), quads)),
        v((span * height2, filters), F32),
        v((height2 + 1, span, filters), F32),
        v((height2 + 1, span, quads), F32),
        v((height2, span, 3 * quads)),
        v((3, height2 + 2, span, filters)),
        v((height2 + 2, span, filters), F32),
        v((rows, spots, quads)),
        v((rows, spots, quads)),
        v((band + 3, span, quads), F32),
        v((band + 2, span, quads)),
        v((band * width2, quads)),
        v((2, 16, quads), F32),
        v((2, 16, quads)),
        v((2, width2, quads)),
        v((2, 16, quads)),
        v((2, width2, quads)),
        v((4, 16, quads)),
        v((strips, height2 * width2, quads)),
        v((strips, height2 * width2, filters)),
        v((height2, full2, quads)),
        v((height2 + 2, 3 * filters, full2)),
        v((owners, piece, 128)),
        v((rows * strips, piece, 128)),
        v((piece, 128)),
        v((owners, piece, 128)),
        pltpu.SemaphoreType.DMA((4,)),
    ]
    scratch += sems(len(WAYS) + 2) + sems(len(WAYS)) + sems(rows) + sems(rows) + sems(rows * strips) + sems(rows * strips)
    for _ in range(2):
        scratch += [
            pltpu.SemaphoreType.DMA((cols,)),
            pltpu.SemaphoreType.DMA((cols * pairs,)),
            pltpu.SemaphoreType.DMA((strips,)),
        ]
    arguments = (
        features_in.reshape(channels * band, width),
        jnp.transpose(filters_one, (1, 2, 0, 3)).reshape(9, channels, channels),
        jnp.transpose(filters_two, (1, 2, 0, 3)).reshape(9, filters, quads),
        jnp.transpose(out_grad, (1, 2, 0)).reshape(width2 * height2, filters),
    )
    arguments = [pltpu.with_memory_space_constraint(a, pltpu.HBM) for a in arguments]
    share = 1 if rows * strips <= 64 else 2
    scale_one = 1.0 / math.sqrt(band * rows * width * strips)
    scale_two = 1.0 / math.sqrt(height2 * full2)
    ig, g1, g2 = pl.pallas_call(
        functools.partial(whole_kernel, rows, strips, band, height2, scale_one, scale_two),
        out_shape=(
            jax.ShapeDtypeStruct((channels * band, width), BF),
            jax.ShapeDtypeStruct((9, channels, channels), F32),
            jax.ShapeDtypeStruct((9, filters, quads), F32),
        ),
        in_specs=[HBM] * 4,
        out_specs=(VMEM,) * 3,
        scratch_shapes=scratch,
        compiler_params=pltpu.CompilerParams(
            collective_id=0, has_side_effects=True, vmem_limit_bytes=share * 28 * 1024 * 1024
        ),
    )(*arguments)
    ig, g1, g2 = write_out(ig, g1, g2)
    grad_one = jnp.transpose(g1.reshape(3, 3, channels, channels), (2, 0, 1, 3))
    grad_two = jnp.transpose(g2.reshape(3, 3, filters, quads), (2, 0, 1, 3))
    return (ig.reshape(channels, band, width), grad_one, grad_two)


def solution(mesh):
    in_specs = (
        P("grp", "row", ("col", "pair")),
        P(),
        P("row", None, None, None),
        P(("grp", "row"), ("col", "pair"), None),
    )
    out_specs = (
        P("grp", "row", ("col", "pair")),
        P("grp", None, None, None),
        P(("grp", "row"), None, None, None),
    )
    return jax.shard_map(local, mesh=mesh, in_specs=in_specs, out_specs=out_specs, check_vma=False)
```

```python
import functools
import math

import jax
import jax.numpy as jnp
from jax import lax
from jax.experimental import pallas as pl
from jax.experimental.pallas import tpu as pltpu
from jax.sharding import PartitionSpec as P

MESH = pl.DeviceIdType.MESH
VMEM = pl.BlockSpec(memory_space=pltpu.VMEM)
HBM = pl.BlockSpec(memory_space=pltpu.HBM)
STRIP = ("col", "pair")
BF = jnp.bfloat16
F32 = jnp.float32

EDGE = 4

DIAGONALS = [(a, b) for a in (-1, 1) for b in (-1, 1)]
WAYS = [(0, -1), (0, 1), (-1, 0), (1, 0)] + DIAGONALS

BY_LANES = (((1,), (1,)), ((), ()))
BY_ROWS = (((0,), (0,)), ((), ()))


def place():
    return lax.axis_index("row"), lax.axis_index(STRIP)


def device_at(row, strip):
    pairs = lax.axis_size("pair")
    return (lax.axis_index("grp"), row, lax.div(strip, pairs), lax.rem(strip, pairs))


def sems(count):
    return [pltpu.SemaphoreType.DMA((count,)), pltpu.SemaphoreType.DMA((count,))]


def around(count, me):
    return lambda step: lax.rem(me + step, count)


def far_first(count, me):
    def peer(step):
        up = step - 1
        up += jnp.where(up >= me, 1, 0)
        down = count - step
        down -= jnp.where(down <= me, 1, 0)
        return jnp.where(me < count // 2, down, up)

    return peer


def near_first(count, me):
    return lambda step: far_first(count, me)(count - step)


def post(count, me, order, device_of, source, landing, send_sem, recv_sem):
    def copy_of(step, slot):
        peer = order(step)
        return pltpu.make_async_remote_copy(
            src_ref=source(peer),
            dst_ref=landing.at[slot(peer)],
            send_sem=send_sem.at[step],
            recv_sem=recv_sem.at[slot(peer)],
            device_id=device_of(peer),
            device_id_type=MESH,
        )

    def start(low=1, high=count):
        @pl.loop(low, high)
        def _(step):
            copy_of(step, lambda peer: me).start()

    def arrive(low=1, high=count):
        @pl.loop(low, high)
        def _(step):
            copy_of(step, lambda peer: peer).wait_recv()

    def sent():
        @pl.loop(1, count)
        def _(step):
            copy_of(step, lambda peer: me).wait_send()

    return start, arrive, sent


def iota(shape, dim):
    return lax.broadcasted_iota(jnp.int32, shape, dim)


def dot(a, b, numbers=(((1,), (0,)), ((), ()))):
    return lax.dot_general(a, b, numbers, preferred_element_type=F32)


def slope(values):
    s = 1.0 / (1.0 + jnp.exp(-values))
    return s * (1.0 + values * (1.0 - s))


def total_of(count, landing):
    value = landing[0].astype(F32)
    for i in range(1, count):
        value += landing[i].astype(F32)
    return value


def whole_kernel(
    rows, strips, band, height2, scale_one, scale_two,
    x_any, f1_any, f2_any, up_any,
    ig_out, g1_out, g2_out,
    x_in, f1, f2, up_in, x_wide, x_turned, own, edges_f, edges, from_side, from_row, from_corner, from_up,
    tile, patches, inner, w1, w1_down, reorder, f2_down, pre, block_f, block, gathered, up_wide, up, pool_f, pool3, near3, sum_two,
    blocks, landed, grad_f, grad, grad_own, rims_f, rims, rim_rows, rim_side, rim_row, rim_corner, pool_all, near_all, pool_map, near_map,
    mine_blocks, one_landed, one_part, one_all,
    load_sem, a_send, a_recv, e_send, e_recv, b_send, b_recv, c_send, c_recv,
    d1_send, d1_recv, d2_send, d2_recv,
    p_send, p_on, p_recv, n_send, n_on, n_recv,
):
    row, strip = place()
    cols, pairs = lax.axis_size("col"), lax.axis_size("pair")
    col, pair = lax.axis_index("col"), lax.axis_index("pair")
    channels = f1.shape[1]
    filters = f2.shape[1]
    quads = 4 * channels
    width = x_in.shape[1]
    width2 = width // 4
    band2 = band // 4
    span = width2 + 2 * EDGE
    full2 = width2 * strips
    mid = pl.ds(EDGE, width2)
    reach = width2 + 4

    def row_device(i):
        return device_at(i, strip)

    def strip_device(i):
        return device_at(row, i)

    def there(way):
        a, b = row + way[0], strip + way[1]
        return (a >= 0) & (a < rows) & (b >= 0) & (b < strips)

    barrier = pltpu.get_barrier_semaphore()
    everyone = rows * strips
    for step in range(1, rows):
        pl.semaphore_signal(barrier, inc=1, device_id=row_device(lax.rem(row + step, rows)), device_id_type=MESH)
    for step in range(1, strips):
        pl.semaphore_signal(
            barrier, inc=1, device_id=strip_device(lax.rem(strip + step, strips)), device_id_type=MESH
        )
    for way in DIAGONALS:
        @pl.when(there(way))
        def _(way=way):
            pl.semaphore_signal(
                barrier, inc=1, device_id=device_at(row + way[0], strip + way[1]), device_id_type=MESH
            )
    loads = [
        pltpu.make_async_copy(source, target, load_sem.at[n])
        for n, (source, target) in enumerate([(x_any, x_in), (up_any, up_in), (f1_any, f1), (f2_any, f2)])
    ]
    for load in loads:
        load.start()

    shape = (width, width)
    pick = (iota(shape, 1) == 4 * (iota(shape, 0) % width2) + iota(shape, 0) // width2).astype(BF)
    low_half = iota((width2, 128), 1) < channels
    shape = (quads, quads)
    for k in range(2):
        inside, outside = iota(shape, 1 - k), iota(shape, k)
        home = 4 * (inside % channels) + 2 * (inside // (2 * channels)) + inside // channels % 2
        reorder[k] = (outside == home).astype(BF)
    grad_f[...] = jnp.zeros(grad_f.shape, F32)
    rims_f[...] = jnp.zeros(rims_f.shape, F32)
    sum_two[...] = jnp.zeros(sum_two.shape, F32)
    for line in (0, band + 1):
        patches[line] = jnp.zeros(patches.shape[1:], BF)
    for u in range(height2):
        pool_f[u, pl.ds(0, 2)] = jnp.zeros((2, quads), F32)
        pool_f[u, pl.ds(2 + reach, 2)] = jnp.zeros((2, quads), F32)
    for j in range(3):
        near3[j, 0] = jnp.zeros(near3.shape[2:], BF)
        near3[j, height2 + 1] = jnp.zeros(near3.shape[2:], BF)
    loads[0].wait()
    x_wide[...] = x_in[...].astype(F32)
    for h in range(band):
        line = x_wide[pl.ds(h, channels, stride=band), :].astype(BF)
        x_turned[pl.ds(2 * h * channels, channels), :] = line
        x_turned[pl.ds((2 * h + 1) * channels, channels), :] = line
    turned = dot(pick, x_turned[...], BY_LANES)
    for h in range(band):
        lanes = slice(h * 128, (h + 1) * 128)
        for half in range(2):
            even = turned[2 * half * width2 : (2 * half + 1) * width2, lanes]
            odd = turned[(2 * half + 1) * width2 : (2 * half + 2) * width2, lanes]
            value = jnp.where(low_half, even, odd)
            tile[h + 1, mid, pl.ds(half * 128, 128)] = value
            own[pl.ds(h * width2, width2), pl.ds(half * 128, 128)] = value.astype(BF)
    for h in range(band):
        edges_f[0, pl.ds(h * EDGE, EDGE)] = tile[h + 1, pl.ds(EDGE, EDGE)]
        edges_f[1, pl.ds(h * EDGE, EDGE)] = tile[h + 1, pl.ds(width2, EDGE)]
    edges[...] = edges_f[:, : band * EDGE].astype(BF)

    diagonals = (jnp.where(row > 0, 1, 0) + jnp.where(row < rows - 1, 1, 0)) * (
        jnp.where(strip > 0, 1, 0) + jnp.where(strip < strips - 1, 1, 0)
    )
    pl.semaphore_wait(barrier, rows - 1 + strips - 1 + diagonals)
    edge_rows = band * EDGE
    up_edge = 2 * height2

    def corner_of(way):
        return (way[1] + 1) // 2, (way[0] + 1) // 2

    def border(kind, way, arriving=False):
        (source_of, slot_of, send_sem, recv_sem), back = kind, (-way[0], -way[1])
        land = way if arriving else back
        return pltpu.make_async_remote_copy(
            src_ref=source_of(way),
            dst_ref=slot_of(land),
            send_sem=send_sem.at[WAYS.index(way)],
            recv_sem=recv_sem.at[WAYS.index(land)],
            device_id=device_at(row + way[0], strip + way[1]),
            device_id_type=MESH,
        )

    def start_border(kind, way):
        @pl.when(there(way))
        def _():
            border(kind, way).start()

    def clear_border(kind, way):
        @pl.when(jnp.logical_not(there(way)))
        def _():
            slot = kind[1](way)
            slot[...] = jnp.zeros(slot.shape, slot.dtype)

    def end_border(kind, way):
        @pl.when(there(way))
        def _():
            border(kind, way, True).wait_recv()

    def sent_border(kind, way):
        @pl.when(there(way))
        def _():
            border(kind, way).wait_send()

    def slots(side_slots, row_slots, corner_slots):
        def slot_of(way):
            side, top = corner_of(way)
            if way[0] == 0:
                return side_slots.at[side]
            if way[1] == 0:
                return row_slots.at[top]
            return corner_slots.at[2 * top + side]

        return slot_of

    def cell_source(way):
        side = corner_of(way)[0]
        if way[0] == 0:
            return edges.at[side]
        if way[1] == 0:
            return own.at[pl.ds(0 if way[0] < 0 else (band - 1) * width2, width2)]
        return edges.at[side, pl.ds(0 if way[0] < 0 else edge_rows - 16, 16)]

    def rim_source(way):
        side, top = corner_of(way)
        return rim_rows.at[top] if way[1] == 0 else rims.at[side]

    cell_kind = (cell_source, slots(from_side, from_row, from_corner), a_send, a_recv)
    rim_kind = (rim_source, slots(rim_side, rim_row, rim_corner), e_send, e_recv)

    def up_border(side, arriving=False):
        land = side if arriving else 1 - side
        return pltpu.make_async_remote_copy(
            src_ref=up_in.at[pl.ds(0 if side == 0 else up_in.shape[0] - up_edge, up_edge)],
            dst_ref=from_up.at[land],
            send_sem=a_send.at[len(WAYS) + side],
            recv_sem=a_recv.at[len(WAYS) + land],
            device_id=device_at(row, strip + (-1, 1)[side]),
            device_id_type=MESH,
        )

    for way in WAYS[2:] + WAYS[:2]:
        start_border(cell_kind, way)
    for way in WAYS:
        clear_border(cell_kind, way)
        clear_border(rim_kind, way)
    loads[1].wait()
    for side in range(2):
        @pl.when(there((0, (-1, 1)[side])))
        def _(side=side):
            up_border(side).start()

        @pl.when(jnp.logical_not(there((0, (-1, 1)[side]))))
        def _(side=side):
            from_up[side] = jnp.zeros(from_up.shape[1:], BF)

    loads[2].wait()
    zero = jnp.zeros((channels, channels), F32)
    nothing = jnp.zeros((channels, 128), BF)
    for i in range(3):
        a, b, c = [f1[3 * i + j].astype(F32) for j in range(3)]
        bc, ab, za, cz = [
            jnp.concatenate(two, 1).astype(BF) for two in ((b, c), (a, b), (zero, a), (c, zero))
        ]
        table = (
            (bc, nothing, za, nothing),
            (ab, cz, nothing, nothing),
            (za, bc, nothing, nothing),
            (nothing, ab, nothing, cz),
        )
        for p in range(4):
            for k in range(4):
                w1[pl.ds(p * channels, channels), pl.ds(i * 512 + k * 128, 128)] = table[p][k]
    for k in range(12):
        w1_down[pl.ds(k * 128, 128)] = w1[:, pl.ds(k * 128, 128)].astype(F32).T.astype(BF)

    def widen(line):
        here = tile[line]
        patches[line, :, pl.ds(0, quads)] = here.astype(BF)
        patches[line, :, pl.ds(quads, 128)] = pltpu.roll(here[:, quads - 128 :], 1, 0).astype(BF)
        patches[line, :, pl.ds(quads + 128, 128)] = pltpu.roll(here[:, :128], span - 1, 0).astype(BF)

    def silu(values):
        return values / (1.0 + jnp.exp(-values))

    def pool(h):
        total = (silu(pre[h]) + silu(pre[h + 1])) * 0.25
        left, right = total[:, :128], total[:, 128:]
        left += pltpu.roll(left, 64, 1)
        right += pltpu.roll(right, 64, 1)
        return jnp.where(iota((span, 128), 1) < channels, left, right)

    side_at = [pl.ds(0, EDGE), pl.ds(EDGE + width2, EDGE)]
    for way in WAYS[:2]:
        end_border(cell_kind, way)
    for side in range(2):
        edge = from_side[side].astype(F32)
        for h in range(band):
            tile[h + 1, side_at[side]] = edge[h * EDGE : (h + 1) * EDGE]
    for line in range(1, band + 1):
        widen(line)
    windows = jnp.concatenate([patches[i : i + band].reshape(band * span, 512) for i in range(3)], 1)
    pre[0:band] = dot(windows, w1_down[...]).reshape(band, span, quads)
    halves = {h: pool(h) for h in range(2, band - 2, 2)}

    for way in WAYS[2:]:
        end_border(cell_kind, way)
    for top in range(2):
        line = 0 if top == 0 else band + 1
        tile[line, mid] = from_row[top].astype(F32)
        for side in range(2):
            corner = from_corner[2 * top + side].astype(F32)
            tile[line, side_at[side]] = corner[16 - EDGE :] if top == 0 else corner[:EDGE]
        widen(line)
    pre[0] += dot(patches[0], w1_down[pl.ds(0, 512)])
    pre[band - 1] += dot(patches[band + 1], w1_down[pl.ds(1024, 512)])
    for h in (0, band - 2):
        halves[h] = pool(h)
    pooled = [jnp.concatenate([halves[4 * u], halves[4 * u + 2]], 1) for u in range(band2)]
    pooled = jnp.concatenate(pooled, 0)
    at_col = strip * width2 - EDGE + iota((band2 * span, quads), 0) % span
    pooled = jnp.where((at_col >= 0) & (at_col < full2), pooled, 0.0)
    for u in range(band2):
        block_f[pl.ds(u * reach, reach)] = pooled[u * span + 2 : u * span + 2 + reach]
    pooled = block_f[: band2 * reach].astype(BF)
    block[...] = pooled
    start, arrive, b_sent = post(
        rows, row, near_first(rows, row), row_device, lambda peer: block, gathered, b_send, b_recv
    )
    start()
    gathered[row] = pooled

    for h in range(band):
        pre[h] = slope(pre[h]) * 0.25
    for line in range(band + 2):
        inner[line, :, pl.ds(0, quads)] = tile[line, mid].astype(BF)
        inner[line, :, pl.ds(quads, 128)] = tile[line, pl.ds(EDGE - 1, width2), pl.ds(quads - 128, 128)].astype(BF)
        inner[line, :, pl.ds(quads + 128, 128)] = tile[line, pl.ds(EDGE + 1, width2), pl.ds(0, 128)].astype(BF)
    for side in range(2):
        @pl.when(there((0, (-1, 1)[side])))
        def _(side=side):
            up_border(side, True).wait_recv()
    up_wide[pl.ds(0, up_edge)] = from_up[0].astype(F32)
    up_wide[pl.ds(up_edge, width2 * height2)] = up_in[...].astype(F32)
    up_wide[pl.ds(up_edge + width2 * height2, up_edge)] = from_up[1].astype(F32)
    for u in range(height2):
        up[u, pl.ds(0, 2)] = jnp.zeros((2, filters), F32)
        up[u, pl.ds(2, width2 + 4)] = up_wide[pl.ds(u, width2 + 4, stride=height2), :]
        up[u, pl.ds(width2 + 6, 2)] = jnp.zeros((2, filters), F32)
    loads[3].wait()
    f2[...] = dot(f2[...].reshape(9 * filters, quads), reorder[0]).astype(BF).reshape(9, filters, quads)
    for t in range(9):
        f2_down[t // 3, pl.ds(t % 3 * quads, quads)] = f2[t].astype(F32).T.astype(BF)

    half, bands = height2 // 2, rows // 2
    near_band = jnp.where(row < bands, 0, bands)
    far_band = bands - near_band

    def forward(band_at):
        at = band_at * band2
        for d in range(half):
            k = d % band2
            pool_f[at + d, pl.ds(2, reach)] = gathered[band_at + d // band2].astype(F32)[
                k * reach : (k + 1) * reach
            ]
            wide = pool_f[at + d]
            pool3[at + d, :, pl.ds(0, quads)] = pltpu.roll(wide, 1, 0).astype(BF)
            pool3[at + d, :, pl.ds(quads, quads)] = wide.astype(BF)
            pool3[at + d, :, pl.ds(2 * quads, quads)] = pltpu.roll(wide, span - 1, 0).astype(BF)
            spot = pl.multiple_of((at + d) * width2, width2)
            pool_all[strip, pl.ds(spot, width2)] = wide[EDGE : EDGE + width2].astype(BF)
        windows = pool3[pl.ds(at, half)].reshape(half * span, 3 * quads)
        if filters % 128 == 0:
            sums = dot(windows, jnp.concatenate([f2_down[i] for i in range(3)], 1))
            sums = [sums[:, i * filters : (i + 1) * filters] for i in range(3)]
        else:
            sums = [dot(windows, f2_down[i]) for i in range(3)]
        for i in range(3):
            sum_two[pl.ds(at + 2 - i, half)] += sums[i].reshape(half, span, filters)

    arrive(1, rows - bands)
    forward(near_band)
    arrive(rows - bands, rows)
    def across(source, table, send_sem, recv_sem, step):
        return pltpu.make_async_remote_copy(
            src_ref=source,
            dst_ref=table.at[strip],
            send_sem=send_sem.at[step],
            recv_sem=recv_sem.at[strip],
            device_id=device_at(row, lax.rem(col + step, cols) * pairs + pair),
            device_id_type=MESH,
        )

    def onward(table, send_sem, recv_sem, column, step):
        slot = column * pairs + pair
        return pltpu.make_async_remote_copy(
            src_ref=table.at[slot],
            dst_ref=table.at[slot],
            send_sem=send_sem.at[column * pairs + step],
            recv_sem=recv_sem.at[slot],
            device_id=device_at(row, col * pairs + lax.rem(pair + step, pairs)),
            device_id_type=MESH,
        )

    def arrival(table, send_sem, recv_sem, slot):
        return pltpu.make_async_remote_copy(
            src_ref=table.at[slot],
            dst_ref=table.at[slot],
            send_sem=send_sem.at[0],
            recv_sem=recv_sem.at[slot],
            device_id=device_at(row, lax.rem(col + 1, cols) * pairs + pair),
            device_id_type=MESH,
        )

    def share(table, send_sem, on_sem, recv_sem):
        for step in range(1, cols):
            across(table.at[strip], table, send_sem, recv_sem, step).start()
        for step in range(1, pairs):
            onward(table, on_sem, recv_sem, col, step).start()

    def pass_on(table, send_sem, on_sem, recv_sem):
        for step in range(1, cols):
            column = lax.rem(col + step, cols)
            arrival(table, send_sem, recv_sem, column * pairs + pair).wait_recv()
            for other in range(1, pairs):
                onward(table, on_sem, recv_sem, column, other).start()

    def settle(table, send_sem, on_sem, recv_sem):
        for step in range(1, cols):
            across(table.at[strip], table, send_sem, recv_sem, step).wait_send()
        for step in range(cols):
            column = lax.rem(col + step, cols)
            for other in range(1, pairs):
                onward(table, on_sem, recv_sem, column, other).wait_send()
                slot = column * pairs + lax.rem(pair + other, pairs)
                arrival(table, send_sem, recv_sem, slot).wait_recv()

    forward(far_band)
    pool_sems = (p_send, p_on, p_recv)
    share(pool_all, *pool_sems)
    spots = height2 * span
    pre_two = sum_two[1 : height2 + 1].reshape(spots, filters)
    near = up[0:height2].reshape(spots, filters) * slope(pre_two)
    near3[0, 1 : height2 + 1] = pltpu.roll(near, spots - 1, 0).astype(BF).reshape(height2, span, filters)
    near3[1, 1 : height2 + 1] = near.astype(BF).reshape(height2, span, filters)
    near3[2, 1 : height2 + 1] = pltpu.roll(near, 1, 0).astype(BF).reshape(height2, span, filters)

    def backward(band_at):
        at = band_at * band2
        windows = [
            near3[j, pl.ds(at + 2 - i, half)].reshape(half * span, filters) for i in range(3) for j in range(3)
        ]
        if filters % 128 == 0:
            total = dot(jnp.concatenate(windows, 1), f2[...].reshape(9 * filters, quads))
        else:
            total = jnp.zeros((half * span, quads), F32)
            for t in range(9):
                total += dot(windows[t], f2[t])
        for d in range(half):
            blocks[band_at + d // band2, pl.ds(d % band2 * width2, width2)] = total[
                d * span + EDGE : d * span + EDGE + width2
            ].astype(BF)

    start, arrive, c_sent = post(
        rows, row, far_first(rows, row), row_device, lambda peer: blocks.at[peer], landed, c_send, c_recv
    )
    backward(far_band)
    start(1, bands + 1)
    backward(near_band)
    start(bands + 1, rows)
    landed[row] = blocks[row]
    for u in range(height2):
        near_all[strip, pl.ds(u * width2, width2)] = near[
            u * span + EDGE : u * span + EDGE + width2
        ].astype(BF)
    near_sems = (n_send, n_on, n_recv)
    share(near_all, *near_sems)
    arrive()
    parts = total_of(rows, landed)
    wide = {}
    for k in range(band2):
        for i in range(2):
            some = parts[k * width2 : (k + 1) * width2, i * 128 : (i + 1) * 128]
            other = pltpu.roll(some, 64, 1)
            wide[k, i] = jnp.concatenate(
                [jnp.where(low_half, some, other), jnp.where(low_half, other, some)], 1
            )

    for h in range(band):
        k, i = h // 4, (h // 2) % 2
        body = wide[k, i] * pre[h, mid]
        grad_f[h + 1, mid] = body
        grad_own[pl.ds(h * width2, width2)] = body.astype(BF)
        rims_f[0, pl.ds(h, 1)] = body[:1]
        rims_f[1, pl.ds(h, 1)] = body[width2 - 1 :]
        if h in (0, band - 1):
            rim_rows[h // (band - 1)] = body.astype(BF)

    low = iota((channels, 128), 1) < channels
    halves, ends = [], []
    own_spots = band * span
    windows = [inner[i : i + band].reshape(band * width2, 512) for i in range(3)]
    turned = grad_own[...].astype(F32).T.astype(BF)
    taps = dot(turned, jnp.concatenate([window[:, :quads] for window in windows], 1))
    outer = jnp.concatenate([turned[:channels], turned[3 * channels :]], 0)
    outer = dot(outer, jnp.concatenate([window[:, quads:] for window in windows], 1))

    def cut(i, p, k):
        if k < 2:
            return taps[p * channels : (p + 1) * channels, i * quads + k * 128 : i * quads + (k + 1) * 128]
        half = channels * (p // 3)
        return outer[half : half + channels, i * quads + (k - 2) * 128 : i * quads + (k - 1) * 128]

    for i in range(3):
        bc = pltpu.roll(cut(i, 0, 0) + cut(i, 2, 1), 64, 1)
        ab = cut(i, 1, 0) + cut(i, 3, 1)
        za = pltpu.roll(cut(i, 0, 2) + cut(i, 2, 0), 64, 1)
        cz = cut(i, 1, 1) + cut(i, 3, 3)
        halves.append(ab + jnp.where(low, za, bc))
        ends.append(cz + bc)
    short = channels // 2
    last = jnp.where(low[:short], ends[2][:short], pltpu.roll(ends[2][short:], 64, 1))
    packed = halves + [jnp.where(low, ends[0], pltpu.roll(ends[1], 64, 1)), last]
    packed = jnp.concatenate(packed, 0)
    owners, piece = mine_blocks.shape[:2]
    for o in range(owners):
        some = packed[o * piece : (o + 1) * piece]
        if some.shape[0] < piece:
            some = jnp.concatenate([some, jnp.zeros((piece - some.shape[0], 128), F32)], 0)
        mine_blocks[o] = some.astype(BF)

    me = row * strips + strip
    low_row = rows // 2 - 1

    def piece_of(r, s):
        return 2 * s + r - low_row

    def owns(r, s):
        return (r >= low_row) & (r <= low_row + 1) & (piece_of(r, s) < owners)

    my_piece = piece_of(row, strip)
    owning = owns(row, strip)

    def target(step):
        z, s = step // strips, step % strips
        return jnp.where(row < rows // 2, rows - 1 - z, z), lax.rem(col + cols - 1 - s // pairs, cols) * pairs + lax.rem(
            pair + pairs - 1 - s % pairs, pairs
        )

    def to_owner(step, arriving=False):
        r, s = target(step)
        other = r * strips + s
        return pltpu.make_async_remote_copy(
            src_ref=mine_blocks.at[my_piece if arriving else piece_of(r, s)],
            dst_ref=one_landed.at[other if arriving else me],
            send_sem=d1_send.at[step],
            recv_sem=d1_recv.at[other if arriving else me],
            device_id=device_at(r, s),
            device_id_type=MESH,
        )

    def from_owner(step, arriving=False):
        r, s = target(step)
        slot = piece_of(r, s) if arriving else my_piece
        return pltpu.make_async_remote_copy(
            src_ref=one_part,
            dst_ref=one_all.at[slot],
            send_sem=d2_send.at[step],
            recv_sem=d2_recv.at[slot],
            device_id=device_at(r, s),
            device_id_type=MESH,
        )

    def each_other(action):
        def one(step):
            r, s = target(step)

            @pl.when(r * strips + s != me)
            def _():
                action(step, owns(r, s))

        if everyone > 16:
            pl.loop(0, everyone)(one)
        else:
            for step in range(everyone):
                one(step)

    def send_out(step, owner):
        @pl.when(owner)
        def _():
            to_owner(step).start()

    def settle_out(step, owner):
        @pl.when(owner)
        def _():
            to_owner(step).wait_send()

        @pl.when(owning)
        def _():
            to_owner(step, True).wait_recv()

    def send_back(step, owner):
        @pl.when(owning)
        def _():
            from_owner(step).start()

    def settle_back(step, owner):
        @pl.when(owning)
        def _():
            from_owner(step).wait_send()

        @pl.when(owner)
        def _():
            from_owner(step, True).wait_recv()

    each_other(send_out)

    @pl.when(owning)
    def _():
        one_landed[me] = mine_blocks[my_piece]

    rims[...] = rims_f[...].astype(BF)
    for way in WAYS:
        start_border(rim_kind, way)

    each_other(settle_out)

    @pl.when(owning)
    def _():
        if everyone > 16:
            part = lax.fori_loop(
                1, everyone, lambda i, t: t + one_landed[i].astype(F32), one_landed[0].astype(F32)
            )
        else:
            part = total_of(everyone, one_landed)
        one_part[...] = part.astype(BF)
        one_all[my_piece] = part.astype(BF)

    each_other(send_back)
    pass_on(pool_all, *pool_sems)
    pass_on(near_all, *near_sems)

    settle(pool_all, *pool_sems)
    settle(near_all, *near_sems)
    near_map[0] = jnp.zeros(near_map.shape[1:], BF)
    near_map[height2 + 1] = jnp.zeros(near_map.shape[1:], BF)
    at_lane = iota((filters, full2), 1)

    def assemble(u):
        at = u * width2
        if not isinstance(u, int):
            at = pl.multiple_of(at, width2)
        line = [near_all[s, pl.ds(at, width2)].astype(F32) for s in range(strips)]
        line = jnp.concatenate(line, 0).T
        after = jnp.where(at_lane < full2 - 1, pltpu.roll(line, full2 - 1, 1), 0.0)
        before = jnp.where(at_lane > 0, pltpu.roll(line, 1, 1), 0.0)
        for j, value in enumerate((after, line, before)):
            near_map[u + 1, pl.ds(j * filters, filters)] = value.astype(BF)
        line = jnp.concatenate([pool_all[s, pl.ds(at, width2)] for s in range(strips)], 0)
        pool_map[u] = dot(line, reorder[1]).astype(BF)

    chunk = max(1, 1024 // full2)
    steps = height2 // chunk
    if steps == 1:
        for u in range(height2):
            assemble(u)
    else:
        pl.loop(0, height2)(assemble)

    def filter_taps(i, step):
        at = step * chunk
        left = jnp.concatenate([near_map[at + k + 2 - i] for k in range(chunk)], 1)
        right = pool_map[pl.ds(at, chunk)].reshape(chunk * full2, quads)
        return scale_two * dot(left, right).reshape(3, filters, quads)

    def filter_gradient(i):
        g2_out[3 * i : 3 * i + 3] = filter_taps(i, 0)
        if steps > 1:
            @pl.loop(1, steps)
            def _(step):
                g2_out[3 * i : 3 * i + 3] += filter_taps(i, step)

    for i in range(3):
        filter_gradient(i)

    for way in WAYS:
        end_border(rim_kind, way)
    for h in range(band):
        for side, at in ((0, EDGE - 1), (1, EDGE + width2)):
            grad_f[h + 1, pl.ds(at, 1)] = rim_side[side].astype(F32)[h : h + 1]
    for top, line, h in ((0, 0, band - 1), (1, band + 1, 0)):
        grad_f[line, mid] = rim_row[top].astype(F32)
        for side, at in ((0, EDGE - 1), (1, EDGE + width2)):
            grad_f[line, pl.ds(at, 1)] = rim_corner[2 * top + side].astype(F32)[h : h + 1]
    for line in range(band + 2):
        grad[line] = grad_f[line].astype(BF)
    cells = jnp.concatenate([grad[2 - i : 2 - i + band].reshape(own_spots, quads) for i in range(3)], 1)
    kernel = jnp.concatenate([w1[:, i * 512 : (i + 1) * 512] for i in range(3)], 0)
    total = dot(cells, kernel)
    before = pltpu.roll(total[:, quads : quads + 128], own_spots - 1, 0)
    after = pltpu.roll(total[:, quads + 128 :], 1, 0)
    sides = (total[:, :128] + after, total[:, 128:quads] + before)
    turned = []
    for h in range(band):
        lines_of = []
        for b in range(4):
            value = sides[b // 2][h * span + EDGE : h * span + EDGE + width2]
            lines_of.append(jnp.where(low_half == (b % 2 == 0), value, 0.0).astype(BF))
        turned.append(jnp.concatenate(lines_of, 0))
    turned = dot(jnp.concatenate(turned, 1), pick, BY_ROWS)
    for h in range(band):
        at = 2 * h * channels
        x_wide[pl.ds(h, channels, stride=band), :] = (
            turned[at : at + channels] + turned[at + channels : at + 2 * channels]
        )
    ig_out[...] = x_wide[...].astype(BF)

    b_sent()
    c_sent()
    for way in WAYS:
        sent_border(cell_kind, way)
        sent_border(rim_kind, way)
    for side in range(2):
        @pl.when(there((0, (-1, 1)[side])))
        def _(side=side):
            up_border(side).wait_send()
    each_other(settle_back)
    done = scale_one * one_all[...].astype(F32).reshape(owners * piece, 128)
    rolled = pltpu.roll(done, 64, 1)
    for i in range(3):
        for j in range(3):
            at = (i if j < 2 else 3 + i // 2) * channels
            if (i, j) == (2, 2):
                value = jnp.concatenate([done[at : at + short], rolled[at : at + short]], 0)
            else:
                value = (done if (j if j < 2 else i % 2) == 0 else rolled)[at : at + channels]
            g1_out[3 * i + j] = value[:, :channels]


def write_kernel(*refs):
    count = len(refs) // 2
    sources, targets, sem = refs[:count], refs[count:-1], refs[-1]
    copies = [pltpu.make_async_copy(sources[n], targets[n], sem.at[n]) for n in range(count)]
    for copy in copies:
        copy.start()
    for copy in copies:
        copy.wait()


def write_out(*arrays):
    arrays = [pltpu.with_memory_space_constraint(a, pltpu.VMEM) for a in arrays]
    return pl.pallas_call(
        write_kernel,
        out_shape=tuple(jax.ShapeDtypeStruct(a.shape, a.dtype) for a in arrays),
        in_specs=[VMEM] * len(arrays),
        out_specs=(HBM,) * len(arrays),
        scratch_shapes=[pltpu.SemaphoreType.DMA((len(arrays),))],
    )(*arrays)


def local(features_in, filters_one, filters_two, out_grad):
    channels, band, width = features_in.shape
    rows, strips = lax.axis_size("row"), lax.axis_size(STRIP)
    cols, pairs = lax.axis_size("col"), lax.axis_size("pair")
    filters = filters_two.shape[0]
    quads = 4 * channels
    height2 = out_grad.shape[2]
    width2, band2 = width // 4, band // 4
    span = width2 + 2 * EDGE
    full2 = width2 * strips
    spots = band2 * width2
    halves = 9 * channels // 2
    piece = -(-halves // (2 * strips) // 8) * 8
    owners = -(-halves // piece)

    def v(shape, kind=BF):
        return pltpu.VMEM(shape, kind)

    scratch = [
        v((channels * band, width)),
        v((9, channels, channels)),
        v((9, filters, quads)),
        v((width2 * height2, filters)),
        v((channels * band, width), F32),
        v((2 * channels * band, width)),
        v((band * width2, quads)),
        v((2, band * EDGE + 8, quads), F32),
        v((2, band * EDGE, quads)),
        v((2, band * EDGE, quads)),
        v((2, width2, quads)),
        v((4, 16, quads)),
        v((2, 2 * height2, filters)),
        v((band + 3, span, quads), F32),
        v((band + 2, span, 512)),
        v((band + 2, width2, 512)),
        v((quads, 3 * 512)),
        v((3 * 512, quads)),
        v((2, quads, quads)),
        v((3, 3 * quads, filters)),
        v((band + 1, span, quads), F32),
        v((band2 * (width2 + 4) + 8, quads), F32),
        v((band2 * (width2 + 4), quads)),
        v((rows, band2 * (width2 + 4), quads)),
        v((span * height2, filters), F32),
        v((height2 + 1, span, filters), F32),
        v((height2 + 1, span, quads), F32),
        v((height2, span, 3 * quads)),
        v((3, height2 + 2, span, filters)),
        v((height2 + 2, span, filters), F32),
        v((rows, spots, quads)),
        v((rows, spots, quads)),
        v((band + 3, span, quads), F32),
        v((band + 2, span, quads)),
        v((band * width2, quads)),
        v((2, 16, quads), F32),
        v((2, 16, quads)),
        v((2, width2, quads)),
        v((2, 16, quads)),
        v((2, width2, quads)),
        v((4, 16, quads)),
        v((strips, height2 * width2, quads)),
        v((strips, height2 * width2, filters)),
        v((height2, full2, quads)),
        v((height2 + 2, 3 * filters, full2)),
        v((owners, piece, 128)),
        v((rows * strips, piece, 128)),
        v((piece, 128)),
        v((owners, piece, 128)),
        pltpu.SemaphoreType.DMA((4,)),
    ]
    scratch += sems(len(WAYS) + 2) + sems(len(WAYS)) + sems(rows) + sems(rows) + sems(rows * strips) + sems(rows * strips)
    for _ in range(2):
        scratch += [
            pltpu.SemaphoreType.DMA((cols,)),
            pltpu.SemaphoreType.DMA((cols * pairs,)),
            pltpu.SemaphoreType.DMA((strips,)),
        ]
    arguments = (
        features_in.reshape(channels * band, width),
        jnp.transpose(filters_one, (1, 2, 0, 3)).reshape(9, channels, channels),
        jnp.transpose(filters_two, (1, 2, 0, 3)).reshape(9, filters, quads),
        jnp.transpose(out_grad, (1, 2, 0)).reshape(width2 * height2, filters),
    )
    arguments = [pltpu.with_memory_space_constraint(a, pltpu.HBM) for a in arguments]
    share = 1 if rows * strips <= 64 else 2
    scale_one = 1.0 / math.sqrt(band * rows * width * strips)
    scale_two = 1.0 / math.sqrt(height2 * full2)
    ig, g1, g2 = pl.pallas_call(
        functools.partial(whole_kernel, rows, strips, band, height2, scale_one, scale_two),
        out_shape=(
            jax.ShapeDtypeStruct((channels * band, width), BF),
            jax.ShapeDtypeStruct((9, channels, channels), F32),
            jax.ShapeDtypeStruct((9, filters, quads), F32),
        ),
        in_specs=[HBM] * 4,
        out_specs=(VMEM,) * 3,
        scratch_shapes=scratch,
        compiler_params=pltpu.CompilerParams(
            collective_id=0, has_side_effects=True, vmem_limit_bytes=share * 28 * 1024 * 1024
        ),
    )(*arguments)
    ig, g1, g2 = write_out(ig, g1, g2)
    grad_one = jnp.transpose(g1.reshape(3, 3, channels, channels), (2, 0, 1, 3))
    grad_two = jnp.transpose(g2.reshape(3, 3, filters, quads), (2, 0, 1, 3))
    return (ig.reshape(channels, band, width), grad_one, grad_two)


def solution(mesh):
    in_specs = (
        P("grp", "row", ("col", "pair")),
        P(),
        P("row", None, None, None),
        P(("grp", "row"), ("col", "pair"), None),
    )
    out_specs = (
        P("grp", "row", ("col", "pair")),
        P("grp", None, None, None),
        P(("grp", "row"), None, None, None),
    )
    return jax.shard_map(local, mesh=mesh, in_specs=in_specs, out_specs=out_specs, check_vma=False)
```

```python
import functools
import math

import jax
import jax.numpy as jnp
from jax import lax
from jax.experimental import pallas as pl
from jax.experimental.pallas import tpu as pltpu
from jax.sharding import PartitionSpec as P

MESH = pl.DeviceIdType.MESH
VMEM = pl.BlockSpec(memory_space=pltpu.VMEM)
HBM = pl.BlockSpec(memory_space=pltpu.HBM)
STRIP = ("col", "pair")
BF = jnp.bfloat16
F32 = jnp.float32

EDGE = 4

DIAGONALS = [(a, b) for a in (-1, 1) for b in (-1, 1)]
WAYS = [(0, -1), (0, 1), (-1, 0), (1, 0)] + DIAGONALS

BY_LANES = (((1,), (1,)), ((), ()))
BY_ROWS = (((0,), (0,)), ((), ()))


def place():
    return lax.axis_index("row"), lax.axis_index(STRIP)


def device_at(row, strip):
    pairs = lax.axis_size("pair")
    return (lax.axis_index("grp"), row, lax.div(strip, pairs), lax.rem(strip, pairs))


def sems(count):
    return [pltpu.SemaphoreType.DMA((count,)), pltpu.SemaphoreType.DMA((count,))]


def around(count, me):
    return lambda step: lax.rem(me + step, count)


def far_first(count, me):
    def peer(step):
        up = step - 1
        up += jnp.where(up >= me, 1, 0)
        down = count - step
        down -= jnp.where(down <= me, 1, 0)
        return jnp.where(me < count // 2, down, up)

    return peer


def near_first(count, me):
    return lambda step: far_first(count, me)(count - step)


def post(count, me, order, device_of, source, landing, send_sem, recv_sem):
    def copy_of(step, slot):
        peer = order(step)
        return pltpu.make_async_remote_copy(
            src_ref=source(peer),
            dst_ref=landing.at[slot(peer)],
            send_sem=send_sem.at[step],
            recv_sem=recv_sem.at[slot(peer)],
            device_id=device_of(peer),
            device_id_type=MESH,
        )

    def start(low=1, high=count):
        @pl.loop(low, high)
        def _(step):
            copy_of(step, lambda peer: me).start()

    def arrive(low=1, high=count):
        @pl.loop(low, high)
        def _(step):
            copy_of(step, lambda peer: peer).wait_recv()

    def sent():
        @pl.loop(1, count)
        def _(step):
            copy_of(step, lambda peer: me).wait_send()

    return start, arrive, sent


def iota(shape, dim):
    return lax.broadcasted_iota(jnp.int32, shape, dim)


def dot(a, b, numbers=(((1,), (0,)), ((), ()))):
    return lax.dot_general(a, b, numbers, preferred_element_type=F32)


def slope(values):
    s = 1.0 / (1.0 + jnp.exp(-values))
    return s * (1.0 + values * (1.0 - s))


def total_of(count, landing):
    value = landing[0].astype(F32)
    for i in range(1, count):
        value += landing[i].astype(F32)
    return value


def whole_kernel(
    rows, strips, band, height2, scale_one, scale_two,
    x_any, f1_any, f2_any, up_any,
    ig_out, g1_out, g2_out,
    x_in, f1, f2, up_in, x_wide, x_turned, own, edges_f, edges, from_side, from_row, from_corner, from_up,
    tile, patches, inner, w1, w1_down, reorder, f2_down, pre, block_f, block, gathered, up_wide, up, pool_f, pool3, near3, sum_two,
    blocks, landed, grad_f, grad, grad_own, rims_f, rims, rim_rows, rim_side, rim_row, rim_corner, pool_all, near_all, pool_map, near_map,
    mine_blocks, one_landed, one_part, one_all,
    load_sem, a_send, a_recv, e_send, e_recv, b_send, b_recv, c_send, c_recv,
    d1_send, d1_recv, d2_send, d2_recv,
    p_send, p_on, p_recv, n_send, n_on, n_recv,
):
    row, strip = place()
    cols, pairs = lax.axis_size("col"), lax.axis_size("pair")
    col, pair = lax.axis_index("col"), lax.axis_index("pair")
    channels = f1.shape[1]
    filters = f2.shape[1]
    quads = 4 * channels
    width = x_in.shape[1]
    width2 = width // 4
    band2 = band // 4
    span = width2 + 2 * EDGE
    full2 = width2 * strips
    mid = pl.ds(EDGE, width2)
    reach = width2 + 4

    def row_device(i):
        return device_at(i, strip)

    def strip_device(i):
        return device_at(row, i)

    def there(way):
        a, b = row + way[0], strip + way[1]
        return (a >= 0) & (a < rows) & (b >= 0) & (b < strips)

    barrier = pltpu.get_barrier_semaphore()
    everyone = rows * strips
    for step in range(1, rows):
        pl.semaphore_signal(barrier, inc=1, device_id=row_device(lax.rem(row + step, rows)), device_id_type=MESH)
    for step in range(1, strips):
        pl.semaphore_signal(
            barrier, inc=1, device_id=strip_device(lax.rem(strip + step, strips)), device_id_type=MESH
        )
    for way in DIAGONALS:
        @pl.when(there(way))
        def _(way=way):
            pl.semaphore_signal(
                barrier, inc=1, device_id=device_at(row + way[0], strip + way[1]), device_id_type=MESH
            )
    loads = [
        pltpu.make_async_copy(source, target, load_sem.at[n])
        for n, (source, target) in enumerate([(x_any, x_in), (up_any, up_in), (f1_any, f1), (f2_any, f2)])
    ]
    for load in loads[:3]:
        load.start()

    shape = (width, width)
    pick = (iota(shape, 1) == 4 * (iota(shape, 0) % width2) + iota(shape, 0) // width2).astype(BF)
    low_half = iota((width2, 128), 1) < channels
    shape = (quads, quads)
    for k in range(2):
        inside, outside = iota(shape, 1 - k), iota(shape, k)
        home = 4 * (inside % channels) + 2 * (inside // (2 * channels)) + inside // channels % 2
        reorder[k] = (outside == home).astype(BF)
    grad_f[...] = jnp.zeros(grad_f.shape, F32)
    rims_f[...] = jnp.zeros(rims_f.shape, F32)
    sum_two[...] = jnp.zeros(sum_two.shape, F32)
    for line in (0, band + 1):
        patches[line] = jnp.zeros(patches.shape[1:], BF)
    for u in range(height2):
        pool_f[u, pl.ds(0, 2)] = jnp.zeros((2, quads), F32)
        pool_f[u, pl.ds(2 + reach, 2)] = jnp.zeros((2, quads), F32)
    for j in range(3):
        near3[j, 0] = jnp.zeros(near3.shape[2:], BF)
        near3[j, height2 + 1] = jnp.zeros(near3.shape[2:], BF)
    loads[0].wait()
    loads[3].start()
    x_wide[...] = x_in[...].astype(F32)
    for h in range(band):
        line = x_wide[pl.ds(h, channels, stride=band), :].astype(BF)
        x_turned[pl.ds(2 * h * channels, channels), :] = line
        x_turned[pl.ds((2 * h + 1) * channels, channels), :] = line
    turned = dot(pick, x_turned[...], BY_LANES)
    for h in range(band):
        lanes = slice(h * 128, (h + 1) * 128)
        for half in range(2):
            even = turned[2 * half * width2 : (2 * half + 1) * width2, lanes]
            odd = turned[(2 * half + 1) * width2 : (2 * half + 2) * width2, lanes]
            value = jnp.where(low_half, even, odd)
            tile[h + 1, mid, pl.ds(half * 128, 128)] = value
            own[pl.ds(h * width2, width2), pl.ds(half * 128, 128)] = value.astype(BF)
    for h in range(band):
        edges_f[0, pl.ds(h * EDGE, EDGE)] = tile[h + 1, pl.ds(EDGE, EDGE)]
        edges_f[1, pl.ds(h * EDGE, EDGE)] = tile[h + 1, pl.ds(width2, EDGE)]
    edges[...] = edges_f[:, : band * EDGE].astype(BF)

    diagonals = (jnp.where(row > 0, 1, 0) + jnp.where(row < rows - 1, 1, 0)) * (
        jnp.where(strip > 0, 1, 0) + jnp.where(strip < strips - 1, 1, 0)
    )
    pl.semaphore_wait(barrier, rows - 1 + strips - 1 + diagonals)
    edge_rows = band * EDGE
    up_edge = 2 * height2

    def corner_of(way):
        return (way[1] + 1) // 2, (way[0] + 1) // 2

    def border(kind, way, arriving=False):
        (source_of, slot_of, send_sem, recv_sem), back = kind, (-way[0], -way[1])
        land = way if arriving else back
        return pltpu.make_async_remote_copy(
            src_ref=source_of(way),
            dst_ref=slot_of(land),
            send_sem=send_sem.at[WAYS.index(way)],
            recv_sem=recv_sem.at[WAYS.index(land)],
            device_id=device_at(row + way[0], strip + way[1]),
            device_id_type=MESH,
        )

    def start_border(kind, way):
        @pl.when(there(way))
        def _():
            border(kind, way).start()

    def clear_border(kind, way):
        @pl.when(jnp.logical_not(there(way)))
        def _():
            slot = kind[1](way)
            slot[...] = jnp.zeros(slot.shape, slot.dtype)

    def end_border(kind, way):
        @pl.when(there(way))
        def _():
            border(kind, way, True).wait_recv()

    def sent_border(kind, way):
        @pl.when(there(way))
        def _():
            border(kind, way).wait_send()

    def slots(side_slots, row_slots, corner_slots):
        def slot_of(way):
            side, top = corner_of(way)
            if way[0] == 0:
                return side_slots.at[side]
            if way[1] == 0:
                return row_slots.at[top]
            return corner_slots.at[2 * top + side]

        return slot_of

    def cell_source(way):
        side = corner_of(way)[0]
        if way[0] == 0:
            return edges.at[side]
        if way[1] == 0:
            return own.at[pl.ds(0 if way[0] < 0 else (band - 1) * width2, width2)]
        return edges.at[side, pl.ds(0 if way[0] < 0 else edge_rows - 16, 16)]

    def rim_source(way):
        side, top = corner_of(way)
        return rim_rows.at[top] if way[1] == 0 else rims.at[side]

    cell_kind = (cell_source, slots(from_side, from_row, from_corner), a_send, a_recv)
    rim_kind = (rim_source, slots(rim_side, rim_row, rim_corner), e_send, e_recv)

    def up_border(side, arriving=False):
        land = side if arriving else 1 - side
        return pltpu.make_async_remote_copy(
            src_ref=up_in.at[pl.ds(0 if side == 0 else up_in.shape[0] - up_edge, up_edge)],
            dst_ref=from_up.at[land],
            send_sem=a_send.at[len(WAYS) + side],
            recv_sem=a_recv.at[len(WAYS) + land],
            device_id=device_at(row, strip + (-1, 1)[side]),
            device_id_type=MESH,
        )

    for way in WAYS[2:] + WAYS[:2]:
        start_border(cell_kind, way)
    for way in WAYS:
        clear_border(cell_kind, way)
        clear_border(rim_kind, way)
    loads[1].wait()
    for side in range(2):
        @pl.when(there((0, (-1, 1)[side])))
        def _(side=side):
            up_border(side).start()

        @pl.when(jnp.logical_not(there((0, (-1, 1)[side]))))
        def _(side=side):
            from_up[side] = jnp.zeros(from_up.shape[1:], BF)

    loads[2].wait()
    zero = jnp.zeros((channels, channels), F32)
    nothing = jnp.zeros((channels, 128), BF)
    for i in range(3):
        a, b, c = [f1[3 * i + j].astype(F32) for j in range(3)]
        bc, ab, za, cz = [
            jnp.concatenate(two, 1).astype(BF) for two in ((b, c), (a, b), (zero, a), (c, zero))
        ]
        table = (
            (bc, nothing, za, nothing),
            (ab, cz, nothing, nothing),
            (za, bc, nothing, nothing),
            (nothing, ab, nothing, cz),
        )
        for p in range(4):
            for k in range(4):
                w1[pl.ds(p * channels, channels), pl.ds(i * 512 + k * 128, 128)] = table[p][k]
    for k in range(12):
        w1_down[pl.ds(k * 128, 128)] = w1[:, pl.ds(k * 128, 128)].astype(F32).T.astype(BF)

    def widen(line):
        here = tile[line]
        patches[line, :, pl.ds(0, quads)] = here.astype(BF)
        patches[line, :, pl.ds(quads, 128)] = pltpu.roll(here[:, quads - 128 :], 1, 0).astype(BF)
        patches[line, :, pl.ds(quads + 128, 128)] = pltpu.roll(here[:, :128], span - 1, 0).astype(BF)

    def silu(values):
        return values / (1.0 + jnp.exp(-values))

    def pool(h):
        total = (silu(pre[h]) + silu(pre[h + 1])) * 0.25
        left, right = total[:, :128], total[:, 128:]
        left += pltpu.roll(left, 64, 1)
        right += pltpu.roll(right, 64, 1)
        return jnp.where(iota((span, 128), 1) < channels, left, right)

    side_at = [pl.ds(0, EDGE), pl.ds(EDGE + width2, EDGE)]
    for way in WAYS[:2]:
        end_border(cell_kind, way)
    for side in range(2):
        edge = from_side[side].astype(F32)
        for h in range(band):
            tile[h + 1, side_at[side]] = edge[h * EDGE : (h + 1) * EDGE]
    for line in range(1, band + 1):
        widen(line)
    windows = jnp.concatenate([patches[i : i + band].reshape(band * span, 512) for i in range(3)], 1)
    pre[0:band] = dot(windows, w1_down[...]).reshape(band, span, quads)
    halves = {h: pool(h) for h in range(2, band - 2, 2)}

    for way in WAYS[2:]:
        end_border(cell_kind, way)
    for top in range(2):
        line = 0 if top == 0 else band + 1
        tile[line, mid] = from_row[top].astype(F32)
        for side in range(2):
            corner = from_corner[2 * top + side].astype(F32)
            tile[line, side_at[side]] = corner[16 - EDGE :] if top == 0 else corner[:EDGE]
        widen(line)
    pre[0] += dot(patches[0], w1_down[pl.ds(0, 512)])
    pre[band - 1] += dot(patches[band + 1], w1_down[pl.ds(1024, 512)])
    for h in (0, band - 2):
        halves[h] = pool(h)
    pooled = [jnp.concatenate([halves[4 * u], halves[4 * u + 2]], 1) for u in range(band2)]
    pooled = jnp.concatenate(pooled, 0)
    at_col = strip * width2 - EDGE + iota((band2 * span, quads), 0) % span
    pooled = jnp.where((at_col >= 0) & (at_col < full2), pooled, 0.0)
    for u in range(band2):
        block_f[pl.ds(u * reach, reach)] = pooled[u * span + 2 : u * span + 2 + reach]
    pooled = block_f[: band2 * reach].astype(BF)
    block[...] = pooled
    start, arrive, b_sent = post(
        rows, row, near_first(rows, row), row_device, lambda peer: block, gathered, b_send, b_recv
    )
    start()
    gathered[row] = pooled

    for h in range(band):
        pre[h] = slope(pre[h]) * 0.25
    for line in range(band + 2):
        inner[line, :, pl.ds(0, quads)] = tile[line, mid].astype(BF)
        inner[line, :, pl.ds(quads, 128)] = tile[line, pl.ds(EDGE - 1, width2), pl.ds(quads - 128, 128)].astype(BF)
        inner[line, :, pl.ds(quads + 128, 128)] = tile[line, pl.ds(EDGE + 1, width2), pl.ds(0, 128)].astype(BF)
    for side in range(2):
        @pl.when(there((0, (-1, 1)[side])))
        def _(side=side):
            up_border(side, True).wait_recv()
    up_wide[pl.ds(0, up_edge)] = from_up[0].astype(F32)
    up_wide[pl.ds(up_edge, width2 * height2)] = up_in[...].astype(F32)
    up_wide[pl.ds(up_edge + width2 * height2, up_edge)] = from_up[1].astype(F32)
    for u in range(height2):
        up[u, pl.ds(0, 2)] = jnp.zeros((2, filters), F32)
        up[u, pl.ds(2, width2 + 4)] = up_wide[pl.ds(u, width2 + 4, stride=height2), :]
        up[u, pl.ds(width2 + 6, 2)] = jnp.zeros((2, filters), F32)
    loads[3].wait()
    f2[...] = dot(f2[...].reshape(9 * filters, quads), reorder[0]).astype(BF).reshape(9, filters, quads)
    for t in range(9):
        f2_down[t // 3, pl.ds(t % 3 * quads, quads)] = f2[t].astype(F32).T.astype(BF)

    half, bands = height2 // 2, rows // 2
    near_band = jnp.where(row < bands, 0, bands)
    far_band = bands - near_band

    def forward(band_at):
        at = band_at * band2
        for d in range(half):
            k = d % band2
            pool_f[at + d, pl.ds(2, reach)] = gathered[band_at + d // band2].astype(F32)[
                k * reach : (k + 1) * reach
            ]
            wide = pool_f[at + d]
            pool3[at + d, :, pl.ds(0, quads)] = pltpu.roll(wide, 1, 0).astype(BF)
            pool3[at + d, :, pl.ds(quads, quads)] = wide.astype(BF)
            pool3[at + d, :, pl.ds(2 * quads, quads)] = pltpu.roll(wide, span - 1, 0).astype(BF)
            spot = pl.multiple_of((at + d) * width2, width2)
            pool_all[strip, pl.ds(spot, width2)] = wide[EDGE : EDGE + width2].astype(BF)
        windows = pool3[pl.ds(at, half)].reshape(half * span, 3 * quads)
        if filters % 128 == 0:
            sums = dot(windows, jnp.concatenate([f2_down[i] for i in range(3)], 1))
            sums = [sums[:, i * filters : (i + 1) * filters] for i in range(3)]
        else:
            sums = [dot(windows, f2_down[i]) for i in range(3)]
        for i in range(3):
            sum_two[pl.ds(at + 2 - i, half)] += sums[i].reshape(half, span, filters)

    arrive(1, rows - bands)
    forward(near_band)
    arrive(rows - bands, rows)
    def across(source, table, send_sem, recv_sem, step):
        return pltpu.make_async_remote_copy(
            src_ref=source,
            dst_ref=table.at[strip],
            send_sem=send_sem.at[step],
            recv_sem=recv_sem.at[strip],
            device_id=device_at(row, lax.rem(col + step, cols) * pairs + pair),
            device_id_type=MESH,
        )

    def onward(table, send_sem, recv_sem, column, step):
        slot = column * pairs + pair
        return pltpu.make_async_remote_copy(
            src_ref=table.at[slot],
            dst_ref=table.at[slot],
            send_sem=send_sem.at[column * pairs + step],
            recv_sem=recv_sem.at[slot],
            device_id=device_at(row, col * pairs + lax.rem(pair + step, pairs)),
            device_id_type=MESH,
        )

    def arrival(table, send_sem, recv_sem, slot):
        return pltpu.make_async_remote_copy(
            src_ref=table.at[slot],
            dst_ref=table.at[slot],
            send_sem=send_sem.at[0],
            recv_sem=recv_sem.at[slot],
            device_id=device_at(row, lax.rem(col + 1, cols) * pairs + pair),
            device_id_type=MESH,
        )

    def share(table, send_sem, on_sem, recv_sem):
        for step in range(1, cols):
            across(table.at[strip], table, send_sem, recv_sem, step).start()
        for step in range(1, pairs):
            onward(table, on_sem, recv_sem, col, step).start()

    def pass_on(table, send_sem, on_sem, recv_sem):
        for step in range(1, cols):
            column = lax.rem(col + step, cols)
            arrival(table, send_sem, recv_sem, column * pairs + pair).wait_recv()
            for other in range(1, pairs):
                onward(table, on_sem, recv_sem, column, other).start()

    def settle(table, send_sem, on_sem, recv_sem):
        for step in range(1, cols):
            across(table.at[strip], table, send_sem, recv_sem, step).wait_send()
        for step in range(cols):
            column = lax.rem(col + step, cols)
            for other in range(1, pairs):
                onward(table, on_sem, recv_sem, column, other).wait_send()
                slot = column * pairs + lax.rem(pair + other, pairs)
                arrival(table, send_sem, recv_sem, slot).wait_recv()

    forward(far_band)
    pool_sems = (p_send, p_on, p_recv)
    share(pool_all, *pool_sems)
    spots = height2 * span
    pre_two = sum_two[1 : height2 + 1].reshape(spots, filters)
    near = up[0:height2].reshape(spots, filters) * slope(pre_two)
    near3[0, 1 : height2 + 1] = pltpu.roll(near, spots - 1, 0).astype(BF).reshape(height2, span, filters)
    near3[1, 1 : height2 + 1] = near.astype(BF).reshape(height2, span, filters)
    near3[2, 1 : height2 + 1] = pltpu.roll(near, 1, 0).astype(BF).reshape(height2, span, filters)

    def backward(band_at):
        at = band_at * band2
        windows = [
            near3[j, pl.ds(at + 2 - i, half)].reshape(half * span, filters) for i in range(3) for j in range(3)
        ]
        if filters % 128 == 0:
            total = dot(jnp.concatenate(windows, 1), f2[...].reshape(9 * filters, quads))
        else:
            total = jnp.zeros((half * span, quads), F32)
            for t in range(9):
                total += dot(windows[t], f2[t])
        for d in range(half):
            blocks[band_at + d // band2, pl.ds(d % band2 * width2, width2)] = total[
                d * span + EDGE : d * span + EDGE + width2
            ].astype(BF)

    start, arrive, c_sent = post(
        rows, row, far_first(rows, row), row_device, lambda peer: blocks.at[peer], landed, c_send, c_recv
    )
    backward(far_band)
    start(1, bands + 1)
    backward(near_band)
    start(bands + 1, rows)
    landed[row] = blocks[row]
    for u in range(height2):
        near_all[strip, pl.ds(u * width2, width2)] = near[
            u * span + EDGE : u * span + EDGE + width2
        ].astype(BF)
    near_sems = (n_send, n_on, n_recv)
    share(near_all, *near_sems)
    arrive()
    parts = total_of(rows, landed)
    wide = {}
    for k in range(band2):
        for i in range(2):
            some = parts[k * width2 : (k + 1) * width2, i * 128 : (i + 1) * 128]
            other = pltpu.roll(some, 64, 1)
            wide[k, i] = jnp.concatenate(
                [jnp.where(low_half, some, other), jnp.where(low_half, other, some)], 1
            )

    for h in range(band):
        k, i = h // 4, (h // 2) % 2
        body = wide[k, i] * pre[h, mid]
        grad_f[h + 1, mid] = body
        grad_own[pl.ds(h * width2, width2)] = body.astype(BF)
        rims_f[0, pl.ds(h, 1)] = body[:1]
        rims_f[1, pl.ds(h, 1)] = body[width2 - 1 :]
        if h in (0, band - 1):
            rim_rows[h // (band - 1)] = body.astype(BF)

    low = iota((channels, 128), 1) < channels
    halves, ends = [], []
    own_spots = band * span
    windows = [inner[i : i + band].reshape(band * width2, 512) for i in range(3)]
    turned = grad_own[...].astype(F32).T.astype(BF)
    taps = dot(turned, jnp.concatenate([window[:, :quads] for window in windows], 1))
    outer = jnp.concatenate([turned[:channels], turned[3 * channels :]], 0)
    outer = dot(outer, jnp.concatenate([window[:, quads:] for window in windows], 1))

    def cut(i, p, k):
        if k < 2:
            return taps[p * channels : (p + 1) * channels, i * quads + k * 128 : i * quads + (k + 1) * 128]
        half = channels * (p // 3)
        return outer[half : half + channels, i * quads + (k - 2) * 128 : i * quads + (k - 1) * 128]

    for i in range(3):
        bc = pltpu.roll(cut(i, 0, 0) + cut(i, 2, 1), 64, 1)
        ab = cut(i, 1, 0) + cut(i, 3, 1)
        za = pltpu.roll(cut(i, 0, 2) + cut(i, 2, 0), 64, 1)
        cz = cut(i, 1, 1) + cut(i, 3, 3)
        halves.append(ab + jnp.where(low, za, bc))
        ends.append(cz + bc)
    short = channels // 2
    last = jnp.where(low[:short], ends[2][:short], pltpu.roll(ends[2][short:], 64, 1))
    packed = halves + [jnp.where(low, ends[0], pltpu.roll(ends[1], 64, 1)), last]
    packed = jnp.concatenate(packed, 0)
    owners, piece = mine_blocks.shape[:2]
    for o in range(owners):
        some = packed[o * piece : (o + 1) * piece]
        if some.shape[0] < piece:
            some = jnp.concatenate([some, jnp.zeros((piece - some.shape[0], 128), F32)], 0)
        mine_blocks[o] = some.astype(BF)

    me = row * strips + strip
    low_row = rows // 2 - 1

    def piece_of(r, s):
        return 2 * s + r - low_row

    def owns(r, s):
        return (r >= low_row) & (r <= low_row + 1) & (piece_of(r, s) < owners)

    my_piece = piece_of(row, strip)
    owning = owns(row, strip)

    def target(step):
        z, s = step // strips, step % strips
        return jnp.where(row < rows // 2, rows - 1 - z, z), lax.rem(col + cols - 1 - s // pairs, cols) * pairs + lax.rem(
            pair + pairs - 1 - s % pairs, pairs
        )

    def to_owner(step, arriving=False):
        r, s = target(step)
        other = r * strips + s
        return pltpu.make_async_remote_copy(
            src_ref=mine_blocks.at[my_piece if arriving else piece_of(r, s)],
            dst_ref=one_landed.at[other if arriving else me],
            send_sem=d1_send.at[step],
            recv_sem=d1_recv.at[other if arriving else me],
            device_id=device_at(r, s),
            device_id_type=MESH,
        )

    def from_owner(step, arriving=False):
        r, s = target(step)
        slot = piece_of(r, s) if arriving else my_piece
        return pltpu.make_async_remote_copy(
            src_ref=one_part,
            dst_ref=one_all.at[slot],
            send_sem=d2_send.at[step],
            recv_sem=d2_recv.at[slot],
            device_id=device_at(r, s),
            device_id_type=MESH,
        )

    def each_other(action):
        def one(step):
            r, s = target(step)

            @pl.when(r * strips + s != me)
            def _():
                action(step, owns(r, s))

        if everyone > 16:
            pl.loop(0, everyone)(one)
        else:
            for step in range(everyone):
                one(step)

    def send_out(step, owner):
        @pl.when(owner)
        def _():
            to_owner(step).start()

    def settle_out(step, owner):
        @pl.when(owner)
        def _():
            to_owner(step).wait_send()

        @pl.when(owning)
        def _():
            to_owner(step, True).wait_recv()

    def send_back(step, owner):
        @pl.when(owning)
        def _():
            from_owner(step).start()

    def settle_back(step, owner):
        @pl.when(owning)
        def _():
            from_owner(step).wait_send()

        @pl.when(owner)
        def _():
            from_owner(step, True).wait_recv()

    each_other(send_out)

    @pl.when(owning)
    def _():
        one_landed[me] = mine_blocks[my_piece]

    rims[...] = rims_f[...].astype(BF)
    for way in WAYS:
        start_border(rim_kind, way)

    pass_on(pool_all, *pool_sems)
    pass_on(near_all, *near_sems)
    each_other(settle_out)

    @pl.when(owning)
    def _():
        if everyone > 16:
            part = lax.fori_loop(
                1, everyone, lambda i, t: t + one_landed[i].astype(F32), one_landed[0].astype(F32)
            )
        else:
            part = total_of(everyone, one_landed)
        one_part[...] = part.astype(BF)
        one_all[my_piece] = part.astype(BF)

    each_other(send_back)

    settle(pool_all, *pool_sems)
    settle(near_all, *near_sems)
    near_map[0] = jnp.zeros(near_map.shape[1:], BF)
    near_map[height2 + 1] = jnp.zeros(near_map.shape[1:], BF)
    at_lane = iota((filters, full2), 1)

    def assemble(u):
        at = u * width2
        if not isinstance(u, int):
            at = pl.multiple_of(at, width2)
        line = [near_all[s, pl.ds(at, width2)].astype(F32) for s in range(strips)]
        line = jnp.concatenate(line, 0).T
        after = jnp.where(at_lane < full2 - 1, pltpu.roll(line, full2 - 1, 1), 0.0)
        before = jnp.where(at_lane > 0, pltpu.roll(line, 1, 1), 0.0)
        for j, value in enumerate((after, line, before)):
            near_map[u + 1, pl.ds(j * filters, filters)] = value.astype(BF)
        line = jnp.concatenate([pool_all[s, pl.ds(at, width2)] for s in range(strips)], 0)
        pool_map[u] = dot(line, reorder[1]).astype(BF)

    chunk = max(1, 1024 // full2)
    steps = height2 // chunk
    if steps == 1:
        for u in range(height2):
            assemble(u)
    else:
        pl.loop(0, height2)(assemble)

    def filter_taps(i, step):
        at = step * chunk
        left = jnp.concatenate([near_map[at + k + 2 - i] for k in range(chunk)], 1)
        right = pool_map[pl.ds(at, chunk)].reshape(chunk * full2, quads)
        return scale_two * dot(left, right).reshape(3, filters, quads)

    def filter_gradient(i):
        g2_out[3 * i : 3 * i + 3] = filter_taps(i, 0)
        if steps > 1:
            @pl.loop(1, steps)
            def _(step):
                g2_out[3 * i : 3 * i + 3] += filter_taps(i, step)

    for i in range(3):
        filter_gradient(i)

    for way in WAYS:
        end_border(rim_kind, way)
    for h in range(band):
        for side, at in ((0, EDGE - 1), (1, EDGE + width2)):
            grad_f[h + 1, pl.ds(at, 1)] = rim_side[side].astype(F32)[h : h + 1]
    for top, line, h in ((0, 0, band - 1), (1, band + 1, 0)):
        grad_f[line, mid] = rim_row[top].astype(F32)
        for side, at in ((0, EDGE - 1), (1, EDGE + width2)):
            grad_f[line, pl.ds(at, 1)] = rim_corner[2 * top + side].astype(F32)[h : h + 1]
    for line in range(band + 2):
        grad[line] = grad_f[line].astype(BF)
    cells = jnp.concatenate([grad[2 - i : 2 - i + band].reshape(own_spots, quads) for i in range(3)], 1)
    kernel = jnp.concatenate([w1[:, i * 512 : (i + 1) * 512] for i in range(3)], 0)
    total = dot(cells, kernel)
    before = pltpu.roll(total[:, quads : quads + 128], own_spots - 1, 0)
    after = pltpu.roll(total[:, quads + 128 :], 1, 0)
    sides = (total[:, :128] + after, total[:, 128:quads] + before)
    turned = []
    for h in range(band):
        lines_of = []
        for b in range(4):
            value = sides[b // 2][h * span + EDGE : h * span + EDGE + width2]
            lines_of.append(jnp.where(low_half == (b % 2 == 0), value, 0.0).astype(BF))
        turned.append(jnp.concatenate(lines_of, 0))
    turned = dot(jnp.concatenate(turned, 1), pick, BY_ROWS)
    for h in range(band):
        at = 2 * h * channels
        x_wide[pl.ds(h, channels, stride=band), :] = (
            turned[at : at + channels] + turned[at + channels : at + 2 * channels]
        )
    ig_out[...] = x_wide[...].astype(BF)

    b_sent()
    c_sent()
    for way in WAYS:
        sent_border(cell_kind, way)
        sent_border(rim_kind, way)
    for side in range(2):
        @pl.when(there((0, (-1, 1)[side])))
        def _(side=side):
            up_border(side).wait_send()
    each_other(settle_back)
    done = scale_one * one_all[...].astype(F32).reshape(owners * piece, 128)
    rolled = pltpu.roll(done, 64, 1)
    for i in range(3):
        for j in range(3):
            at = (i if j < 2 else 3 + i // 2) * channels
            if (i, j) == (2, 2):
                value = jnp.concatenate([done[at : at + short], rolled[at : at + short]], 0)
            else:
                value = (done if (j if j < 2 else i % 2) == 0 else rolled)[at : at + channels]
            g1_out[3 * i + j] = value[:, :channels]


def write_kernel(*refs):
    count = len(refs) // 2
    sources, targets, sem = refs[:count], refs[count:-1], refs[-1]
    copies = [pltpu.make_async_copy(sources[n], targets[n], sem.at[n]) for n in range(count)]
    for copy in copies:
        copy.start()
    for copy in copies:
        copy.wait()


def write_out(*arrays):
    arrays = [pltpu.with_memory_space_constraint(a, pltpu.VMEM) for a in arrays]
    return pl.pallas_call(
        write_kernel,
        out_shape=tuple(jax.ShapeDtypeStruct(a.shape, a.dtype) for a in arrays),
        in_specs=[VMEM] * len(arrays),
        out_specs=(HBM,) * len(arrays),
        scratch_shapes=[pltpu.SemaphoreType.DMA((len(arrays),))],
    )(*arrays)


def local(features_in, filters_one, filters_two, out_grad):
    channels, band, width = features_in.shape
    rows, strips = lax.axis_size("row"), lax.axis_size(STRIP)
    cols, pairs = lax.axis_size("col"), lax.axis_size("pair")
    filters = filters_two.shape[0]
    quads = 4 * channels
    height2 = out_grad.shape[2]
    width2, band2 = width // 4, band // 4
    span = width2 + 2 * EDGE
    full2 = width2 * strips
    spots = band2 * width2
    halves = 9 * channels // 2
    piece = -(-halves // (2 * strips) // 8) * 8
    owners = -(-halves // piece)

    def v(shape, kind=BF):
        return pltpu.VMEM(shape, kind)

    scratch = [
        v((channels * band, width)),
        v((9, channels, channels)),
        v((9, filters, quads)),
        v((width2 * height2, filters)),
        v((channels * band, width), F32),
        v((2 * channels * band, width)),
        v((band * width2, quads)),
        v((2, band * EDGE + 8, quads), F32),
        v((2, band * EDGE, quads)),
        v((2, band * EDGE, quads)),
        v((2, width2, quads)),
        v((4, 16, quads)),
        v((2, 2 * height2, filters)),
        v((band + 3, span, quads), F32),
        v((band + 2, span, 512)),
        v((band + 2, width2, 512)),
        v((quads, 3 * 512)),
        v((3 * 512, quads)),
        v((2, quads, quads)),
        v((3, 3 * quads, filters)),
        v((band + 1, span, quads), F32),
        v((band2 * (width2 + 4) + 8, quads), F32),
        v((band2 * (width2 + 4), quads)),
        v((rows, band2 * (width2 + 4), quads)),
        v((span * height2, filters), F32),
        v((height2 + 1, span, filters), F32),
        v((height2 + 1, span, quads), F32),
        v((height2, span, 3 * quads)),
        v((3, height2 + 2, span, filters)),
        v((height2 + 2, span, filters), F32),
        v((rows, spots, quads)),
        v((rows, spots, quads)),
        v((band + 3, span, quads), F32),
        v((band + 2, span, quads)),
        v((band * width2, quads)),
        v((2, 16, quads), F32),
        v((2, 16, quads)),
        v((2, width2, quads)),
        v((2, 16, quads)),
        v((2, width2, quads)),
        v((4, 16, quads)),
        v((strips, height2 * width2, quads)),
        v((strips, height2 * width2, filters)),
        v((height2, full2, quads)),
        v((height2 + 2, 3 * filters, full2)),
        v((owners, piece, 128)),
        v((rows * strips, piece, 128)),
        v((piece, 128)),
        v((owners, piece, 128)),
        pltpu.SemaphoreType.DMA((4,)),
    ]
    scratch += sems(len(WAYS) + 2) + sems(len(WAYS)) + sems(rows) + sems(rows) + sems(rows * strips) + sems(rows * strips)
    for _ in range(2):
        scratch += [
            pltpu.SemaphoreType.DMA((cols,)),
            pltpu.SemaphoreType.DMA((cols * pairs,)),
            pltpu.SemaphoreType.DMA((strips,)),
        ]
    arguments = (
        features_in.reshape(channels * band, width),
        jnp.transpose(filters_one, (1, 2, 0, 3)).reshape(9, channels, channels),
        jnp.transpose(filters_two, (1, 2, 0, 3)).reshape(9, filters, quads),
        jnp.transpose(out_grad, (1, 2, 0)).reshape(width2 * height2, filters),
    )
    arguments = [pltpu.with_memory_space_constraint(a, pltpu.HBM) for a in arguments]
    share = 1 if rows * strips <= 64 else 2
    scale_one = 1.0 / math.sqrt(band * rows * width * strips)
    scale_two = 1.0 / math.sqrt(height2 * full2)
    ig, g1, g2 = pl.pallas_call(
        functools.partial(whole_kernel, rows, strips, band, height2, scale_one, scale_two),
        out_shape=(
            jax.ShapeDtypeStruct((channels * band, width), BF),
            jax.ShapeDtypeStruct((9, channels, channels), F32),
            jax.ShapeDtypeStruct((9, filters, quads), F32),
        ),
        in_specs=[HBM] * 4,
        out_specs=(VMEM,) * 3,
        scratch_shapes=scratch,
        compiler_params=pltpu.CompilerParams(
            collective_id=0, has_side_effects=True, vmem_limit_bytes=share * 28 * 1024 * 1024
        ),
    )(*arguments)
    ig, g1, g2 = write_out(ig, g1, g2)
    grad_one = jnp.transpose(g1.reshape(3, 3, channels, channels), (2, 0, 1, 3))
    grad_two = jnp.transpose(g2.reshape(3, 3, filters, quads), (2, 0, 1, 3))
    return (ig.reshape(channels, band, width), grad_one, grad_two)


def solution(mesh):
    in_specs = (
        P("grp", "row", ("col", "pair")),
        P(),
        P("row", None, None, None),
        P(("grp", "row"), ("col", "pair"), None),
    )
    out_specs = (
        P("grp", "row", ("col", "pair")),
        P("grp", None, None, None),
        P(("grp", "row"), None, None, None),
    )
    return jax.shard_map(local, mesh=mesh, in_specs=in_specs, out_specs=out_specs, check_vma=False)
```
